32 devices in a mesh: dp: 8 (over z, core), tensor: 4 (over y, x).
Axes of the slice: x: 2, y: 2, z: 4, core: 2. Of those that a mesh axis runs over, the one named last changes fastest.
Arguments:
- tokens: bfloat16 [36928, 1024], P(('dp', 'tensor')), may hold values from -6 to 6
- first_gain: float32 [1024], replicated, may hold values from 0.5 to 1.5
- first_shift: float32 [1024], replicated, may hold values from -1.5 to 1.5
- joint_weight: bfloat16 [1024, 3, 1024], P('dp', None, 'tensor'), may hold values from -0.1875 to 0.1875
- joint_bias: bfloat16 [2, 16, 64], P(None, 'tensor', 'dp'), may hold values from -3 to 3
- output_weight: bfloat16 [1024, 1024], P('tensor', 'dp'), may hold values from -1 to 1
- output_bias: float32 [1024], replicated, may hold values from -1.5 to 1.5
- second_gain: float32 [1024], replicated, may hold values from 0.5 to 1.5
- second_shift: float32 [1024], replicated, may hold values from -1.5 to 1.5
- expand_weight: bfloat16 [1024, 4096], P('dp', 'tensor'), may hold values from -0.1875 to 0.1875
- expand_bias: bfloat16 [64, 64], P('tensor', 'dp'), may hold values from -3 to 3
- shrink_weight: bfloat16 [4096, 1024], P('tensor', 'dp'), may hold values from -0.1875 to 0.1875
- shrink_bias: float32 [1024], replicated, may hold values from -1.5 to 1.5
- cotangent: bfloat16 [36928, 1024], P(('dp', 'tensor')), may hold values from -6 to 6
- image_count: int32 [8], P('dp'), may hold values from 1 to 8, 56 in all
- threshold: float32 [16], P('tensor'), may hold values from 2 to 20
Outputs:
- block_out: bfloat16 [36928, 1024], P(('dp', 'tensor'))
- tokens_grad: bfloat16 [36928, 1024], P(('dp', 'tensor'))
- first_gain_grad: float32 [1024], P('dp')
- first_shift_grad: float32 [1024], P('dp')
- joint_grad: float32 [1024, 3, 1024], P('dp', None, 'tensor')
- joint_bias_grad: float32 [2, 16, 64], P(None, 'tensor', 'dp')
- output_grad: float32 [1024, 1024], P('tensor', 'dp')
- output_bias_grad: float32 [1024], P('dp')
- second_gain_grad: float32 [1024], P('dp')
- second_shift_grad: float32 [1024], P('dp')
- expand_grad: float32 [1024, 4096], P('dp', 'tensor')
- expand_bias_grad: float32 [64, 64], P('tensor', 'dp')
- shrink_grad: float32 [4096, 1024], P('tensor', 'dp')
- shrink_bias_grad: float32 [1024], P('dp')
- clipped_joint: bfloat16 [1024, 2, 1024], P('dp', None, 'tensor')
- clipped_bias: bfloat16 [16, 64], P('tensor', 'dp')
- factors: float32 [16], P('tensor')
The draws below stay inside these ranges and needn't reach their ends.
Inputs may be any that keep to these rules, and one draw needn't show every extreme that they name: `image_count`: every index of dp holds 1 to 8 images, in its first slots; the counts sum to 56 and some index holds exactly 8.
All inputs are finite; a program needn't handle non-finite values. No bound on the sum of `image_count` on one device may be relied on, other than what follows from the above.
Results may differ from the reference program's by a relative error of at most 0.023.
Values may be sent and summed in bfloat16 or wider, within the bound.
No kernel may reach another device: no remote copies, remote signals or barrier semaphores. Data moves between devices by JAX's collectives and lax.ppermute only.
A program may use at most 320 MiB of HBM per device.

```python
import math
import jax
import jax.numpy as jnp
import numpy as np
from jax import lax

D = 1024
HEADS = 16
HEAD_DIM = 64
FF = 4096
SEQ = 577
IMG_CAP = 8
GROUPS = 8
SLOTS = 64
IMAGES = 56
TOKENS = 36928


def shard_levels(stream_key, dims, pieces, low, top_value):
    loudness = 1.0
    for dim, parts in pieces:
        draws = jax.random.uniform(jax.random.fold_in(jax.random.fold_in(stream_key, 6), dim), (parts,), jnp.float32, low / len(pieces), top_value / len(pieces))
        loudness = loudness * jnp.repeat(jnp.exp(draws), dims[dim] // parts).reshape((-1,) + (1,) * (len(dims) - 1 - dim))
    return loudness


def split_up(number_of, total, bound, slope):
    weights = [(1 << 20) // math.isqrt(standing ** slope) + 1 for standing in range(2, number_of + 1)]
    surplus, holding = total - bound - (number_of - 1), [1] * (number_of - 1)
    while surplus > 0:
        movable = [i for i in range(number_of - 1) if holding[i] < bound]
        whole, left = sum([weights[i] for i in movable]), surplus
        for i in movable:
            more = min(bound - holding[i], max(1, left * weights[i] // whole), surplus)
            holding[i] = holding[i] + more
            surplus = surplus - more
    return np.array([bound] + holding)


def ragged_sizes(stream_key, number_of, total, limit, lean):
    if number_of == 2:
        one = jax.random.randint(stream_key, (), max(1, total - limit), min(limit, total - 1) + 1)
        return jnp.stack([one, total - one])
    sizes = jnp.asarray(split_up(number_of, total, limit, lean), jnp.int32)
    couples = (number_of - 1) // 2
    donor, taker = sizes[1:1 + 2 * couples:2], sizes[2:2 + 2 * couples:2]
    room = jnp.minimum(donor - 1, limit - taker)
    moved = jax.random.randint(jax.random.fold_in(stream_key, 1), (couples,), 0, 1 << 20) % (room + 1)
    sizes = sizes.at[1:1 + 2 * couples:2].set(donor - moved).at[2:2 + 2 * couples:2].set(taker + moved)
    return sizes[jax.random.permutation(jax.random.fold_in(stream_key, 2), number_of)]


def centred(own_key, shape, width, most, cuts=(), held_as=jnp.bfloat16):
    values = jax.random.normal(own_key, shape, jnp.float32) * width
    if len(cuts) > 0:
        values = shard_levels(own_key, shape, cuts, -0.22, 0.18) * values
    return jnp.clip(values, min=-most, max=most).astype(held_as)


def setup_inputs(seed: int = 0) -> dict:
    streams_of = jax.random.split(jax.random.key(seed), 17)
    tokens = centred(streams_of[0], (TOKENS, D), 1.0, 6.0, ((0, 32),))
    first_gain = jnp.clip(1.0 + 0.1 * jax.random.normal(streams_of[1], (D,), jnp.float32), 0.5, 1.5)
    first_shift = centred(streams_of[2], (D,), 0.3, 1.5, (), jnp.float32)
    joint_weight = centred(streams_of[3], (D, 3, D), D ** -0.5, 0.1875, ((0, 8), (2, 4)))
    joint_bias = centred(streams_of[4], (2, HEADS, HEAD_DIM), 0.5, 3.0, ((1, 4), (2, 8)))
    output_weight = centred(streams_of[5], (D, D), (D // 32) ** -0.5, 1.0, ((0, 4), (1, 8)))
    output_bias = centred(streams_of[6], (D,), 0.3, 1.5, (), jnp.float32)
    second_gain = jnp.clip(1.0 + 0.1 * jax.random.normal(streams_of[7], (D,), jnp.float32), 0.5, 1.5)
    second_shift = centred(streams_of[8], (D,), 0.3, 1.5, (), jnp.float32)
    expand_weight = centred(streams_of[9], (D, FF), D ** -0.5, 0.1875, ((0, 8), (1, 4)))
    expand_bias = centred(streams_of[10], (FF // HEAD_DIM, HEAD_DIM), 0.5, 3.0, ((0, 4), (1, 8)))
    shrink_weight = centred(streams_of[11], (FF, D), (FF // 4) ** -0.5, 0.1875, ((0, 4), (1, 8)))
    shrink_bias = centred(streams_of[12], (D,), 0.3, 1.5, (), jnp.float32)
    cotangent = centred(streams_of[13], (TOKENS, D), 1.0, 6.0, ((0, 32),))
    image_count = ragged_sizes(streams_of[14], GROUPS, IMAGES, IMG_CAP, 2).astype(jnp.int32)
    threshold = jnp.clip(jnp.exp(math.log(20.0) - 2.3025851 * jax.random.uniform(streams_of[15], (HEADS,), jnp.float32) ** shard_levels(streams_of[15], (HEADS,), ((0, 4),), -0.2, 0.2)), 2.0, 20.0)
    return dict(tokens=tokens, first_gain=first_gain, first_shift=first_shift, joint_weight=joint_weight, joint_bias=joint_bias, output_weight=output_weight, output_bias=output_bias, second_gain=second_gain, second_shift=second_shift, expand_weight=expand_weight, expand_bias=expand_bias, shrink_weight=shrink_weight, shrink_bias=shrink_bias, cotangent=cotangent, image_count=image_count, threshold=threshold)


@jax.custom_vjp
def low(v):
    return lax.optimization_barrier(v.astype(jnp.bfloat16)).astype(jnp.float32)

@jax.custom_vjp
def low_back(v):
    return v

def low_keep(v):
    return (low(v), None)

def low_pass(kept, grad):
    return (grad,)

def back_keep(v):
    return (v, None)

def back_low(kept, grad):
    return (low(grad),)
low.defvjp(low_keep, low_pass)
low_back.defvjp(back_keep, back_low)
highest = lax.Precision.HIGHEST

def layer_norm(values, gain, shift):
    center = values - lax.optimization_barrier(jnp.mean(values, axis=-1, keepdims=True))
    spread = lax.optimization_barrier(jnp.mean(center * center, axis=-1, keepdims=True))
    return center * lax.rsqrt(spread + 1e-05) * gain + shift

def one_image(params, image, status):
    gain_one, shift_one, joint, joint_b, out_w, out_b, gain_two, shift_two, expand, expand_b, shrink, shrink_b = params
    normed = low(layer_norm(image, gain_one, shift_one))
    packed = jnp.einsum('rd,dcj->rcj', normed, joint, precision=highest)
    biases = jnp.stack([joint_b[0], jnp.zeros_like(joint_b[0]), joint_b[1]])
    packed = low_back(low(packed + biases))
    heads = packed.reshape(SEQ, 3, HEADS, HEAD_DIM)
    queries = heads[:, 0]
    keys = heads[:, 1]
    values = heads[:, 2]
    scale = HEAD_DIM ** (-0.5)
    scores = low_back(scale * jnp.einsum('qhd,khd->hqk', queries, keys, precision=highest))
    peak = lax.optimization_barrier(jnp.max(scores, axis=(1, 2)))
    shifted = scores - lax.optimization_barrier(jnp.max(scores, axis=-1, keepdims=True))
    expo = jnp.exp(shifted)
    probs = expo / lax.optimization_barrier(jnp.sum(expo, axis=-1, keepdims=True))
    mixed = jnp.einsum('hqk,khd->qhd', low(probs), values, precision=highest).reshape(SEQ, D)
    mixed = low_back(low(mixed))
    branch = low_back(jnp.dot(mixed, out_w, precision=highest) + out_b)
    middle = image + branch
    second = low(layer_norm(middle, gain_two, shift_two))
    hidden = low_back(jnp.dot(second, expand, precision=highest) + expand_b)
    active = low(hidden * jax.nn.sigmoid(1.702 * hidden))
    result = low_back(jnp.dot(active, shrink, precision=highest) + shrink_b)
    return (status * (middle + result), jnp.where(status > 0, peak, -1e+30))

def reference(tokens, first_gain, first_shift, joint_weight, joint_bias, output_weight, output_bias, second_gain, second_shift, expand_weight, expand_bias, shrink_weight, shrink_bias, cotangent, image_count, threshold):
    single = jnp.float32
    slot = jnp.arange(SLOTS, dtype=jnp.int32)
    status = (slot % IMG_CAP < image_count[slot // IMG_CAP]).astype(single)
    images = tokens.astype(single).reshape(SLOTS, SEQ, D)
    params = (first_gain, first_shift, joint_weight.astype(single), joint_bias.astype(single).reshape(2, D), output_weight.astype(single), output_bias, second_gain, second_shift, expand_weight.astype(single), expand_bias.astype(single).reshape(FF), shrink_weight.astype(single), shrink_bias)

    def forward(params, images):

        def step(item):
            return one_image(params, item[0], item[1])
        outs, peaks = lax.map(jax.checkpoint(step), (images, status))
        return (outs.reshape(TOKENS, D), lax.optimization_barrier(jnp.max(peaks, axis=0)))
    output, pullback, peak = jax.vjp(forward, params, images, has_aux=True)
    grads, image_grads = pullback(cotangent.astype(single))
    factors = jnp.sqrt(threshold / jnp.maximum(peak, threshold))
    columns = jnp.repeat(factors, HEAD_DIM)
    clipped_joint = (joint_weight[:, 0:2, :].astype(single) * columns).astype(jnp.bfloat16)
    clipped_bias = (joint_bias[0].astype(single) * factors[:, None]).astype(jnp.bfloat16)
    return (output.astype(jnp.bfloat16), image_grads.reshape(TOKENS, D).astype(jnp.bfloat16), grads[0], grads[1], grads[2], grads[3].reshape(2, HEADS, HEAD_DIM), grads[4], grads[5], grads[6], grads[7], grads[8], grads[9].reshape(FF // HEAD_DIM, HEAD_DIM), grads[10], grads[11], clipped_joint, clipped_bias, factors)
```

```python
from functools import partial

import jax
import jax.numpy as jnp
from jax import lax
from jax.experimental import pallas as pl
from jax.experimental.pallas import tpu as pltpu
from jax.sharding import PartitionSpec as P

D = 1024
FF = 4096
HEADS = 16
HEAD_DIM = 64
SEQ = 577
SP = 592
LP = 640
LOG2E = 1.4426950408889634
NEG = -1e30
BF = jnp.bfloat16
F32 = jnp.float32
AXES = ("dp", "tensor")
VMEM_LIMIT = 60 * 2**20


def dotf(a, b, ca, cb):
    return lax.dot_general(a, b, (((ca,), (cb,)), ((), ())), preferred_element_type=F32)


def params():
    return pltpu.CompilerParams(vmem_limit_bytes=VMEM_LIMIT)


def cost(flops, nbytes, trans=0):
    return pl.CostEstimate(flops=int(flops), bytes_accessed=int(nbytes), transcendentals=int(trans))


def whole(shape):
    zeros = (0,) * len(shape)
    return pl.BlockSpec(shape, lambda *_: zeros)


class Layout:
    def __init__(self, ndp, nt):
        self.ndp, self.nt, self.nz = ndp, nt, ndp // 2
        self.size = ndp * nt
        self.rows = D // ndp
        self.cols = FF // nt
        self.tbits = nt.bit_length() - 1
        self.zbits = self.nz.bit_length() - 1
        self.core = nt
        self.cw = D // nt

    def mask(self, bit):
        kind, b = bit
        return (1 << b) if kind == "t" else (self.nt * 2) << b

    def order(self, half):
        z = [("z", b) for b in reversed(range(self.zbits))]
        t = [("t", b) for b in range(self.tbits)]
        if half == 1:
            t = t[::-1]
        out = []
        while z or t:
            if z and len(z) >= len(t):
                out.append(z.pop(0))
            else:
                out.append(t.pop(0))
        return out


def swap(x, mask, size):
    return lax.ppermute(x, AXES, [(i, i ^ mask) for i in range(size)])


def gather_half(lay, piece, half):
    held = [(piece[None], [(0, 0, 0)])]
    for bit in lay.order(half):
        if len(held) == 4:
            held = [(jnp.concatenate([b for b, _ in held]), [o for _, os in held for o in os])]
        kind, b = bit
        more = []
        for buf, offs in held:
            got = swap(buf, lay.mask(bit), lay.size)
            if kind == "z":
                new = [(z ^ (1 << b), t, c) for z, t, c in offs]
            else:
                new = [(z, t ^ (1 << b), c) for z, t, c in offs]
            more.append((got, new))
        held = held + more
    more = []
    for buf, offs in held:
        more.append((swap(buf, lay.core, lay.size), [(z, t, 1) for z, t, _ in offs]))
    return held + more


def gather_group(lay, piece_a, piece_b):
    return gather_half(lay, piece_a, 0), gather_half(lay, piece_b, 1)


def group_refs(group):
    return [buf for half in group for buf, _ in half]


def piece_list(group):
    out = []
    n = 0
    for h, half in enumerate(group):
        for _, offs in half:
            for i, (z, t, c) in enumerate(offs):
                out.append((h, n, i, z, t, c))
            n += 1
    return out


def start_pieces(lay, pieces, bufs, me, spans, dst, sem):
    for h, n, i, z, t, c in pieces:
        row = ((z ^ me[0]) * 2 + (c ^ me[1])) * lay.rows
        row = pl.multiple_of(row, lay.rows)
        ref, base = dst(t, t ^ me[2])
        for first, width, at in spans[h]:
            if isinstance(base, int):
                where = pl.ds(base + at, width)
            else:
                where = pl.ds(pl.multiple_of(base + at, 128), width)
            pltpu.make_async_copy(
                bufs[n].at[i, pl.ds(0, lay.rows), pl.ds(first, width)],
                ref.at[pl.ds(row, lay.rows), where],
                sem(t),
            ).start()


def wait_all(ref, sem):
    pltpu.make_async_copy(ref, ref, sem).wait()


ANY = pl.BlockSpec(memory_space=pl.ANY)


def project(lay, me, group, normed, bias_rows):
    rows = normed.shape[0]
    bufs = group_refs(group)
    pieces = piece_list(group)
    cw = lay.cw
    half = lay.cols // 2
    spans = ([(0, 2 * cw, 0)], [(0, cw, 2 * cw)])

    def kernel(me_ref, *refs):
        src = refs[: len(bufs)]
        x_ref, b_ref, o_ref, w, sem = refs[len(bufs) :]
        o = pl.program_id(0)
        idx = (me_ref[0], me_ref[1], me_ref[2])

        @pl.when(o == 0)
        def _():
            start_pieces(lay, pieces, src, idx, spans, lambda to, t: (w.at[to], 0), lambda to: sem.at[to])

        wait_all(w.at[o], sem.at[o])
        y = jnp.dot(x_ref[...], w[o], preferred_element_type=F32) + b_ref[...]
        o_ref[:, :cw] = (y[:, :cw] * HEAD_DIM**-0.5).astype(BF)
        o_ref[:, cw:] = y[:, cw:].astype(BF)

    return pl.pallas_call(
        kernel,
        grid_spec=pltpu.PrefetchScalarGridSpec(
            num_scalar_prefetch=1,
            grid=(lay.nt,),
            in_specs=[ANY] * len(bufs)
            + [
                pl.BlockSpec((rows, D), lambda o, m: (0, 0)),
                pl.BlockSpec((1, 3 * cw), lambda o, m: (0, o ^ m[2])),
            ],
            out_specs=pl.BlockSpec((rows, 3 * cw), lambda o, m: (0, o ^ m[2])),
            scratch_shapes=[
                pltpu.VMEM((lay.nt, D, 3 * cw), BF),
                pltpu.SemaphoreType.DMA((lay.nt,)),
            ],
        ),
        out_shape=jax.ShapeDtypeStruct((rows, 3 * D), BF),
        compiler_params=params(),
        cost_estimate=cost(2 * rows * D * 3 * D, 16e6),
        name="project",
    )(me, *bufs, normed, bias_rows)


def flip(x):
    pad = jnp.zeros((LP - x.shape[0], x.shape[1]), x.dtype)
    return jnp.concatenate([x, pad], axis=0).T


def key_rows():
    row = lax.broadcasted_iota(jnp.int32, (16, LP), 0)
    lane = lax.broadcasted_iota(jnp.int32, (16, LP), 1)
    return jnp.where(row < 3, 1.0, jnp.where((row == 3) & (lane >= SEQ), NEG, 0.0)).astype(BF)


def split_rows(v):
    row = lax.broadcasted_iota(jnp.int32, (16, LP), 0)
    hi = v.astype(BF).astype(F32)
    mid = (v - hi).astype(BF).astype(F32)
    lo = v - hi - mid
    rest = jnp.where(row == 2, lo, jnp.where(row == 3, 1.0, 0.0))
    return jnp.where(row == 0, hi, jnp.where(row == 1, mid, rest)).astype(BF)


def split_query(q):
    v = q.astype(F32) * LOG2E
    hi = v.astype(BF)
    return hi, (v - hi.astype(F32)).astype(BF)


def attend_kernel(hl, p_ref, o_ref, lse_ref, top_ref):
    cw = hl * HEAD_DIM
    xt = flip(p_ref[...])
    aux = key_rows()
    none = split_rows(jnp.zeros((1, LP), F32))
    first = lax.broadcasted_iota(jnp.int32, (16, LP), 0) == 0
    ones = jnp.where(first, 1.0, 0.0).astype(BF)
    valid = lax.broadcasted_iota(jnp.int32, (1, LP), 1) < SEQ
    outs = []
    for h in range(hl):
        q = xt[h * HEAD_DIM : (h + 1) * HEAD_DIM]
        k = xt[cw + h * HEAD_DIM : cw + (h + 1) * HEAD_DIM]
        v = xt[2 * cw + h * HEAD_DIM : 2 * cw + (h + 1) * HEAD_DIM]
        hi, lo = split_query(q)
        s = dotf(jnp.concatenate([k, k, aux], 0), jnp.concatenate([hi, lo, none], 0), 0, 0)
        m = jnp.max(s, axis=0, keepdims=True)
        p = jnp.exp2(s - m).astype(BF)
        o = dotf(jnp.concatenate([v, ones], 0), p, 1, 0)
        total = o[HEAD_DIM : HEAD_DIM + 1]
        outs.append((o[:HEAD_DIM] / total).astype(BF))
        lse_ref[0, 0, h : h + 1, :] = m + jnp.log2(total)
        top_ref[0, 0, h : h + 1, :] = jnp.where(valid, m, NEG)
    o_ref[...] = jnp.concatenate(outs, 0).T[:SP]


def attend(lay, packed):
    rows = packed.shape[0]
    own = rows // SP
    cw = lay.cw
    hl = cw // HEAD_DIM
    stat = pl.BlockSpec((1, 1, hl, LP), lambda i, t: (i, t, 0, 0))
    stat_shape = jax.ShapeDtypeStruct((own, lay.nt, hl, LP), F32)
    return pl.pallas_call(
        partial(attend_kernel, hl),
        grid=(own, lay.nt),
        in_specs=[pl.BlockSpec((SP, 3 * cw), lambda i, t: (i, t))],
        out_specs=[pl.BlockSpec((SP, cw), lambda i, t: (i, t)), stat, stat],
        out_shape=[jax.ShapeDtypeStruct((rows, D), BF), stat_shape, stat_shape],
        compiler_params=params(),
        cost_estimate=cost(22e9, 10e6),
        name="attend",
    )(packed)


def attend_back_kernel(hl, p_ref, o_ref, g_ref, lse_ref, d_ref, sum_ref):
    cw = hl * HEAD_DIM
    xt = flip(p_ref[...])
    ot = flip(o_ref[...])
    gt = flip(g_ref[...])
    aux = key_rows()
    ones = jnp.where(lax.broadcasted_iota(jnp.int32, (16, LP), 0) < 3, 1.0, 0.0).astype(BF)
    dq, dk, dv = [], [], []
    for h in range(hl):
        at = slice(h * HEAD_DIM, (h + 1) * HEAD_DIM)
        q = xt[at]
        k = xt[cw + h * HEAD_DIM : cw + (h + 1) * HEAD_DIM]
        v = xt[2 * cw + h * HEAD_DIM : 2 * cw + (h + 1) * HEAD_DIM]
        g = gt[at]
        hi, lo = split_query(q)
        delta = jnp.sum(ot[at].astype(F32) * g.astype(F32), axis=0, keepdims=True)
        minus = split_rows(-lse_ref[0, 0, h : h + 1, :])
        s = dotf(jnp.concatenate([k, k, aux], 0), jnp.concatenate([hi, lo, minus], 0), 0, 0)
        p = jnp.exp2(s)
        d = dotf(jnp.concatenate([v, ones], 0), jnp.concatenate([g, split_rows(-delta)], 0), 0, 0)
        ds = (p * d).astype(BF)
        dv.append(dotf(g, p.astype(BF), 1, 1).astype(BF))
        dq.append((HEAD_DIM**-0.5 * dotf(k, ds, 1, 0)).astype(BF))
        dk.append(dotf(q, ds, 1, 1).astype(BF))
    out = jnp.concatenate(dq + dk + dv, 0).T[:SP]
    d_ref[...] = out
    sum_ref[0, 0, :, :] = jnp.sum(out.astype(F32), axis=0, keepdims=True)


def attend_back(lay, packed, mixed, dmixed, lse):
    rows = packed.shape[0]
    own = rows // SP
    cw = lay.cw
    hl = cw // HEAD_DIM
    return pl.pallas_call(
        partial(attend_back_kernel, hl),
        grid=(own, lay.nt),
        in_specs=[
            pl.BlockSpec((SP, 3 * cw), lambda i, t: (i, t)),
            pl.BlockSpec((SP, cw), lambda i, t: (i, t)),
            pl.BlockSpec((SP, cw), lambda i, t: (i, t)),
            pl.BlockSpec((1, 1, hl, LP), lambda i, t: (i, t, 0, 0)),
        ],
        out_specs=[
            pl.BlockSpec((SP, 3 * cw), lambda i, t: (i, t)),
            pl.BlockSpec((1, 1, 1, 3 * cw), lambda i, t: (i, t, 0, 0)),
        ],
        out_shape=[
            jax.ShapeDtypeStruct(packed.shape, BF),
            jax.ShapeDtypeStruct((own, lay.nt, 1, 3 * cw), F32),
        ],
        compiler_params=params(),
        cost_estimate=cost(35e9, 20e6),
        name="attend_back",
    )(packed, mixed, dmixed, lse)


def unit_of(values):
    center = values - jnp.mean(values, axis=-1, keepdims=True)
    inverse = lax.rsqrt(jnp.mean(center * center, axis=-1, keepdims=True) + 1e-05)
    return center * inverse, inverse


def norm_back(grad, unit, inverse, gain):
    scaled = grad * gain
    inner = (
        scaled
        - jnp.mean(scaled, axis=-1, keepdims=True)
        - unit * jnp.mean(scaled * unit, axis=-1, keepdims=True)
    )
    return inner * inverse


def add_rows(ref, first, rows):
    step = pl.program_id(0)

    @pl.when(step == 0)
    def _():
        for r, row in enumerate(rows):
            ref[r : r + 1, :] = row

    @pl.when(step > 0)
    def _():
        for r, row in enumerate(rows):
            ref[r : r + 1, :] += row


def column_sum(x):
    return jnp.sum(x, axis=0, keepdims=True)


def out_project(lay, me, group, mixed, inputs, bias, gain, shift):
    rows = mixed.shape[0]
    bufs = group_refs(group)
    pieces = piece_list(group)
    cw = lay.cw
    spans = ([], [(cw, cw, 0)])

    def kernel(me_ref, *refs):
        src = refs[: len(bufs)]
        m_ref, x_ref, b_ref, g_ref, s_ref, mid_ref, sec_ref, w, sem = refs[len(bufs) :]
        idx = (me_ref[0], me_ref[1], me_ref[2])

        @pl.when(pl.program_id(0) == 0)
        def _():
            start_pieces(lay, pieces, src, idx, spans, lambda to, t: (w, t * cw), lambda to: sem)
            wait_all(w, sem)

        middle = x_ref[...].astype(F32) + dotf(m_ref[...], w[...], 1, 1) + b_ref[...]
        mid_ref[...] = middle
        unit, _ = unit_of(middle)
        sec_ref[...] = (unit * g_ref[...] + s_ref[...]).astype(BF)

    block = pl.BlockSpec((SP, D), lambda i, m: (i, 0))
    row = pl.BlockSpec((1, D), lambda i, m: (0, 0))
    return pl.pallas_call(
        kernel,
        grid_spec=pltpu.PrefetchScalarGridSpec(
            num_scalar_prefetch=1,
            grid=(rows // SP,),
            in_specs=[ANY] * len(bufs) + [block, block, row, row, row],
            out_specs=[block, block],
            scratch_shapes=[pltpu.VMEM((D, D), BF), pltpu.SemaphoreType.DMA],
        ),
        out_shape=[jax.ShapeDtypeStruct((rows, D), F32), jax.ShapeDtypeStruct((rows, D), BF)],
        compiler_params=params(),
        cost_estimate=cost(2 * rows * D * D, 14e6),
        name="out_project",
    )(me, *bufs, mixed, inputs, bias, gain, shift)


def feed(lay, me, expand, shrink, second, dresult, bias):
    rows = second.shape[0]
    bufs_e, bufs_s = group_refs(expand), group_refs(shrink)
    pieces_e, pieces_s = piece_list(expand), piece_list(shrink)
    ne, ns = len(bufs_e), len(bufs_s)
    cols = lay.cols
    half = cols // 2
    spans = ([(0, half, 0)], [(0, half, half)])
    step_rows = SP

    def kernel(me_ref, *refs):
        src_e, src_s = refs[:ne], refs[ne : ne + ns]
        x_ref, g_ref, b_ref, a_ref, d_ref, c_ref, we, ws, sem_e, sem_s = refs[ne + ns :]
        o = pl.program_id(0)
        idx = (me_ref[0], me_ref[1], me_ref[2])

        @pl.when(o == 0)
        def _():
            start_pieces(lay, pieces_e, src_e, idx, spans, lambda to, t: (we.at[to], 0), lambda to: sem_e.at[to])
            start_pieces(lay, pieces_s, src_s, idx, spans, lambda to, t: (ws.at[to], 0), lambda to: sem_s.at[to])

        wait_all(we.at[o], sem_e.at[o])
        wait_all(ws.at[o], sem_s.at[o])
        for j in range(cols // 512):
            cs = slice(j * 512, (j + 1) * 512)
            total = None
            for r in range(rows // step_rows):
                rs = slice(r * step_rows, (r + 1) * step_rows)
                hidden = jnp.dot(x_ref[rs, :], we[o, :, cs], preferred_element_type=F32) + b_ref[:, cs]
                dact = jnp.dot(g_ref[rs, :], ws[o, :, cs], preferred_element_type=F32)
                sigma = jax.nn.sigmoid(1.702 * hidden)
                active = hidden * sigma
                a_ref[rs, cs] = active.astype(BF)
                dh = (dact * (sigma + 1.702 * active * (1.0 - sigma))).astype(BF)
                d_ref[rs, cs] = dh
                part = column_sum(dh.astype(F32))
                total = part if total is None else total + part
            c_ref[:, cs] = total

    return pl.pallas_call(
        kernel,
        grid_spec=pltpu.PrefetchScalarGridSpec(
            num_scalar_prefetch=1,
            grid=(lay.nt,),
            in_specs=[ANY] * (ne + ns)
            + [
                pl.BlockSpec((rows, D), lambda o, m: (0, 0)),
                pl.BlockSpec((rows, D), lambda o, m: (0, 0)),
                pl.BlockSpec((1, cols), lambda o, m: (0, o ^ m[2])),
            ],
            out_specs=[
                pl.BlockSpec((rows, cols), lambda o, m: (0, o ^ m[2])),
                pl.BlockSpec((rows, cols), lambda o, m: (0, o ^ m[2])),
                pl.BlockSpec((1, cols), lambda o, m: (0, o ^ m[2])),
            ],
            scratch_shapes=[
                pltpu.VMEM((lay.nt, D, cols), BF),
                pltpu.VMEM((lay.nt, D, cols), BF),
                pltpu.SemaphoreType.DMA((lay.nt,)),
                pltpu.SemaphoreType.DMA((lay.nt,)),
            ],
        ),
        out_shape=[
            jax.ShapeDtypeStruct((rows, FF), BF),
            jax.ShapeDtypeStruct((rows, FF), BF),
            jax.ShapeDtypeStruct((1, FF), F32),
        ],
        compiler_params=params(),
        cost_estimate=cost(4 * rows * D * FF, 40e6),
        name="feed",
    )(me, *bufs_e, *bufs_s, second, dresult, bias)


def feed_out(lay, me, shrink, active, middle, bias):
    rows = active.shape[0]
    bufs = group_refs(shrink)
    pieces = piece_list(shrink)
    cols = lay.cols
    half = cols // 2
    spans = ([(0, half, 0)], [(0, half, half)])
    own = rows // SP

    def kernel(me_ref, *refs):
        src = refs[: len(bufs)]
        a_ref, mid_ref, b_ref, o_ref, w, sem = refs[len(bufs) :]
        idx = (me_ref[0], me_ref[1], me_ref[2])

        @pl.when(pl.program_id(0) == 0)
        def _():
            start_pieces(lay, pieces, src, idx, spans, lambda to, t: (w, t * cols), lambda to: sem)
            wait_all(w, sem)

        live = me_ref[2] * own + pl.program_id(0) < me_ref[3]
        out = mid_ref[...] + dotf(a_ref[...], w[...], 1, 1) + b_ref[...]
        o_ref[...] = jnp.where(live, out, 0.0).astype(BF)

    return pl.pallas_call(
        kernel,
        grid_spec=pltpu.PrefetchScalarGridSpec(
            num_scalar_prefetch=1,
            grid=(own,),
            in_specs=[ANY] * len(bufs)
            + [
                pl.BlockSpec((SP, FF), lambda i, m: (i, 0)),
                pl.BlockSpec((SP, D), lambda i, m: (i, 0)),
                pl.BlockSpec((1, D), lambda i, m: (0, 0)),
            ],
            out_specs=pl.BlockSpec((SP, D), lambda i, m: (i, 0)),
            scratch_shapes=[pltpu.VMEM((D, FF), BF), pltpu.SemaphoreType.DMA],
        ),
        out_shape=jax.ShapeDtypeStruct((rows, D), BF),
        compiler_params=params(),
        cost_estimate=cost(2 * rows * D * FF, 25e6),
        name="feed_out",
    )(me, *bufs, active, middle, bias)


def feed_back(lay, me, expand, joint, dhidden, middle, dresult, gain):
    rows = dhidden.shape[0]
    bufs_e, bufs_o = group_refs(expand), group_refs(joint)
    pieces_e, pieces_o = piece_list(expand), piece_list(joint)
    ne, no = len(bufs_e), len(bufs_o)
    cols, cw = lay.cols, lay.cw
    half = cols // 2
    spans = ([(0, half, 0)], [(0, half, half)])
    spans_o = ([], [(cw, cw, 0)])

    def kernel(me_ref, *refs):
        src_e, src_o = refs[:ne], refs[ne : ne + no]
        h_ref, mid_ref, g_ref, n_ref, dm_ref, db_ref, dx_ref, v_ref, we, wo, sem_e, sem_o = refs[ne + no :]
        idx = (me_ref[0], me_ref[1], me_ref[2])

        @pl.when(pl.program_id(0) == 0)
        def _():
            start_pieces(lay, pieces_e, src_e, idx, spans, lambda to, t: (we, t * cols), lambda to: sem_e)
            start_pieces(lay, pieces_o, src_o, idx, spans_o, lambda to, t: (wo, t * cw), lambda to: sem_o)
            wait_all(we, sem_e)
            wait_all(wo, sem_o)

        dsecond = dotf(h_ref[...], we[...], 1, 1)
        unit, inverse = unit_of(mid_ref[...])
        dmiddle = g_ref[...].astype(F32) + norm_back(dsecond, unit, inverse, n_ref[...])
        dm_ref[...] = dmiddle
        dbranch = dmiddle.astype(BF)
        db_ref[...] = dbranch
        dx_ref[...] = jnp.dot(dbranch, wo[...], preferred_element_type=F32).astype(BF)
        add_rows(v_ref, 0, [column_sum(dsecond * unit), column_sum(dsecond), column_sum(dbranch.astype(F32)), column_sum(g_ref[...].astype(F32))])

    block = pl.BlockSpec((SP, D), lambda i, m: (i, 0))
    return pl.pallas_call(
        kernel,
        grid_spec=pltpu.PrefetchScalarGridSpec(
            num_scalar_prefetch=1,
            grid=(rows // SP,),
            in_specs=[ANY] * (ne + no)
            + [
                pl.BlockSpec((SP, FF), lambda i, m: (i, 0)),
                block,
                block,
                pl.BlockSpec((1, D), lambda i, m: (0, 0)),
            ],
            out_specs=[block, block, block, pl.BlockSpec((4, D), lambda i, m: (0, 0))],
            scratch_shapes=[
                pltpu.VMEM((D, FF), BF),
                pltpu.VMEM((D, D), BF),
                pltpu.SemaphoreType.DMA,
                pltpu.SemaphoreType.DMA,
            ],
        ),
        out_shape=[
            jax.ShapeDtypeStruct((rows, D), F32),
            jax.ShapeDtypeStruct((rows, D), BF),
            jax.ShapeDtypeStruct((rows, D), BF),
            jax.ShapeDtypeStruct((4, D), F32),
        ],
        compiler_params=params(),
        cost_estimate=cost(2 * rows * D * (FF + D), 35e6),
        name="feed_back",
    )(me, *bufs_e, *bufs_o, dhidden, middle, dresult, gain)


def project_back(lay, me, group, dpacked, inputs, dmiddle, gain):
    rows = dpacked.shape[0]
    bufs = group_refs(group)
    pieces = piece_list(group)
    cw = lay.cw
    spans = ([(0, 2 * cw, 0)], [(0, cw, 2 * cw)])

    def kernel(me_ref, *refs):
        src = refs[: len(bufs)]
        p_ref, x_ref, dm_ref, n_ref, o_ref, v_ref, w, sem = refs[len(bufs) :]
        idx = (me_ref[0], me_ref[1], me_ref[2])

        @pl.when(pl.program_id(0) == 0)
        def _():
            start_pieces(lay, pieces, src, idx, spans, lambda to, t: (w, t * 3 * cw), lambda to: sem)
            wait_all(w, sem)

        dnormed = dotf(p_ref[...], w[...], 1, 1)
        unit, inverse = unit_of(x_ref[...].astype(F32))
        o_ref[...] = (dm_ref[...] + norm_back(dnormed, unit, inverse, n_ref[...])).astype(BF)
        add_rows(v_ref, 0, [column_sum(dnormed * unit), column_sum(dnormed)])

    block = pl.BlockSpec((SP, D), lambda i, m: (i, 0))
    return pl.pallas_call(
        kernel,
        grid_spec=pltpu.PrefetchScalarGridSpec(
            num_scalar_prefetch=1,
            grid=(rows // SP,),
            in_specs=[ANY] * len(bufs)
            + [
                pl.BlockSpec((SP, 3 * D), lambda i, m: (i, 0)),
                block,
                block,
                pl.BlockSpec((1, D), lambda i, m: (0, 0)),
            ],
            out_specs=[block, pl.BlockSpec((2, D), lambda i, m: (0, 0))],
            scratch_shapes=[pltpu.VMEM((D, 3 * D), BF), pltpu.SemaphoreType.DMA],
        ),
        out_shape=[jax.ShapeDtypeStruct((rows, D), BF), jax.ShapeDtypeStruct((2, D), F32)],
        compiler_params=params(),
        cost_estimate=cost(2 * rows * D * 3 * D, 25e6),
        name="project_back",
    )(me, *bufs, dpacked, inputs, dmiddle, gain)


def insert_bit(s, b, value):
    return ((s >> b) << (b + 1)) | (value << b) | (s & ((1 << b) - 1))


def weight_grad(lay, me, lhss, halves, toffs, steps, sibling, received=None, name="grad"):
    rows = lhss[0].shape[0]
    z, dr = lay.nz, lay.rows
    half = lay.cols // 2
    nl = len(lhss)
    parts = [(h, *part) for h in range(2) for part in halves[h]]
    nr = 0 if received is None else 2

    def kernel(me_ref, *refs):
        lhs_refs = refs[:nl]
        rhs_refs = refs[nl : nl + len(parts)]
        got = refs[nl + len(parts) : nl + len(parts) + nr]
        outs = refs[nl + len(parts) + nr : nl + len(parts) + nr + 2]
        sel = refs[nl + len(parts) + nr + 2 :]
        s = pl.program_id(0)

        @pl.when(s == 0)
        def _():
            side = me_ref[1] ^ 1 if sibling else me_ref[1]
            for ref, scratch in zip(lhs_refs, sel):
                for zo in range(z):
                    at = pl.multiple_of((zo ^ me_ref[0]) * (2 * dr), 128)
                    block = ref[:, pl.ds(at, 2 * dr)]
                    scratch[:, zo * dr : (zo + 1) * dr] = jnp.where(side == 0, block[:, :dr], block[:, dr:])

        at = [0, 0]
        for (h, li, _, width, _), ref in zip(parts, rhs_refs):
            y = dotf(sel[li][...], ref[...], 0, 0).reshape(z, dr, width)
            cs = pl.ds(at[h], width)
            at[h] += width
            if nr:
                y = y + got[h][0, :, :, cs].astype(F32)
            outs[h][0, :, :, cs] = y.astype(BF)

    def rhs_spec(h, width, index):
        return pl.BlockSpec((rows, width), lambda s, m: (0, index(toffs[h](s) ^ m[2])))

    def got_spec(h):
        return pl.BlockSpec((1, z, dr, half), lambda s, m: (toffs[h](s), 0, 0, 0))

    piece = pl.BlockSpec((1, z, dr, half), lambda s, m: (s, 0, 0, 0))
    return pl.pallas_call(
        kernel,
        grid_spec=pltpu.PrefetchScalarGridSpec(
            num_scalar_prefetch=1,
            grid=(steps,),
            in_specs=[pl.BlockSpec((rows, D), lambda s, m: (0, 0))] * nl
            + [rhs_spec(h, width, index) for h, _, _, width, index in parts]
            + [got_spec(h) for h in range(nr)],
            out_specs=[piece, piece],
            scratch_shapes=[pltpu.VMEM((rows, z * dr), BF)] * nl,
        ),
        out_shape=[jax.ShapeDtypeStruct((steps, z, dr, half), BF)] * 2,
        compiler_params=params(),
        cost_estimate=cost(2 * rows * z * dr * steps * 2 * half, 15e6),
        name=name,
    )(me, *lhss, *[part[2] for part in parts], *(received or []))


def half_axes(lay, half):
    first = lay.order(half)[-1]
    t = [("t", b) for b in reversed(range(lay.tbits)) if ("t", b) != first]
    z = [("z", b) for b in reversed(range(lay.zbits))]
    return t + z


def scatter_half(lay, half, send, keep):
    order = lay.order(half)[::-1]
    axes = half_axes(lay, half)
    shape = (2,) * len(axes) + send.shape[2:]
    got = swap(send, lay.mask(order[0]), lay.size).reshape(shape)
    keep = keep.reshape(shape)
    for bit in order[1:]:
        axis = axes.index(bit)
        pick = lambda x, i: lax.index_in_dim(x, i, axis, keepdims=False)
        send = (pick(keep, 1).astype(F32) + pick(got, 1).astype(F32)).astype(BF)
        keep = (pick(keep, 0).astype(F32) + pick(got, 0).astype(F32)).astype(BF)
        axes = axes[:axis] + axes[axis + 1 :]
        got = swap(send, lay.mask(bit), lay.size)
    return keep.astype(F32) + got.astype(F32)


def reduce_group(lay, me, lhss, halves, name):
    every = lambda s: s
    both = weight_grad(lay, me, lhss, halves, (every, every), lay.nt, True, name=name + "_other")
    received = [swap(x, lay.core, lay.size) for x in both]
    bits = [lay.order(h)[-1][1] for h in range(2)]
    out = []
    for value in (1, 0):
        toffs = tuple(partial(lambda b, s: insert_bit(s, b, value), b) for b in bits)
        out.append(
            weight_grad(
                lay, me, lhss, halves, toffs, lay.nt // 2, False, received, name=name + ("_keep", "_send")[value]
            )
        )
    send, keep = out
    return [scatter_half(lay, h, send[h], keep[h]) for h in range(2)]


def all_sum(lay, x, combine=jnp.add):
    for bit in lay.order(0):
        x = combine(x, swap(x, lay.mask(bit), lay.size))
    return combine(x, swap(x, lay.core, lay.size))


def pad_rows(x):
    own = x.shape[0] // SEQ
    return jnp.pad(x.reshape(own, SEQ, D), ((0, 0), (0, SP - SEQ), (0, 0))).reshape(own * SP, D)


def unpad_rows(x):
    own = x.shape[0] // SP
    return x.reshape(own, SP, D)[:, :SEQ].reshape(own * SEQ, D)


def per_device(
    lay,
    tokens,
    first_gain,
    first_shift,
    joint_weight,
    joint_bias,
    output_weight,
    output_bias,
    second_gain,
    second_shift,
    expand_weight,
    expand_bias,
    shrink_weight,
    shrink_bias,
    cotangent,
    image_count,
    threshold,
):
    own = tokens.shape[0] // SEQ
    nt, cw, dr = lay.nt, lay.cw, lay.rows
    half = lay.cols // 2
    hl = cw // HEAD_DIM
    tensor = lax.axis_index("tensor").astype(jnp.int32)
    dp = lax.axis_index("dp").astype(jnp.int32)
    count = image_count[0]
    me = jnp.stack([dp // 2, dp % 2, tensor, count])

    joint_a = joint_weight[:, :2].reshape(dr, 2 * cw)
    small = jnp.concatenate([joint_bias.reshape(-1), expand_bias.reshape(-1)])
    n_small = small.shape[0]
    extra = jnp.pad(small[None], ((0, 15), (0, half - n_small)))
    joint_b = jnp.concatenate(
        [jnp.concatenate([joint_weight[:, 2], output_weight.T], axis=1), extra], axis=0
    )
    joint = gather_group(lay, joint_a, joint_b)
    shrink_t = shrink_weight.T
    expand = gather_group(lay, expand_weight[:, :half], expand_weight[:, half:])
    shrink = gather_group(lay, shrink_t[:, :half], shrink_t[:, half:])

    found = jnp.concatenate([buf[:, dr, :n_small] for buf, _ in joint[1]])
    offsets = [(z * 2 + c) * nt + t for _, offs in joint[1] for z, t, c in offs]
    order = jnp.asarray(offsets, jnp.int32) ^ (dp * nt + tensor)
    pick = (jnp.arange(lay.size, dtype=jnp.int32)[:, None] == order[None, :]).astype(BF)
    biases = jnp.dot(pick, found, preferred_element_type=F32)
    nb = joint_bias.size
    jb = biases[:, :nb].reshape(lay.ndp, nt, 2, hl, HEAD_DIM // lay.ndp)
    jb = jb.transpose(1, 2, 3, 0, 4).reshape(nt, 2, cw)
    bias_rows = jnp.concatenate([jb[:, 0], jnp.zeros_like(jb[:, 0]), jb[:, 1]], axis=1).reshape(1, 3 * D)
    eb = biases[:, nb:].reshape(lay.ndp, nt, FF // HEAD_DIM // nt, HEAD_DIM // lay.ndp)
    expand_row = eb.transpose(1, 2, 0, 3).reshape(1, FF)

    image_ids = tensor * own + jnp.arange(own, dtype=jnp.int32)
    image_live = image_ids < count
    inputs = pad_rows(tokens)
    live_rows = jnp.repeat(image_live, SEQ)[:, None]
    dresult = pad_rows(jnp.where(live_rows, cotangent, jnp.zeros_like(cotangent)))
    unit, _ = unit_of(inputs.astype(F32))
    normed = (unit * first_gain + first_shift).astype(BF)

    packed = project(lay, me, joint, normed, bias_rows)
    mixed, lse, tops = attend(lay, packed)
    row = lambda v: v.reshape(1, D)
    middle, second = out_project(
        lay, me, joint, mixed, inputs, row(output_bias), row(second_gain), row(second_shift)
    )
    active, dhidden, expand_sum = feed(lay, me, expand, shrink, second, dresult, expand_row)

    col = lambda h: (lambda t: t * 2 + h)
    shrink_pieces = reduce_group(
        lay, me, [dresult], [[(0, active, half, col(h))] for h in range(2)], "shrink_grad"
    )
    expand_pieces = reduce_group(
        lay, me, [second], [[(0, dhidden, half, col(h))] for h in range(2)], "expand_grad"
    )
    dmiddle, dbranch, dmixed, sums_two = feed_back(
        lay, me, expand, joint, dhidden, middle, dresult, row(second_gain)
    )
    dpacked, packed_sums = attend_back(lay, packed, mixed, dmixed, lse)
    part = lambda c: (lambda t: t * 3 + c)
    joint_pieces = reduce_group(
        lay,
        me,
        [normed, dbranch],
        [
            [(0, dpacked, cw, part(0)), (0, dpacked, cw, part(1))],
            [(0, dpacked, cw, part(2)), (1, mixed, cw, lambda t: t)],
        ],
        "joint_grad",
    )
    token_rows, sums_one = project_back(lay, me, joint, dpacked, inputs, dmiddle, row(first_gain))
    result = feed_out(lay, me, shrink, active, middle, row(shrink_bias))
    block_out = unpad_rows(result)
    tokens_grad = unpad_rows(token_rows)

    early = jnp.concatenate([sums_two.reshape(-1, 128), expand_sum.reshape(-1, 128)])
    early = all_sum(lay, early)
    head_sums = jnp.sum(packed_sums, axis=0).reshape(nt, 3, cw)
    late = jnp.concatenate(
        [sums_one.reshape(-1, 128), head_sums[:, 0].reshape(-1, 128), head_sums[:, 2].reshape(-1, 128)]
    )
    late = all_sum(lay, late)
    sums_two = early[: 4 * D // 128].reshape(4, D)
    expand_sum = early[4 * D // 128 :].reshape(FF)
    sums_one = late[: 2 * D // 128].reshape(2, D)
    bias_sum = late[2 * D // 128 :].reshape(2, D)
    mine = lambda v: lax.dynamic_slice_in_dim(v, dp * dr, dr, v.ndim - 1)
    sums_one, sums_two = mine(sums_one), mine(sums_two)
    share = HEAD_DIM // lay.ndp
    units = FF // HEAD_DIM // nt
    expand_bias_grad = lax.dynamic_slice(
        expand_sum.reshape(FF // HEAD_DIM, HEAD_DIM), (tensor * units, dp * share), (units, share)
    )
    joint_bias_grad = lax.dynamic_slice(
        bias_sum.reshape(2, HEADS, HEAD_DIM), (0, tensor * hl, dp * share), (2, hl, share)
    )

    tops = jnp.max(tops, axis=-1).reshape(own, HEADS) / LOG2E
    peak = jnp.max(jnp.where(image_live[:, None], tops, NEG), axis=0)
    peak = all_sum(lay, jnp.broadcast_to(peak[:, None], (HEADS, 128)), jnp.maximum)[:, 0]
    top = lax.dynamic_slice_in_dim(peak, tensor * hl, hl, 0)
    factors = jnp.sqrt(threshold / jnp.maximum(top, threshold))
    columns = jnp.repeat(factors, HEAD_DIM)
    clipped_joint = (joint_weight[:, 0:2, :].astype(F32) * columns).astype(BF)
    clipped_bias = (joint_bias[0].astype(F32) * factors[:, None]).astype(BF)

    ja, jb = joint_pieces
    joint_grad = jnp.concatenate([ja, jb[:, :cw]], axis=1).reshape(dr, 3, cw)
    output_grad = jb[:, cw:].T
    expand_grad = jnp.concatenate(expand_pieces, axis=1)
    shrink_grad = jnp.concatenate(shrink_pieces, axis=1).T
    return (
        block_out,
        tokens_grad,
        sums_one[0],
        sums_one[1],
        joint_grad,
        joint_bias_grad,
        output_grad,
        sums_two[2],
        sums_two[0],
        sums_two[1],
        expand_grad,
        expand_bias_grad,
        shrink_grad,
        sums_two[3],
        clipped_joint,
        clipped_bias,
        factors,
    )


def solution(mesh):
    placed = (
        P(("dp", "tensor"), None),
        P(),
        P(),
        P("dp", None, "tensor"),
        P(None, "tensor", "dp"),
        P("tensor", "dp"),
        P(),
        P(),
        P(),
        P("dp", "tensor"),
        P("tensor", "dp"),
        P("tensor", "dp"),
        P(),
        P(("dp", "tensor"), None),
        P("dp"),
        P("tensor"),
    )
    lay = Layout(mesh.shape["dp"], mesh.shape["tensor"])
    return jax.shard_map(
        partial(per_device, lay),
        mesh=mesh,
        in_specs=placed,
        out_specs=(
            P(("dp", "tensor"), None),
            P(("dp", "tensor"), None),
            P("dp"),
            P("dp"),
            P("dp", None, "tensor"),
            P(None, "tensor", "dp"),
            P("tensor", "dp"),
            P("dp"),
            P("dp"),
            P("dp"),
            P("dp", "tensor"),
            P("tensor", "dp"),
            P("tensor", "dp"),
            P("dp"),
            P("dp", None, "tensor"),
            P("tensor", "dp"),
            P("tensor"),
        ),
        check_vma=False,
    )
```

```python
from functools import partial

import jax
import jax.numpy as jnp
from jax import lax
from jax.experimental import pallas as pl
from jax.experimental.pallas import tpu as pltpu
from jax.sharding import PartitionSpec as P

D = 1024
FF = 4096
HEADS = 16
HEAD_DIM = 64
SEQ = 577
SP = 592
LP = 640
LOG2E = 1.4426950408889634
NEG = -1e30
BF = jnp.bfloat16
F32 = jnp.float32
AXES = ("dp", "tensor")
VMEM_LIMIT = 60 * 2**20


def dotf(a, b, ca, cb):
    return lax.dot_general(a, b, (((ca,), (cb,)), ((), ())), preferred_element_type=F32)


def whole(shape):
    zeros = (0,) * len(shape)
    return pl.BlockSpec(shape, lambda *_: zeros)


ANY = pl.BlockSpec(memory_space=pl.ANY)


class Runner:
    def __init__(self, me):
        self.me = me
        self.token = jnp.zeros((8, 128), F32)

    def __call__(self, name, us, kernel, grid, ins, outs, scratch=(), through=()):
        n_in, n_out = len(ins), len(outs)
        through = [self.token] + list(through)
        n = len(through)

        def body(me_ref, *refs):
            first = refs[:n_in]
            second = refs[n_in + n : n_in + n + n_out]
            kernel(me_ref, *first, *second, *refs[n_in + 2 * n + n_out :])

        got = pl.pallas_call(
            body,
            grid_spec=pltpu.PrefetchScalarGridSpec(
                num_scalar_prefetch=1,
                grid=grid,
                in_specs=[spec for _, spec in ins] + [ANY] * n,
                out_specs=[spec for _, spec in outs] + [ANY] * n,
                scratch_shapes=list(scratch),
            ),
            out_shape=[shape for shape, _ in outs] + [jax.ShapeDtypeStruct(a.shape, a.dtype) for a in through],
            input_output_aliases={1 + n_in + i: n_out + i for i in range(n)},
            compiler_params=pltpu.CompilerParams(vmem_limit_bytes=VMEM_LIMIT),
            cost_estimate=pl.CostEstimate(flops=int(2e11), bytes_accessed=int(2e8), transcendentals=0),
            name=name,
        )(self.me, *[a for a, _ in ins], *through)
        self.token = got[n_out]
        return got[:n_out], got[n_out + 1 :]


class Layout:
    def __init__(self, ndp, nt):
        self.ndp, self.nt, self.nz = ndp, nt, ndp // 2
        self.size = ndp * nt
        self.rows = D // ndp
        self.cols = FF // nt
        self.tbits = nt.bit_length() - 1
        self.zbits = self.nz.bit_length() - 1
        self.core = nt
        self.cw = D // nt


def stage_mask(lay, bit):
    kind, b = bit
    return (1 << b) if kind == "t" else (lay.nt * 2) << b


def swap(x, mask, size):
    return lax.ppermute(x, AXES, [(i, i ^ mask) for i in range(size)])


class Gather:
    def __init__(self, lay, piece):
        self.lay = lay
        self.held = piece[None]

    def along(self):
        step = 2 * self.lay.nt
        self.got = [self.held] + [swap(self.held, z * step, self.lay.size) for z in range(1, self.lay.nz)]

    def spread(self):
        self.held = jnp.concatenate(self.got)
        self.got = [self.held] + [swap(self.held, t, self.lay.size) for t in range(1, self.lay.nt)]
        self.other = [swap(self.held, self.lay.core, self.lay.size)]

    def share(self):
        lay = self.lay
        self.bufs = self.got + self.other + [swap(b, lay.core, lay.size) for b in self.got[1:]]
        self.pieces = [(c * lay.nt + t, z, z, t, c) for c in range(2) for t in range(lay.nt) for z in range(lay.nz)]


class Chain:
    def __init__(self, lay, piece, reverse):
        self.lay = lay
        z = [("z", b) for b in reversed(range(lay.zbits))]
        t = [("t", b) for b in range(lay.tbits)]
        t = t[::-1] if reverse else t
        self.stages = []
        while z or t:
            self.stages.append(z.pop(0) if z and len(z) >= len(t) else t.pop(0))
        self.held, self.offs = piece[None], [(0, 0)]

    def send(self):
        self.got = swap(self.held, stage_mask(self.lay, self.stages[0]), self.lay.size)

    def land(self):
        kind, b = self.stages.pop(0)
        dz, dt = ((1 << b), 0) if kind == "z" else (0, (1 << b))
        self.offs = self.offs + [(z ^ dz, t ^ dt) for z, t in self.offs]
        self.held = jnp.concatenate([self.held, self.got])

    def share(self):
        self.bufs = [self.held, swap(self.held, self.lay.core, self.lay.size)]
        self.pieces = [(c, i, z, t, c) for c in range(2) for i, (z, t) in enumerate(self.offs)]


class Shards:
    def __init__(self, lay, piece):
        self.bufs = [lax.all_gather(piece, AXES)]


def gate(run, *lists):
    flat = [x for some in lists for x in some]
    _, flat = run("gate", 0.5, lambda *refs: None, (1,), [], [], (), flat)
    flat = list(flat)
    return [[flat.pop(0) for _ in some] for some in lists]


def start_pieces(lay, group, bufs, me_ref, spans, sem, keep=None):
    me = (me_ref[0], me_ref[1], me_ref[2])
    if isinstance(group, Shards):
        pieces = [(0, dp * lay.nt + t, dp * lay.rows, t ^ me[2], t) for t in range(lay.nt) for dp in range(lay.ndp)]
    else:
        pieces = []
        for b, i, z, t, c in group.pieces:
            if keep is None or keep(t):
                row = pl.multiple_of(((z ^ me[0]) * 2 + (c ^ me[1])) * lay.rows, lay.rows)
                pieces.append((b, i, row, t, t ^ me[2]))
    for b, i, row, to, t in pieces:
        for first, width, place in spans:
            ref, at = place(to, t)
            if not isinstance(at, int):
                at = pl.multiple_of(at, 128)
            pltpu.make_async_copy(
                bufs[b].at[i, pl.ds(0, lay.rows), pl.ds(first, width)],
                ref.at[pl.ds(row, lay.rows), pl.ds(at, width)],
                sem(to),
            ).start()


def wait_all(ref, sem):
    pltpu.make_async_copy(ref, ref, sem).wait()


def flip(x):
    pad = jnp.zeros((LP - x.shape[0], x.shape[1]), x.dtype)
    return jnp.concatenate([x, pad], axis=0).T


def key_rows():
    row = lax.broadcasted_iota(jnp.int32, (16, LP), 0)
    lane = lax.broadcasted_iota(jnp.int32, (16, LP), 1)
    return jnp.where(row < 3, 1.0, jnp.where((row == 3) & (lane >= SEQ), NEG, 0.0)).astype(BF)


def split_rows(v):
    row = lax.broadcasted_iota(jnp.int32, (16, LP), 0)
    hi = v.astype(BF).astype(F32)
    mid = (v - hi).astype(BF).astype(F32)
    lo = v - hi - mid
    rest = jnp.where(row == 2, lo, jnp.where(row == 3, 1.0, 0.0))
    return jnp.where(row == 0, hi, jnp.where(row == 1, mid, rest)).astype(BF)


def split_query(q):
    v = q.astype(F32) * LOG2E
    hi = v.astype(BF)
    return hi, (v - hi.astype(F32)).astype(BF)


def attend_kernel(hl, p_ref, o_ref, lse_ref, top_ref):
    cw = hl * HEAD_DIM
    xt = flip(p_ref[...])
    aux = key_rows()
    none = split_rows(jnp.zeros((1, LP), F32))
    first = lax.broadcasted_iota(jnp.int32, (16, LP), 0) == 0
    ones = jnp.where(first, 1.0, 0.0).astype(BF)
    valid = lax.broadcasted_iota(jnp.int32, (1, LP), 1) < SEQ
    outs = []
    for h in range(hl):
        q = xt[h * HEAD_DIM : (h + 1) * HEAD_DIM]
        k = xt[cw + h * HEAD_DIM : cw + (h + 1) * HEAD_DIM]
        v = xt[2 * cw + h * HEAD_DIM : 2 * cw + (h + 1) * HEAD_DIM]
        hi, lo = split_query(q)
        s = dotf(jnp.concatenate([k, k, aux], 0), jnp.concatenate([hi, lo, none], 0), 0, 0)
        m = jnp.max(s, axis=0, keepdims=True)
        p = jnp.exp2(s - m).astype(BF)
        o = dotf(jnp.concatenate([v, ones], 0), p, 1, 0)
        total = o[HEAD_DIM : HEAD_DIM + 1]
        outs.append((o[:HEAD_DIM] / total).astype(BF))
        lse_ref[0, 0, h : h + 1, :] = m + jnp.log2(total)
        top_ref[0, 0, h : h + 1, :] = jnp.where(valid, m, NEG)
    o_ref[...] = jnp.concatenate(outs, 0).T[:SP]


def attend_back_kernel(hl, p_ref, o_ref, g_ref, lse_ref, d_ref, sum_ref):
    cw = hl * HEAD_DIM
    xt = flip(p_ref[...])
    ot = flip(o_ref[...])
    gt = flip(g_ref[...])
    aux = key_rows()
    ones = jnp.where(lax.broadcasted_iota(jnp.int32, (16, LP), 0) < 3, 1.0, 0.0).astype(BF)
    dq, dk, dv = [], [], []
    for h in range(hl):
        at = slice(h * HEAD_DIM, (h + 1) * HEAD_DIM)
        q = xt[at]
        k = xt[cw + h * HEAD_DIM : cw + (h + 1) * HEAD_DIM]
        v = xt[2 * cw + h * HEAD_DIM : 2 * cw + (h + 1) * HEAD_DIM]
        g = gt[at]
        hi, lo = split_query(q)
        delta = jnp.sum(ot[at].astype(F32) * g.astype(F32), axis=0, keepdims=True)
        minus = split_rows(-lse_ref[0, 0, h : h + 1, :])
        s = dotf(jnp.concatenate([k, k, aux], 0), jnp.concatenate([hi, lo, minus], 0), 0, 0)
        p = jnp.exp2(s)
        d = dotf(jnp.concatenate([v, ones], 0), jnp.concatenate([g, split_rows(-delta)], 0), 0, 0)
        ds = (p * d).astype(BF)
        dv.append(dotf(g, p.astype(BF), 1, 1).astype(BF))
        dq.append((HEAD_DIM**-0.5 * dotf(k, ds, 1, 0)).astype(BF))
        dk.append(dotf(q, ds, 1, 1).astype(BF))
    out = jnp.concatenate(dq + dk + dv, 0).T[:SP]
    d_ref[...] = out
    sum_ref[0, 0, :, :] = jnp.sum(out.astype(F32), axis=0, keepdims=True)


def unit_of(values):
    center = values - jnp.mean(values, axis=-1, keepdims=True)
    inverse = lax.rsqrt(jnp.mean(center * center, axis=-1, keepdims=True) + 1e-05)
    return center * inverse, inverse


def norm_back(grad, unit, inverse, gain):
    scaled = grad * gain
    inner = (
        scaled
        - jnp.mean(scaled, axis=-1, keepdims=True)
        - unit * jnp.mean(scaled * unit, axis=-1, keepdims=True)
    )
    return inner * inverse


def add_rows(ref, rows):
    step = pl.program_id(0)

    @pl.when(step == 0)
    def _():
        for r, row in enumerate(rows):
            ref[r : r + 1, :] = row

    @pl.when(step > 0)
    def _():
        for r, row in enumerate(rows):
            ref[r : r + 1, :] += row


def column_sum(x):
    return jnp.sum(x, axis=0, keepdims=True)


def row_block(width):
    return pl.BlockSpec((SP, width), lambda i, m: (i, 0))


def one_row(width):
    return pl.BlockSpec((1, width), lambda i, m: (0, 0))


def put_pieces(lay, me_ref, y, other, own, first=0):
    dr, width = lay.rows, y.shape[1]
    cs = pl.ds(first, width)
    y = y.astype(BF)
    for c in range(2):

        @pl.when(me_ref[1] == c)
        def _(c=c):
            for z in range(lay.nz):
                at = z ^ me_ref[0]
                a, b = (2 * z + c) * dr, (2 * z + 1 - c) * dr
                own[0, at, :, cs] = y[a : a + dr]
                other[0, at, :, cs] = y[b : b + dr]


def piece_out(lay, width):
    return (
        jax.ShapeDtypeStruct((lay.nt, lay.nz, lay.rows, width), BF),
        pl.BlockSpec((1, lay.nz, lay.rows, width), lambda o, *rest: (o, 0, 0, 0)),
    )


def start_joint(lay, joint, bufs, me_ref, place, sem, keep=None):
    for h, chain in enumerate(joint):
        width = chain.held.shape[-1]
        at = 0 if h == 0 else 3 * lay.cw - width
        spans = [(0, width, lambda to, t: (place(to), at))]
        start_pieces(lay, chain, bufs[2 * h : 2 * h + 2], me_ref, spans, sem, keep)


def attend_all(lay, run, joint, normed, bias_rows):
    rows = normed.shape[0]
    own, cw = rows // SP, lay.cw
    hl = cw // HEAD_DIM
    wide = 3 * cw

    def kernel(me_ref, *refs):
        bufs = refs[:4]
        x_ref, b_ref, p_ref, o_ref, lse_ref, top_ref, w, sem = refs[4:]
        o, i = pl.program_id(0), pl.program_id(1)

        @pl.when((o == 0) & (i == 0))
        def _():
            start_joint(lay, joint, bufs, me_ref, lambda to: w.at[to], lambda to: sem.at[to])

        @pl.when(i == 0)
        def _():
            wait_all(w.at[o], sem.at[o])

        y = jnp.dot(x_ref[...], w[o], preferred_element_type=F32) + b_ref[...]
        p_ref[:, :cw] = (y[:, :cw] * HEAD_DIM**-0.5).astype(BF)
        p_ref[:, cw:] = y[:, cw:].astype(BF)
        attend_kernel(hl, p_ref, o_ref, lse_ref, top_ref)

    stat = pl.BlockSpec((1, 1, hl, LP), lambda o, i, m: (i, o ^ m[2], 0, 0))
    stat_shape = jax.ShapeDtypeStruct((own, lay.nt, hl, LP), F32)
    out, _ = run(
        "attend", 36, kernel, (lay.nt, own),
        [(b, ANY) for chain in joint for b in chain.bufs]
        + [
            (normed, pl.BlockSpec((SP, D), lambda o, i, m: (i, 0))),
            (bias_rows, pl.BlockSpec((1, wide), lambda o, i, m: (0, o ^ m[2]))),
        ],
        [
            (jax.ShapeDtypeStruct((rows, lay.nt * wide), BF), pl.BlockSpec((SP, wide), lambda o, i, m: (i, o ^ m[2]))),
            (jax.ShapeDtypeStruct((rows, D), BF), pl.BlockSpec((SP, cw), lambda o, i, m: (i, o ^ m[2]))),
            (stat_shape, stat),
            (stat_shape, stat),
        ],
        [pltpu.VMEM((lay.nt, D, wide), BF), pltpu.SemaphoreType.DMA((lay.nt,))],
    )
    return out


def out_project(lay, run, group, mixed, inputs, bias, gain, shift):
    rows = inputs.shape[0]
    cw = lay.cw
    nb = len(group.bufs)

    def kernel(me_ref, *refs):
        bufs = refs[:nb]
        m_ref, x_ref, b_ref, g_ref, s_ref, mid_ref, sec_ref, w, sem = refs[nb:]

        @pl.when(pl.program_id(0) == 0)
        def _():
            spans = [(0, cw, lambda to, t: (w, t * cw))]
            start_pieces(lay, group, bufs, me_ref, spans, lambda to: sem)
            wait_all(w, sem)

        middle = x_ref[...].astype(F32) + dotf(m_ref[...], w[...], 1, 1) + b_ref[...]
        mid_ref[...] = middle.astype(BF)
        unit, _ = unit_of(middle)
        sec_ref[...] = (unit * g_ref[...] + s_ref[...]).astype(BF)

    out, _ = run(
        "out_project", 10, kernel, (rows // SP,),
        [(b, ANY) for b in group.bufs]
        + [(mixed, row_block(D)), (inputs, row_block(D))]
        + [(v, one_row(D)) for v in (bias, gain, shift)],
        [
            (jax.ShapeDtypeStruct((rows, D), BF), row_block(D)),
            (jax.ShapeDtypeStruct((rows, D), BF), row_block(D)),
        ],
        [pltpu.VMEM((D, D), BF), pltpu.SemaphoreType.DMA],
    )
    return out


def feed(lay, run, group, second, dresult, bias, dsecond=None, through=()):
    rows = second.shape[0]
    half = lay.cols // 2
    more = dsecond is not None
    nb = len(group.bufs)

    def kernel(me_ref, *refs):
        bufs = refs[:nb]
        x_ref, g_ref, b_ref, *refs = refs[nb:]
        if more:
            before, *refs = refs
        a_ref, s_ref, sec_ref, other, mine, we, ws, d_s, acc, sem_e, sem_s, sem = refs
        o = pl.program_id(0)

        @pl.when(o == 0)
        def _():
            spans = [(0, half, lambda to, t: (we.at[to], 0))]
            start_pieces(lay, group, bufs, me_ref, spans, lambda to: sem_e.at[to])
            spans = [(half, half, lambda to, t: (ws.at[to], 0))]
            start_pieces(lay, group, bufs, me_ref, spans, lambda to: sem_s.at[to])
            if more:
                pltpu.make_async_copy(before, acc, sem).start()
                pltpu.make_async_copy(before, acc, sem).wait()
            else:
                acc[...] = jnp.zeros_like(acc)

        wait_all(we.at[o], sem_e.at[o])
        wait_all(ws.at[o], sem_s.at[o])
        total = None
        for r in range(rows // SP):
            rs = slice(r * SP, (r + 1) * SP)
            hidden = jnp.dot(x_ref[rs, :], we[o], preferred_element_type=F32) + b_ref[...]
            dact = jnp.dot(g_ref[rs, :], ws[o], preferred_element_type=F32)
            sigma = 0.5 + 0.5 * jnp.tanh(0.851 * hidden)
            active = hidden * sigma
            a_ref[rs, :] = active.astype(BF)
            dh = (dact * (sigma + 1.702 * active * (1.0 - sigma))).astype(BF)
            d_s[rs, :] = dh
            part = column_sum(dh.astype(F32))
            total = part if total is None else total + part
            acc[rs, :] += dotf(dh, we[o], 1, 1)
        s_ref[...] = total
        put_pieces(lay, me_ref, dotf(x_ref[...], d_s[...], 0, 0), other, mine)
        put_pieces(lay, me_ref, dotf(g_ref[...], a_ref[...], 0, 0), other, mine, half)

        @pl.when(o == lay.nt - 1)
        def _():
            sec_ref[...] = acc[...].astype(sec_ref.dtype)

    line = pl.BlockSpec((1, half), lambda o, m: (0, o ^ m[2]))
    full = pl.BlockSpec((rows, D), lambda o, m: (0, 0))
    weights = pltpu.VMEM((lay.nt, D, half), BF)
    sems = pltpu.SemaphoreType.DMA((lay.nt,))
    return run(
        "feed", 33, kernel, (lay.nt,),
        [(b, ANY) for b in group.bufs]
        + [(second, full), (dresult, full), (bias, line)] + ([(dsecond, ANY)] if more else []),
        [
            (jax.ShapeDtypeStruct((rows, lay.nt * half), BF), pl.BlockSpec((rows, half), lambda o, m: (0, o ^ m[2]))),
            (jax.ShapeDtypeStruct((1, lay.nt * half), F32), line),
            (jax.ShapeDtypeStruct((rows, D), BF if more else F32), full),
        ]
        + [piece_out(lay, 2 * half)] * 2,
        [
            weights,
            weights,
            pltpu.VMEM((rows, half), BF),
            pltpu.VMEM((rows, D), F32),
            sems,
            sems,
            pltpu.SemaphoreType.DMA,
        ],
        through,
    )


def feed_out(lay, run, groups, active, middle, bias, more=()):
    rows = middle.shape[0]
    own = rows // SP
    half = lay.cols // 2
    wide = lay.nt * half

    n0, n1 = [len(group.bufs) for group in groups]

    def kernel(me_ref, *refs):
        bufs = (refs[:n0], refs[n0 : n0 + n1])
        a0_ref, a1_ref, mid_ref, b_ref, o_ref, w, sem = refs[n0 + n1 :]

        @pl.when(pl.program_id(0) == 0)
        def _():
            for g, group in enumerate(groups):
                spans = [(half, half, lambda to, t, g=g: (w.at[g], t * half))]
                start_pieces(lay, group, bufs[g], me_ref, spans, lambda to: sem)
            wait_all(w, sem)

        live = me_ref[2] * own + pl.program_id(0) < me_ref[3]
        out = mid_ref[...].astype(F32) + dotf(a0_ref[...], w[0], 1, 1) + dotf(a1_ref[...], w[1], 1, 1) + b_ref[...]
        o_ref[...] = jnp.where(live, out, 0.0).astype(BF)

    (result,), more = run(
        "feed_out", 20, kernel, (own,),
        [(b, ANY) for g in groups for b in g.bufs]
        + [(a, row_block(wide)) for a in active]
        + [(middle, row_block(D)), (bias, one_row(D))],
        [(jax.ShapeDtypeStruct((rows, D), BF), row_block(D))],
        [pltpu.VMEM((2, D, wide), BF), pltpu.SemaphoreType.DMA],
        more,
    )
    return result, more


def feed_back(lay, run, group, dsecond, middle, dresult, mixed, gain):
    rows = middle.shape[0]
    cw, nt = lay.cw, lay.nt
    steps = rows // SP

    nb = len(group.bufs)

    def kernel(me_ref, *refs):
        bufs = refs[:nb]
        d_ref, mid_ref, g_ref, m_ref, n_ref, dm_ref, dx_ref, v_ref, other, own, w, acc, sem = refs[nb:]
        i = pl.program_id(0)

        @pl.when(i == 0)
        def _():
            spans = [(0, cw, lambda to, t: (w, t * cw))]
            start_pieces(lay, group, bufs, me_ref, spans, lambda to: sem)
            wait_all(w, sem)

        dsecond = d_ref[...].astype(F32)
        unit, inverse = unit_of(mid_ref[...].astype(F32))
        dout = g_ref[...].astype(F32)
        dmiddle = dout + norm_back(dsecond, unit, inverse, n_ref[...])
        dbranch = dmiddle.astype(BF)
        dm_ref[...] = dbranch
        dx_ref[...] = jnp.dot(dbranch, w[...], preferred_element_type=F32).astype(BF)
        sums = [dsecond * unit, dsecond, dbranch.astype(F32), dout]
        add_rows(v_ref, [column_sum(v) for v in sums])
        y = dotf(dbranch, m_ref[...], 0, 0)

        @pl.when(i == 0)
        def _():
            acc[...] = y

        @pl.when(i > 0)
        def _():
            acc[...] += y

        @pl.when(i == steps - 1)
        def _():
            for t in range(nt):
                to = t ^ me_ref[2]
                put_pieces(
                    lay, me_ref, acc[:, t * cw : (t + 1) * cw], other.at[pl.ds(to, 1)], own.at[pl.ds(to, 1)]
                )

    piece = jax.ShapeDtypeStruct((nt, lay.nz, lay.rows, cw), BF)
    out, _ = run(
        "feed_back", 10, kernel, (steps,),
        [(b, ANY) for b in group.bufs]
        + [(v, row_block(D)) for v in (dsecond, middle, dresult, mixed)]
        + [(gain, one_row(D))],
        [
            (jax.ShapeDtypeStruct((rows, D), BF), row_block(D)),
            (jax.ShapeDtypeStruct((rows, D), BF), row_block(D)),
            (jax.ShapeDtypeStruct((4, D), F32), whole((4, D))),
            (piece, whole(piece.shape)),
            (piece, whole(piece.shape)),
        ],
        [pltpu.VMEM((D, D), BF), pltpu.VMEM((D, D), F32), pltpu.SemaphoreType.DMA],
    )
    return out


def attend_back(lay, run, to, joint, packed, mixed, dmixed, lse, normed, output, last=None):
    rows = packed.shape[0]
    own, cw = rows // SP, lay.cw
    hl = cw // HEAD_DIM
    w3 = 3 * cw
    np = 0 if last is None else len(last[0])

    def kernel(me_ref, *refs):
        bufs = refs[:4]
        p_ref, m_ref, g_ref, lse_ref, x_ref, go_other, go_own, *refs = refs[4:]
        if last is not None:
            parts = refs[:np]
            in_ref, dm_ref, gain_ref, *refs = refs[np:]
            sum_ref, out_ref, v_ref, other, mine, w, dp, total, sem = refs
        else:
            sum_ref, out_ref, other, mine, w, dp, total, sem = refs
        i = pl.program_id(0)

        @pl.when(i == 0)
        def _():
            start_joint(lay, joint, bufs, me_ref, lambda _: w, lambda _: sem, lambda t: t == to)

        attend_back_kernel(hl, p_ref, m_ref, g_ref, lse_ref, dp, sum_ref)

        @pl.when(i == 0)
        def _():
            wait_all(w, sem)

        dnormed = dotf(dp[...], w[...], 1, 1)
        y = dotf(x_ref[...], dp[...], 0, 0)
        if last is None:
            out_ref[...] = dnormed.astype(BF)
        else:
            for part in parts:
                dnormed += part[...].astype(F32)
            unit, inverse = unit_of(in_ref[...].astype(F32))
            dinput = norm_back(dnormed, unit, inverse, gain_ref[...])
            out_ref[...] = (dm_ref[...].astype(F32) + dinput).astype(BF)
            add_rows(v_ref, [column_sum(dnormed * unit), column_sum(dnormed)])

        @pl.when(i == 0)
        def _():
            total[...] = y

        @pl.when(i > 0)
        def _():
            total[...] += y

        @pl.when(i == own - 1)
        def _():
            put_pieces(lay, me_ref, total[...], other, mine)
            other[:, :, :, w3:] = go_other[...]
            mine[:, :, :, w3:] = go_own[...]

    spec = lambda width: pl.BlockSpec((SP, width), lambda i, m: (i, to ^ m[2]))
    part = pl.BlockSpec((1, lay.nz, lay.rows, cw), lambda i, m: (to, 0, 0, 0))
    piece = jax.ShapeDtypeStruct((1, lay.nz, lay.rows, w3 + cw), BF)
    out, _ = run(
        "attend_back", 38, kernel, (own,),
        [(b, ANY) for chain in joint for b in chain.bufs]
        + [
            (packed, spec(w3)),
            (mixed, spec(cw)),
            (dmixed, spec(cw)),
            (lse, pl.BlockSpec((1, 1, hl, LP), lambda i, m: (i, to ^ m[2], 0, 0))),
            (normed, row_block(D)),
            (output[0], part),
            (output[1], part),
        ]
        + ([(x, row_block(D)) for x in (*last[0], last[1], last[2])] + [(last[3], one_row(D))] if last else []),
        [
            (jax.ShapeDtypeStruct((own, 1, 1, w3), F32), pl.BlockSpec((1, 1, 1, w3), lambda i, m: (i, 0, 0, 0))),
            (jax.ShapeDtypeStruct((rows, D), BF), row_block(D)),
        ]
        + ([(jax.ShapeDtypeStruct((2, D), F32), whole((2, D)))] if last else [])
        + [(piece, whole(piece.shape))] * 2,
        [pltpu.VMEM((D, w3), BF), pltpu.VMEM((SP, w3), BF), pltpu.VMEM((D, w3), F32), pltpu.SemaphoreType.DMA],
    )
    return out


def insert_bit(s, b, value):
    return ((s >> b) << (b + 1)) | (value << b) | (s & ((1 << b) - 1))


def along(lay, run, arrays, more=()):
    z, dr, width = arrays[0].shape
    n = len(arrays)
    w = 256 if width % 256 == 0 else 128

    def kernel(me_ref, *refs):
        for k in range(z):
            total = refs[0][k].astype(F32)
            for ref in refs[1:n]:
                total += ref[k].astype(F32)
            refs[n + k][...] = total.astype(BF)

    block = pl.BlockSpec((z, dr, w), lambda s, m: (0, 0, s))
    out = (jax.ShapeDtypeStruct((dr, width), BF), pl.BlockSpec((dr, w), lambda s, m: (0, s)))
    sums, more = run("add_plane", 4, kernel, (width // w,), [(x, block) for x in arrays], [out] * z, (), more)
    return [swap(x, k * 2 * lay.nt, lay.size) if k else x for k, x in enumerate(sums)], more


def total_of(ends):
    total = ends[0].astype(F32)
    for x in ends[1:]:
        total = total + x.astype(F32)
    return total


class Butterfly:
    def __init__(self, lay, reverse, other, own):
        self.lay = lay
        bits = list(range(lay.tbits))
        self.bits = bits[::-1] if reverse else bits
        self.left = bits[::-1]
        self.keep = own
        self.got = swap(other, lay.core, lay.size)

    def fold(self, run):
        bit = self.bits.pop(0)
        low = len(self.left) - 1 - self.left.index(bit)
        self.left.remove(bit)
        n, z, dr, width = self.keep.shape
        block = (1, z // 2, dr, width)
        ins, outs = [], []
        for value in (1, 0):
            spec = pl.BlockSpec(block, lambda s, j, m, value=value: (insert_bit(s, low, value), j, 0, 0))
            ins += [(self.keep, spec), (self.got, spec)]
            shape = jax.ShapeDtypeStruct((n // 2, z, dr, width), BF)
            outs.append((shape, pl.BlockSpec(block, lambda s, j, m: (s, j, 0, 0))))

        def kernel(me_ref, *refs):
            for i in range(2):
                refs[4 + i][...] = refs[2 * i][...] + refs[2 * i + 1][...]

        (send, self.keep), _ = run("add", 4, kernel, (n // 2, 2), ins, outs)
        self.got = swap(send, 1 << bit, self.lay.size)

    def along(self, run, more=()):
        self.ends, more = along(self.lay, run, [self.keep[0], self.got[0]], more)
        return more


class Direct:
    def __init__(self, lay):
        self.lay = lay
        self.parts = []

    def start(self, to, other, own):
        self.waiting = (to, own[0], swap(other[0], self.lay.core, self.lay.size))

    def spread(self, run):
        to, own, got = self.waiting
        z, dr, width = own.shape

        def kernel(me_ref, a_ref, b_ref, o_ref):
            o_ref[...] = a_ref[...] + b_ref[...]

        block = pl.BlockSpec((1, dr, width), lambda s, m: (s, 0, 0))
        (x,), _ = run("add_core", 2, kernel, (z,), [(own, block), (got, block)], [(jax.ShapeDtypeStruct(own.shape, BF), block)])
        self.parts.append(swap(x, to, self.lay.size))

    def along(self, run, more=()):
        self.ends, more = along(self.lay, run, list(self.waiting[1:]) + self.parts, more)
        return more


class Sum:
    def __init__(self, lay, x, combine=jnp.add):
        self.lay, self.x, self.combine = lay, x, combine
        self.masks = [1 << b for b in range((lay.size - 1).bit_length())]
        self.send()

    def send(self):
        self.got = swap(self.x, self.masks.pop(0), self.lay.size)

    def land(self, passed=None):
        if passed:
            self.got = passed[0]
        self.x = self.combine(self.x, self.got)
        if self.masks:
            self.send()
        else:
            self.got = None


def pad_rows(x):
    own = x.shape[0] // SEQ
    return jnp.pad(x.reshape(own, SEQ, D), ((0, 0), (0, SP - SEQ), (0, 0))).reshape(own * SP, D)


def unpad_rows(x):
    own = x.shape[0] // SP
    return x.reshape(own, SP, D)[:, :SEQ].reshape(own * SEQ, D)


def per_device(
    lay,
    tokens,
    first_gain,
    first_shift,
    joint_weight,
    joint_bias,
    output_weight,
    output_bias,
    second_gain,
    second_shift,
    expand_weight,
    expand_bias,
    shrink_weight,
    shrink_bias,
    cotangent,
    image_count,
    threshold,
):
    own = tokens.shape[0] // SEQ
    nt, cw, dr = lay.nt, lay.cw, lay.rows
    half = lay.cols // 2
    hl = cw // HEAD_DIM
    tensor = lax.axis_index("tensor").astype(jnp.int32)
    dp = lax.axis_index("dp").astype(jnp.int32)
    count = image_count[0]
    run = Runner(jnp.stack([dp // 2, dp % 2, tensor, count]))

    shrink_t = shrink_weight.T
    split = 3 * cw // 2 if cw % 256 == 0 else 2 * cw
    flat = joint_weight.reshape(dr, 3 * cw)
    joint = [Chain(lay, flat[:, :split], False), Chain(lay, flat[:, split:], True)]
    small = jnp.concatenate([joint_bias.reshape(-1), expand_bias.reshape(-1)])
    n_small = small.shape[0]
    piece = jnp.concatenate([output_weight.T, jnp.pad(small[None], ((0, 15), (0, cw - n_small)))])
    ((piece,),) = gate(run, [piece])
    output = Shards(lay, piece)
    halves = [
        jnp.concatenate([w[:, g * half : (g + 1) * half] for w in (expand_weight, shrink_t)], axis=1)
        for g in range(2)
    ]
    feeds = [Gather(lay, halves[0])]

    biases = output.bufs[0][:, dr].astype(F32)
    nb = joint_bias.size
    jb = biases[:, :nb].reshape(lay.ndp, nt, 2, hl, HEAD_DIM // lay.ndp)
    jb = jb.transpose(2, 1, 3, 0, 4).reshape(2, nt, 1, cw)
    bias_rows = jnp.concatenate([jb[0], jnp.zeros_like(jb[0]), jb[1]], axis=1).reshape(1, 3 * D)
    eb = biases[:, nb:n_small].reshape(lay.ndp, nt, FF // HEAD_DIM // nt, HEAD_DIM // lay.ndp)
    eb = eb.transpose(1, 2, 0, 3).reshape(nt, 2, half)
    expand_rows = [eb[:, g].reshape(1, nt * half) for g in range(2)]

    image_ids = tensor * own + jnp.arange(own, dtype=jnp.int32)
    image_live = image_ids < count
    inputs = pad_rows(tokens)
    live_rows = jnp.repeat(image_live, SEQ)[:, None]
    dresult = pad_rows(jnp.where(live_rows, cotangent, jnp.zeros_like(cotangent)))
    unit, _ = unit_of(inputs.astype(F32))
    normed = (unit * first_gain + first_shift).astype(BF)
    row = lambda v: v.reshape(1, D)

    for chain in joint:
        chain.send()
    while len(joint[0].stages) > 2:
        for chain in joint:
            chain.land()
            chain.send()
    (joint[0].got, joint[1].got), (feeds[0].held,) = gate(run, [chain.got for chain in joint], [feeds[0].held])
    for chain in joint:
        chain.land()
        chain.send()
    feeds[0].along()
    (joint[0].got, joint[1].got), feeds[0].got[1:], (inputs, dresult, normed), (halves[1],) = gate(
        run, [chain.got for chain in joint], feeds[0].got[1:], [inputs, dresult, normed], [halves[1]]
    )
    for chain in joint:
        chain.land()
        chain.share()
    feeds.append(Shards(lay, halves[1]))
    feeds[0].spread()
    packed, mixed, lse, tops = attend_all(lay, run, joint, normed, bias_rows)
    (feeds[0].got[1:],) = gate(run, feeds[0].got[1:])
    feeds[0].share()
    middle, second = out_project(
        lay, run, output, mixed, inputs, row(output_bias), row(second_gain), row(second_shift)
    )

    (active0, expand_sum0, dsecond, *pieces), _ = feed(lay, run, feeds[0], second, dresult, expand_rows[0])
    grads = [Butterfly(lay, True, *pieces)]
    active1, expand_sum1, dsecond, *pieces = feed(
        lay, run, feeds[1], second, dresult, expand_rows[1], dsecond
    )[0]
    grads.append(Butterfly(lay, False, *pieces))
    grads[0].fold(run)
    dmiddle, dmixed, sums_two, *out_pieces = feed_back(
        lay, run, output, dsecond, middle, dresult, mixed, row(second_gain)
    )
    grads[1].fold(run)

    packed_sums, dnormed = [], []
    total = Direct(lay)

    def back(to, last=None):
        part, out, *more = attend_back(
            lay, run, to, joint, packed, mixed, dmixed, lse, normed, out_pieces, last
        )
        packed_sums.append(part)
        total.start(to, *more[-2:])
        return out, more[0]

    for n, to in enumerate(range(nt - 1, 0, -1)):
        dnormed.append(back(to)[0])
        if n < 2:
            grads[n].fold(run)
        elif n == 2 and not grads[0].bits:
            grads[0].along(run)
        total.spread(run)
    token_rows, sums_one = back(0, (dnormed, inputs, dmiddle, row(first_gain)))

    tops = jnp.max(tops, axis=-1).reshape(own, HEADS) / LOG2E
    peak = jnp.max(jnp.where(image_live[:, None], tops, NEG), axis=0)
    peak = jnp.broadcast_to(peak[:, None], (HEADS, 128))
    expand_sum = jnp.stack([expand_sum0.reshape(nt, half), expand_sum1.reshape(nt, half)], axis=1)
    heads = jnp.concatenate([jnp.sum(x, axis=0) for x in packed_sums[::-1]]).reshape(nt, 3, cw)
    heads = heads[jnp.arange(nt) ^ tensor]
    vectors = [sums_two, expand_sum, sums_one, heads[:, 0], heads[:, 2]]
    sums = jnp.concatenate([peak] + [v.reshape(-1, 128) for v in vectors])
    is_peak = lax.broadcasted_iota(jnp.int32, sums.shape, 0) < HEADS
    small = Sum(lay, sums, lambda a, b: jnp.where(is_peak, jnp.maximum(a, b), a + b))
    while grads[1].bits:
        for sc in grads:
            sc.fold(run)
    if nt != 4:
        grads[0].along(run)
    small.land(grads[1].along(run, [small.got]))
    small.land(total.along(run, [small.got]))
    result, passed = feed_out(lay, run, feeds, [active0, active1], middle, row(shrink_bias), [small.got])
    small.land(passed)
    while small.got is not None:
        small.land()

    block_out = unpad_rows(result)
    tokens_grad = unpad_rows(token_rows)
    sums = small.x
    peak = sums[:HEADS, 0]
    at = [HEADS, HEADS + 4 * D // 128, HEADS + (4 * D + FF) // 128, HEADS + (6 * D + FF) // 128]
    sums_two = sums[at[0] : at[1]].reshape(4, D)
    expand_sum = sums[at[1] : at[2]].reshape(FF)
    sums_one = sums[at[2] : at[3]].reshape(2, D)
    bias_sum = sums[at[3] :].reshape(2, D)
    mine = lambda v: lax.dynamic_slice_in_dim(v, dp * dr, dr, v.ndim - 1)
    sums_one, sums_two = mine(sums_one), mine(sums_two)
    share = HEAD_DIM // lay.ndp
    units = FF // HEAD_DIM // nt
    expand_bias_grad = lax.dynamic_slice(
        expand_sum.reshape(FF // HEAD_DIM, HEAD_DIM), (tensor * units, dp * share), (units, share)
    )
    joint_bias_grad = lax.dynamic_slice(
        bias_sum.reshape(2, HEADS, HEAD_DIM), (0, tensor * hl, dp * share), (2, hl, share)
    )

    top = lax.dynamic_slice_in_dim(peak, tensor * hl, hl, 0)
    factors = jnp.sqrt(threshold / jnp.maximum(top, threshold))
    columns = jnp.repeat(factors, HEAD_DIM)
    clipped_joint = (joint_weight[:, 0:2, :].astype(F32) * columns).astype(BF)
    clipped_bias = (joint_bias[0].astype(F32) * factors[:, None]).astype(BF)

    feed_a, feed_b, total = [total_of(g.ends) for g in (*grads, total)]
    joint_grad = total[:, : 3 * cw].reshape(dr, 3, cw)
    output_grad = total[:, 3 * cw :].T
    expand_grad = jnp.concatenate([feed_a[:, :half], feed_b[:, :half]], axis=1)
    shrink_grad = jnp.concatenate([feed_a[:, half:], feed_b[:, half:]], axis=1).T
    return (
        block_out,
        tokens_grad,
        sums_one[0],
        sums_one[1],
        joint_grad,
        joint_bias_grad,
        output_grad,
        sums_two[2],
        sums_two[0],
        sums_two[1],
        expand_grad,
        expand_bias_grad,
        shrink_grad,
        sums_two[3],
        clipped_joint,
        clipped_bias,
        factors,
    )


def solution(mesh):
    placed = (
        P(("dp", "tensor"), None),
        P(),
        P(),
        P("dp", None, "tensor"),
        P(None, "tensor", "dp"),
        P("tensor", "dp"),
        P(),
        P(),
        P(),
        P("dp", "tensor"),
        P("tensor", "dp"),
        P("tensor", "dp"),
        P(),
        P(("dp", "tensor"), None),
        P("dp"),
        P("tensor"),
    )
    lay = Layout(mesh.shape["dp"], mesh.shape["tensor"])
    return jax.shard_map(
        partial(per_device, lay),
        mesh=mesh,
        in_specs=placed,
        out_specs=(
            P(("dp", "tensor"), None),
            P(("dp", "tensor"), None),
            P("dp"),
            P("dp"),
            P("dp", None, "tensor"),
            P(None, "tensor", "dp"),
            P("tensor", "dp"),
            P("dp"),
            P("dp"),
            P("dp"),
            P("dp", "tensor"),
            P("tensor", "dp"),
            P("tensor", "dp"),
            P("dp"),
            P("dp", None, "tensor"),
            P("tensor", "dp"),
            P("tensor"),
        ),
        check_vma=False,
    )
```

```python
from functools import partial

import jax
import jax.numpy as jnp
from jax import lax
from jax.experimental import pallas as pl
from jax.experimental.pallas import tpu as pltpu
from jax.sharding import PartitionSpec as P

D = 1024
FF = 4096
HEADS = 16
HEAD_DIM = 64
SEQ = 577
SP = 592
LP = 640
LOG2E = 1.4426950408889634
NEG = -1e30
BF = jnp.bfloat16
F32 = jnp.float32
AXES = ("dp", "tensor")
VMEM_LIMIT = 60 * 2**20


def dotf(a, b, ca, cb):
    return lax.dot_general(a, b, (((ca,), (cb,)), ((), ())), preferred_element_type=F32)


def whole(shape):
    zeros = (0,) * len(shape)
    return pl.BlockSpec(shape, lambda *_: zeros)


ANY = pl.BlockSpec(memory_space=pl.ANY)


class Runner:
    def __init__(self, me):
        self.me = me
        self.token = jnp.zeros((8, 128), F32)

    def __call__(self, name, us, kernel, grid, ins, outs, scratch=(), through=()):
        n_in, n_out = len(ins), len(outs)
        through = [self.token] + list(through)
        n = len(through)

        def body(me_ref, *refs):
            first = refs[:n_in]
            second = refs[n_in + n : n_in + n + n_out]
            kernel(me_ref, *first, *second, *refs[n_in + 2 * n + n_out :])

        got = pl.pallas_call(
            body,
            grid_spec=pltpu.PrefetchScalarGridSpec(
                num_scalar_prefetch=1,
                grid=grid,
                in_specs=[spec for _, spec in ins] + [ANY] * n,
                out_specs=[spec for _, spec in outs] + [ANY] * n,
                scratch_shapes=list(scratch),
            ),
            out_shape=[shape for shape, _ in outs] + [jax.ShapeDtypeStruct(a.shape, a.dtype) for a in through],
            input_output_aliases={1 + n_in + i: n_out + i for i in range(n)},
            compiler_params=pltpu.CompilerParams(vmem_limit_bytes=VMEM_LIMIT),
            cost_estimate=pl.CostEstimate(flops=int(us * 1.1e9), bytes_accessed=int(us * 1e6), transcendentals=0),
            name=name,
        )(self.me, *[a for a, _ in ins], *through)
        self.token = got[n_out]
        return got[:n_out], got[n_out + 1 :]


class Layout:
    def __init__(self, ndp, nt):
        self.ndp, self.nt, self.nz = ndp, nt, ndp // 2
        self.size = ndp * nt
        self.rows = D // ndp
        self.cols = FF // nt
        self.tbits = nt.bit_length() - 1
        self.zbits = self.nz.bit_length() - 1
        self.core = nt
        self.cw = D // nt


def stage_mask(lay, bit):
    kind, b = bit
    return (1 << b) if kind == "t" else (lay.nt * 2) << b


def swap(x, mask, size):
    return lax.ppermute(x, AXES, [(i, i ^ mask) for i in range(size)])


class Chain:
    def __init__(self, lay, piece, reverse):
        self.lay = lay
        z = [("z", b) for b in reversed(range(lay.zbits))]
        t = [("t", b) for b in range(lay.tbits)]
        t = t[::-1] if reverse else t
        self.stages = []
        while z or t:
            self.stages.append(z.pop(0) if z and len(z) >= len(t) else t.pop(0))
        self.held, self.offs = piece[None], [(0, 0)]

    def send(self):
        self.got = swap(self.held, stage_mask(self.lay, self.stages[0]), self.lay.size)

    def land(self):
        kind, b = self.stages.pop(0)
        dz, dt = ((1 << b), 0) if kind == "z" else (0, (1 << b))
        self.offs = self.offs + [(z ^ dz, t ^ dt) for z, t in self.offs]
        self.held = jnp.concatenate([self.held, self.got])

    def send_last(self):
        self.send()
        self.bufs = [self.held, None, swap(self.held, self.lay.core, self.lay.size), None]

    def share(self):
        (kind, b), lay = self.stages.pop(0), self.lay
        dz, dt = ((1 << b), 0) if kind == "z" else (0, (1 << b))
        self.bufs[1], self.bufs[3] = self.got, swap(self.got, lay.core, lay.size)
        more = [(z ^ dz, t ^ dt) for z, t in self.offs]
        self.pieces = [
            (2 * c + k, i, z, t, c)
            for c in range(2)
            for k, offs in enumerate((self.offs, more))
            for i, (z, t) in enumerate(offs)
        ]


class Shards:
    def __init__(self, lay, piece):
        self.bufs = [lax.all_gather(piece, AXES)]


def gate(run, *lists):
    flat = [x for some in lists for x in some]
    _, flat = run("gate", 0, lambda *refs: None, (1,), [], [], (), flat)
    flat = list(flat)
    return [[flat.pop(0) for _ in some] for some in lists]


def start_pieces(lay, group, bufs, me_ref, spans, sem, keep=None):
    me = (me_ref[0], me_ref[1], me_ref[2])
    if isinstance(group, Shards):
        pieces = [(0, dp * lay.nt + t, dp * lay.rows, t ^ me[2], t) for t in range(lay.nt) for dp in range(lay.ndp)]
    else:
        pieces = []
        for b, i, z, t, c in group.pieces:
            if keep is None or keep(t):
                row = pl.multiple_of(((z ^ me[0]) * 2 + (c ^ me[1])) * lay.rows, lay.rows)
                pieces.append((b, i, row, t, t ^ me[2]))
    for b, i, row, to, t in pieces:
        for first, width, place in spans:
            ref, at = place(to, t)
            if not isinstance(at, int):
                at = pl.multiple_of(at, 128)
            pltpu.make_async_copy(
                bufs[b].at[i, pl.ds(0, lay.rows), pl.ds(first, width)],
                ref.at[pl.ds(row, lay.rows), pl.ds(at, width)],
                sem(to),
            ).start()


def wait_all(ref, sem):
    pltpu.make_async_copy(ref, ref, sem).wait()


def flip(x):
    pad = jnp.zeros((LP - x.shape[0], x.shape[1]), x.dtype)
    return jnp.concatenate([x, pad], axis=0).T


def key_rows():
    row = lax.broadcasted_iota(jnp.int32, (16, LP), 0)
    lane = lax.broadcasted_iota(jnp.int32, (16, LP), 1)
    return jnp.where(row < 3, 1.0, jnp.where((row == 3) & (lane >= SEQ), NEG, 0.0)).astype(BF)


def split_rows(v):
    row = lax.broadcasted_iota(jnp.int32, (16, LP), 0)
    hi = v.astype(BF).astype(F32)
    mid = (v - hi).astype(BF).astype(F32)
    lo = v - hi - mid
    rest = jnp.where(row == 2, lo, jnp.where(row == 3, 1.0, 0.0))
    return jnp.where(row == 0, hi, jnp.where(row == 1, mid, rest)).astype(BF)


def split_query(q):
    v = q.astype(F32) * LOG2E
    hi = v.astype(BF)
    return hi, (v - hi.astype(F32)).astype(BF)


def attend_kernel(hl, p_ref, o_ref, lse_ref, top_ref):
    cw = hl * HEAD_DIM
    xt = flip(p_ref[...])
    aux = key_rows()
    none = split_rows(jnp.zeros((1, LP), F32))
    first = lax.broadcasted_iota(jnp.int32, (16, LP), 0) == 0
    ones = jnp.where(first, 1.0, 0.0).astype(BF)
    valid = lax.broadcasted_iota(jnp.int32, (1, LP), 1) < SEQ
    outs = []
    for h in range(hl):
        q = xt[h * HEAD_DIM : (h + 1) * HEAD_DIM]
        k = xt[cw + h * HEAD_DIM : cw + (h + 1) * HEAD_DIM]
        v = xt[2 * cw + h * HEAD_DIM : 2 * cw + (h + 1) * HEAD_DIM]
        hi, lo = split_query(q)
        s = dotf(jnp.concatenate([k, k, aux], 0), jnp.concatenate([hi, lo, none], 0), 0, 0)
        m = jnp.max(s, axis=0, keepdims=True)
        p = jnp.exp2(s - m).astype(BF)
        o = dotf(jnp.concatenate([v, ones], 0), p, 1, 0)
        total = o[HEAD_DIM : HEAD_DIM + 1]
        outs.append((o[:HEAD_DIM] / total).astype(BF))
        lse_ref[0, 0, h : h + 1, :] = m + jnp.log2(total)
        top_ref[0, 0, h : h + 1, :] = jnp.where(valid, m, NEG)
    o_ref[...] = jnp.concatenate(outs, 0).T[:SP]


def attend_back_kernel(hl, p_ref, o_ref, g_ref, lse_ref, d_ref, sum_ref):
    cw = hl * HEAD_DIM
    xt = flip(p_ref[...])
    ot = flip(o_ref[...])
    gt = flip(g_ref[...])
    aux = key_rows()
    ones = jnp.where(lax.broadcasted_iota(jnp.int32, (16, LP), 0) < 3, 1.0, 0.0).astype(BF)
    dq, dk, dv = [], [], []
    for h in range(hl):
        at = slice(h * HEAD_DIM, (h + 1) * HEAD_DIM)
        q = xt[at]
        k = xt[cw + h * HEAD_DIM : cw + (h + 1) * HEAD_DIM]
        v = xt[2 * cw + h * HEAD_DIM : 2 * cw + (h + 1) * HEAD_DIM]
        g = gt[at]
        hi, lo = split_query(q)
        delta = jnp.sum(ot[at].astype(F32) * g.astype(F32), axis=0, keepdims=True)
        minus = split_rows(-lse_ref[0, 0, h : h + 1, :])
        s = dotf(jnp.concatenate([k, k, aux], 0), jnp.concatenate([hi, lo, minus], 0), 0, 0)
        p = jnp.exp2(s)
        d = dotf(jnp.concatenate([v, ones], 0), jnp.concatenate([g, split_rows(-delta)], 0), 0, 0)
        ds = (p * d).astype(BF)
        dv.append(dotf(g, p.astype(BF), 1, 1).astype(BF))
        dq.append((HEAD_DIM**-0.5 * dotf(k, ds, 1, 0)).astype(BF))
        dk.append(dotf(q, ds, 1, 1).astype(BF))
    out = jnp.concatenate(dq + dk + dv, 0).T[:SP]
    d_ref[...] = out
    sum_ref[0, 0, :, :] = jnp.sum(out.astype(F32), axis=0, keepdims=True)


def unit_of(values):
    center = values - jnp.mean(values, axis=-1, keepdims=True)
    inverse = lax.rsqrt(jnp.mean(center * center, axis=-1, keepdims=True) + 1e-05)
    return center * inverse, inverse


def norm_back(grad, unit, inverse, gain):
    scaled = grad * gain
    inner = (
        scaled
        - jnp.mean(scaled, axis=-1, keepdims=True)
        - unit * jnp.mean(scaled * unit, axis=-1, keepdims=True)
    )
    return inner * inverse


def add_rows(ref, rows):
    step = pl.program_id(0)

    @pl.when(step == 0)
    def _():
        for r, row in enumerate(rows):
            ref[r : r + 1, :] = row

    @pl.when(step > 0)
    def _():
        for r, row in enumerate(rows):
            ref[r : r + 1, :] += row


def column_sum(x):
    return jnp.sum(x, axis=0, keepdims=True)


def row_block(width):
    return pl.BlockSpec((SP, width), lambda i, m: (i, 0))


def one_row(width):
    return pl.BlockSpec((1, width), lambda i, m: (0, 0))


def put_pieces(lay, me_ref, y, other, own, first=0):
    dr, width = lay.rows, y.shape[1]
    cs = pl.ds(first, width)
    y = y.astype(BF)
    for c in range(2):

        @pl.when(me_ref[1] == c)
        def _(c=c):
            for z in range(lay.nz):
                at = z ^ me_ref[0]
                a, b = (2 * z + c) * dr, (2 * z + 1 - c) * dr
                own[0, at, :, cs] = y[a : a + dr]
                other[0, at, :, cs] = y[b : b + dr]


def piece_out(lay, width):
    return (
        jax.ShapeDtypeStruct((lay.nt, lay.nz, lay.rows, width), BF),
        pl.BlockSpec((1, lay.nz, lay.rows, width), lambda o, *rest: (o, 0, 0, 0)),
    )


def start_joint(lay, joint, bufs, me_ref, place, sem, keep=None):
    for h, chain in enumerate(joint):
        width = chain.held.shape[-1]
        at = 0 if h == 0 else 3 * lay.cw - width
        spans = [(0, width, lambda to, t: (place(to), at))]
        start_pieces(lay, chain, bufs[4 * h : 4 * h + 4], me_ref, spans, sem, keep)


def attend_all(lay, run, joint, normed, bias_rows):
    rows = normed.shape[0]
    own, cw = rows // SP, lay.cw
    hl = cw // HEAD_DIM
    wide = 3 * cw

    def kernel(me_ref, *refs):
        bufs = refs[:8]
        x_ref, b_ref, p_ref, o_ref, lse_ref, top_ref, w, sem = refs[8:]
        o, i = pl.program_id(0), pl.program_id(1)

        @pl.when((o == 0) & (i == 0))
        def _():
            start_joint(lay, joint, bufs, me_ref, lambda to: w.at[to], lambda to: sem.at[to])

        @pl.when(i == 0)
        def _():
            wait_all(w.at[o], sem.at[o])

        y = jnp.dot(x_ref[...], w[o], preferred_element_type=F32) + b_ref[...]
        p_ref[:, :cw] = (y[:, :cw] * HEAD_DIM**-0.5).astype(BF)
        p_ref[:, cw:] = y[:, cw:].astype(BF)
        attend_kernel(hl, p_ref, o_ref, lse_ref, top_ref)

    stat = pl.BlockSpec((1, 1, hl, LP), lambda o, i, m: (i, o ^ m[2], 0, 0))
    stat_shape = jax.ShapeDtypeStruct((own, lay.nt, hl, LP), F32)
    out, _ = run(
        "attend", 36, kernel, (lay.nt, own),
        [(b, ANY) for chain in joint for b in chain.bufs]
        + [
            (normed, pl.BlockSpec((SP, D), lambda o, i, m: (i, 0))),
            (bias_rows, pl.BlockSpec((1, wide), lambda o, i, m: (0, o ^ m[2]))),
        ],
        [
            (jax.ShapeDtypeStruct((rows, lay.nt * wide), BF), pl.BlockSpec((SP, wide), lambda o, i, m: (i, o ^ m[2]))),
            (jax.ShapeDtypeStruct((rows, D), BF), pl.BlockSpec((SP, cw), lambda o, i, m: (i, o ^ m[2]))),
            (stat_shape, stat),
            (stat_shape, stat),
        ],
        [pltpu.VMEM((lay.nt, D, wide), BF), pltpu.SemaphoreType.DMA((lay.nt,))],
    )
    return out


def out_project(lay, run, group, mixed, inputs, bias, gain, shift):
    rows = inputs.shape[0]
    cw = lay.cw
    nb = len(group.bufs)

    def kernel(me_ref, *refs):
        bufs = refs[:nb]
        m_ref, x_ref, b_ref, g_ref, s_ref, mid_ref, sec_ref, w, sem = refs[nb:]

        @pl.when(pl.program_id(0) == 0)
        def _():
            spans = [(0, cw, lambda to, t: (w, t * cw))]
            start_pieces(lay, group, bufs, me_ref, spans, lambda to: sem)
            wait_all(w, sem)

        middle = x_ref[...].astype(F32) + dotf(m_ref[...], w[...], 1, 1) + b_ref[...]
        mid_ref[...] = middle.astype(BF)
        unit, _ = unit_of(middle)
        sec_ref[...] = (unit * g_ref[...] + s_ref[...]).astype(BF)

    out, _ = run(
        "out_project", 9, kernel, (rows // SP,),
        [(b, ANY) for b in group.bufs]
        + [(mixed, row_block(D)), (inputs, row_block(D))]
        + [(v, one_row(D)) for v in (bias, gain, shift)],
        [
            (jax.ShapeDtypeStruct((rows, D), BF), row_block(D)),
            (jax.ShapeDtypeStruct((rows, D), BF), row_block(D)),
        ],
        [pltpu.VMEM((D, D), BF), pltpu.SemaphoreType.DMA],
    )
    return out


def feed(lay, run, expand, shrink, second, dresult, bias, dsecond=None):
    rows = second.shape[0]
    half = lay.cols // 2
    more = dsecond is not None
    (group_e, first_e), (group_s, first_s) = expand, shrink
    ne, ns = len(group_e.bufs), len(group_s.bufs)

    def kernel(me_ref, *refs):
        bufs_e, bufs_s = refs[:ne], refs[ne : ne + ns]
        x_ref, g_ref, b_ref, *refs = refs[ne + ns :]
        if more:
            before, *refs = refs
        a_ref, s_ref, sec_ref, other, mine, we, ws, d_s, acc, sem_e, sem_s, sem = refs
        o = pl.program_id(0)

        @pl.when(o == 0)
        def _():
            spans = [(first_e, half, lambda to, t: (we.at[to], 0))]
            start_pieces(lay, group_e, bufs_e, me_ref, spans, lambda to: sem_e.at[to])
            spans = [(first_s, half, lambda to, t: (ws.at[to], 0))]
            start_pieces(lay, group_s, bufs_s, me_ref, spans, lambda to: sem_s.at[to])
            if more:
                pltpu.make_async_copy(before, acc, sem).start()
                pltpu.make_async_copy(before, acc, sem).wait()
            else:
                acc[...] = jnp.zeros_like(acc)

        wait_all(we.at[o], sem_e.at[o])
        wait_all(ws.at[o], sem_s.at[o])
        total = None
        for r in range(rows // SP):
            rs = slice(r * SP, (r + 1) * SP)
            hidden = jnp.dot(x_ref[rs, :], we[o], preferred_element_type=F32) + b_ref[...]
            dact = jnp.dot(g_ref[rs, :], ws[o], preferred_element_type=F32)
            sigma = 0.5 + 0.5 * jnp.tanh(0.851 * hidden)
            active = hidden * sigma
            a_ref[rs, :] = active.astype(BF)
            dh = (dact * (sigma + 1.702 * active * (1.0 - sigma))).astype(BF)
            d_s[rs, :] = dh
            part = column_sum(dh.astype(F32))
            total = part if total is None else total + part
            acc[rs, :] += dotf(dh, we[o], 1, 1)
        s_ref[...] = total
        put_pieces(lay, me_ref, dotf(x_ref[...], d_s[...], 0, 0), other, mine)
        put_pieces(lay, me_ref, dotf(g_ref[...], a_ref[...], 0, 0), other, mine, half)

        @pl.when(o == lay.nt - 1)
        def _():
            sec_ref[...] = acc[...].astype(sec_ref.dtype)

    line = pl.BlockSpec((1, half), lambda o, m: (0, o ^ m[2]))
    full = pl.BlockSpec((rows, D), lambda o, m: (0, 0))
    weights = pltpu.VMEM((lay.nt, D, half), BF)
    sems = pltpu.SemaphoreType.DMA((lay.nt,))
    out, _ = run(
        "feed", 40, kernel, (lay.nt,),
        [(b, ANY) for b in (*group_e.bufs, *group_s.bufs)]
        + [(second, full), (dresult, full), (bias, line)] + ([(dsecond, ANY)] if more else []),
        [
            (jax.ShapeDtypeStruct((rows, lay.nt * half), BF), pl.BlockSpec((rows, half), lambda o, m: (0, o ^ m[2]))),
            (jax.ShapeDtypeStruct((1, lay.nt * half), F32), line),
            (jax.ShapeDtypeStruct((rows, D), BF if more else F32), full),
        ]
        + [piece_out(lay, 2 * half)] * 2,
        [
            weights,
            weights,
            pltpu.VMEM((rows, half), BF),
            pltpu.VMEM((rows, D), F32),
            sems,
            sems,
            pltpu.SemaphoreType.DMA,
        ],
    )
    return out


def feed_out(lay, run, shrink, active, base, bias=None, more=()):
    rows = base.shape[0]
    own = rows // SP
    half = lay.cols // 2
    wide = lay.nt * half
    group, first = shrink
    nb = len(group.bufs)

    def kernel(me_ref, *refs):
        bufs = refs[:nb]
        a_ref, base_ref, *refs = refs[nb:]
        o_ref, w, sem = refs[-3:]

        @pl.when(pl.program_id(0) == 0)
        def _():
            spans = [(first, half, lambda to, t: (w, t * half))]
            start_pieces(lay, group, bufs, me_ref, spans, lambda to: sem)
            wait_all(w, sem)

        out = base_ref[...].astype(F32) + dotf(a_ref[...], w[...], 1, 1)
        if bias is None:
            o_ref[...] = out
        else:
            live = me_ref[2] * own + pl.program_id(0) < me_ref[3]
            o_ref[...] = jnp.where(live, out + refs[0][...], 0.0).astype(BF)

    (result,), more = run(
        "feed_out", 12, kernel, (own,),
        [(b, ANY) for b in group.bufs]
        + [(active, row_block(wide)), (base, row_block(D))]
        + ([] if bias is None else [(bias, one_row(D))]),
        [(jax.ShapeDtypeStruct((rows, D), F32 if bias is None else BF), row_block(D))],
        [pltpu.VMEM((D, wide), BF), pltpu.SemaphoreType.DMA],
        more,
    )
    return result, more


def feed_back(lay, run, group, dsecond, middle, dresult, mixed, gain):
    rows = middle.shape[0]
    cw, nt = lay.cw, lay.nt
    steps = rows // SP

    nb = len(group.bufs)

    def kernel(me_ref, *refs):
        bufs = refs[:nb]
        d_ref, mid_ref, g_ref, m_ref, n_ref, dm_ref, dx_ref, v_ref, other, own, w, acc, sem = refs[nb:]
        i = pl.program_id(0)

        @pl.when(i == 0)
        def _():
            spans = [(0, cw, lambda to, t: (w, t * cw))]
            start_pieces(lay, group, bufs, me_ref, spans, lambda to: sem)
            wait_all(w, sem)

        dsecond = d_ref[...].astype(F32)
        unit, inverse = unit_of(mid_ref[...].astype(F32))
        dout = g_ref[...].astype(F32)
        dmiddle = dout + norm_back(dsecond, unit, inverse, n_ref[...])
        dbranch = dmiddle.astype(BF)
        dm_ref[...] = dbranch
        dx_ref[...] = jnp.dot(dbranch, w[...], preferred_element_type=F32).astype(BF)
        sums = [dsecond * unit, dsecond, dbranch.astype(F32), dout]
        add_rows(v_ref, [column_sum(v) for v in sums])
        y = dotf(dbranch, m_ref[...], 0, 0)

        @pl.when(i == 0)
        def _():
            acc[...] = y

        @pl.when(i > 0)
        def _():
            acc[...] += y

        @pl.when(i == steps - 1)
        def _():
            for t in range(nt):
                to = t ^ me_ref[2]
                put_pieces(
                    lay, me_ref, acc[:, t * cw : (t + 1) * cw], other.at[pl.ds(to, 1)], own.at[pl.ds(to, 1)]
                )

    piece = jax.ShapeDtypeStruct((nt, lay.nz, lay.rows, cw), BF)
    out, _ = run(
        "feed_back", 19, kernel, (steps,),
        [(b, ANY) for b in group.bufs]
        + [(v, row_block(D)) for v in (dsecond, middle, dresult, mixed)]
        + [(gain, one_row(D))],
        [
            (jax.ShapeDtypeStruct((rows, D), BF), row_block(D)),
            (jax.ShapeDtypeStruct((rows, D), BF), row_block(D)),
            (jax.ShapeDtypeStruct((4, D), F32), whole((4, D))),
            (piece, whole(piece.shape)),
            (piece, whole(piece.shape)),
        ],
        [pltpu.VMEM((D, D), BF), pltpu.VMEM((D, D), F32), pltpu.SemaphoreType.DMA],
    )
    return out


def attend_back(lay, run, to, joint, packed, mixed, dmixed, lse, normed, output, last=None, more=()):
    rows = packed.shape[0]
    own, cw = rows // SP, lay.cw
    hl = cw // HEAD_DIM
    w3 = 3 * cw
    np = 0 if last is None else len(last[0])

    def kernel(me_ref, *refs):
        bufs = refs[:8]
        p_ref, m_ref, g_ref, lse_ref, x_ref, go_other, go_own, *refs = refs[8:]
        if last is not None:
            parts = refs[:np]
            in_ref, dm_ref, gain_ref, *refs = refs[np:]
            sum_ref, out_ref, v_ref, other, mine, w, dp, total, sem = refs
        else:
            sum_ref, out_ref, other, mine, w, dp, total, sem = refs
        i = pl.program_id(0)

        @pl.when(i == 0)
        def _():
            start_joint(lay, joint, bufs, me_ref, lambda _: w, lambda _: sem, lambda t: t == to)

        attend_back_kernel(hl, p_ref, m_ref, g_ref, lse_ref, dp, sum_ref)

        @pl.when(i == 0)
        def _():
            wait_all(w, sem)

        dnormed = dotf(dp[...], w[...], 1, 1)
        y = dotf(x_ref[...], dp[...], 0, 0)
        if last is None:
            out_ref[...] = dnormed.astype(BF)
        else:
            for part in parts:
                dnormed += part[...].astype(F32)
            unit, inverse = unit_of(in_ref[...].astype(F32))
            dinput = norm_back(dnormed, unit, inverse, gain_ref[...])
            out_ref[...] = (dm_ref[...].astype(F32) + dinput).astype(BF)
            add_rows(v_ref, [column_sum(dnormed * unit), column_sum(dnormed)])

        @pl.when(i == 0)
        def _():
            total[...] = y

        @pl.when(i > 0)
        def _():
            total[...] += y

        @pl.when(i == own - 1)
        def _():
            put_pieces(lay, me_ref, total[...], other, mine)
            other[:, :, :, w3:] = go_other[...]
            mine[:, :, :, w3:] = go_own[...]

    spec = lambda width: pl.BlockSpec((SP, width), lambda i, m: (i, to ^ m[2]))
    part = pl.BlockSpec((1, lay.nz, lay.rows, cw), lambda i, m: (to, 0, 0, 0))
    piece = jax.ShapeDtypeStruct((1, lay.nz, lay.rows, w3 + cw), BF)
    return run(
        "attend_back", 20, kernel, (own,),
        [(b, ANY) for chain in joint for b in chain.bufs]
        + [
            (packed, spec(w3)),
            (mixed, spec(cw)),
            (dmixed, spec(cw)),
            (lse, pl.BlockSpec((1, 1, hl, LP), lambda i, m: (i, to ^ m[2], 0, 0))),
            (normed, row_block(D)),
            (output[0], part),
            (output[1], part),
        ]
        + ([(x, row_block(D)) for x in (*last[0], last[1], last[2])] + [(last[3], one_row(D))] if last else []),
        [
            (jax.ShapeDtypeStruct((own, 1, 1, w3), F32), pl.BlockSpec((1, 1, 1, w3), lambda i, m: (i, 0, 0, 0))),
            (jax.ShapeDtypeStruct((rows, D), BF), row_block(D)),
        ]
        + ([(jax.ShapeDtypeStruct((2, D), F32), whole((2, D)))] if last else [])
        + [(piece, whole(piece.shape))] * 2,
        [pltpu.VMEM((D, w3), BF), pltpu.VMEM((SP, w3), BF), pltpu.VMEM((D, w3), F32), pltpu.SemaphoreType.DMA],
        more,
    )


def insert_bit(s, b, value):
    return ((s >> b) << (b + 1)) | (value << b) | (s & ((1 << b) - 1))


def along(lay, run, arrays, more=()):
    z, dr, width = arrays[0].shape
    n = len(arrays)
    w = 256 if width % 256 == 0 else 128

    def kernel(me_ref, *refs):
        for k in range(z):
            total = refs[0][k].astype(F32)
            for ref in refs[1:n]:
                total += ref[k].astype(F32)
            refs[n + k][...] = total.astype(BF)

    block = pl.BlockSpec((z, dr, w), lambda s, m: (0, 0, s))
    out = (jax.ShapeDtypeStruct((dr, width), BF), pl.BlockSpec((dr, w), lambda s, m: (0, s)))
    sums, more = run("add_plane", 0, kernel, (width // w,), [(x, block) for x in arrays], [out] * z, (), more)
    return [swap(x, k * 2 * lay.nt, lay.size) if k else x for k, x in enumerate(sums)], more


def total_of(ends):
    total = ends[0].astype(F32)
    for x in ends[1:]:
        total = total + x.astype(F32)
    return total


class Butterfly:
    def __init__(self, lay, reverse, other, own):
        self.lay = lay
        bits = list(range(lay.tbits))
        self.bits = bits[::-1] if reverse else bits
        self.keep, self.got = [own], [swap(other, lay.core, lay.size)]
        self.left = list(range(lay.nt))

    def fold(self, run, more=()):
        bit = self.bits.pop(0)
        n = len(self.left)
        z, dr, width = self.keep[0].shape[-3:]
        one = len(self.keep) == 1
        block = pl.BlockSpec((n, 1, dr, width), lambda s, m: (0, s, 0, 0)) if one else None
        piece = pl.BlockSpec((1, dr, width), lambda s, m: (s, 0, 0))
        k = len(self.keep)

        def kernel(me_ref, *refs):
            for i in range(n):
                a, b = (refs[0][i], refs[1][i]) if one else (refs[i][...], refs[k + i][...])
                refs[2 * k + i][...] = a + b

        shape = jax.ShapeDtypeStruct((z, dr, width), BF)
        sums, more = run(
            "add", 0, kernel, (z,), [(x, block or piece) for x in (*self.keep, *self.got)], [(shape, piece)] * n, (), more
        )
        self.keep = [x for t, x in zip(self.left, sums) if not t >> bit & 1]
        self.got = [swap(x, 1 << bit, self.lay.size) for t, x in zip(self.left, sums) if t >> bit & 1]
        self.left = [t for t in self.left if not t >> bit & 1]
        return more

    def along(self, run, more=()):
        self.ends, more = along(self.lay, run, self.keep + self.got, more)
        return more


class Direct:
    def __init__(self, lay):
        self.lay = lay
        self.parts, self.waiting = [], []

    def start(self, to, other, own):
        self.waiting.append((to, own[0], swap(other[0], self.lay.core, self.lay.size)))

    def spread(self, run, more=()):
        to, own, got = self.waiting.pop(0)
        z, dr, width = own.shape

        def kernel(me_ref, a_ref, b_ref, o_ref):
            o_ref[...] = a_ref[...] + b_ref[...]

        block = pl.BlockSpec((1, dr, width), lambda s, m: (s, 0, 0))
        shape = jax.ShapeDtypeStruct(own.shape, BF)
        (x,), more = run("add_core", 0, kernel, (z,), [(own, block), (got, block)], [(shape, block)], (), more)
        self.parts.append(swap(x, to, self.lay.size))
        return more

    def along(self, run, more=()):
        self.ends, more = along(self.lay, run, [*self.waiting[0][1:], *self.parts], more)
        return more


class Sum:
    def __init__(self, lay, x, combine=jnp.add):
        self.lay, self.x, self.combine = lay, x, combine
        step = 2 * lay.nt
        self.stages = [list(range(1, lay.nt)), [z * step for z in range(1, lay.nz)], [lay.core]]
        self.send()

    def send(self):
        self.got = [swap(self.x, mask, self.lay.size) for mask in self.stages.pop(0)]

    def land(self, passed=None):
        for got in passed or self.got:
            self.x = self.combine(self.x, got)
        if self.stages:
            self.send()
        else:
            self.got = None


def pad_rows(x):
    own = x.shape[0] // SEQ
    return jnp.pad(x.reshape(own, SEQ, D), ((0, 0), (0, SP - SEQ), (0, 0))).reshape(own * SP, D)


def unpad_rows(x):
    own = x.shape[0] // SP
    return x.reshape(own, SP, D)[:, :SEQ].reshape(own * SEQ, D)


def per_device(
    lay,
    tokens,
    first_gain,
    first_shift,
    joint_weight,
    joint_bias,
    output_weight,
    output_bias,
    second_gain,
    second_shift,
    expand_weight,
    expand_bias,
    shrink_weight,
    shrink_bias,
    cotangent,
    image_count,
    threshold,
):
    own = tokens.shape[0] // SEQ
    nt, cw, dr = lay.nt, lay.cw, lay.rows
    half = lay.cols // 2
    hl = cw // HEAD_DIM
    tensor = lax.axis_index("tensor").astype(jnp.int32)
    dp = lax.axis_index("dp").astype(jnp.int32)
    count = image_count[0]
    run = Runner(jnp.stack([dp // 2, dp % 2, tensor, count]))

    split = 3 * cw // 2 if cw % 256 == 0 else 2 * cw
    flat = joint_weight.reshape(dr, 3 * cw)
    joint = [Chain(lay, flat[:, :split], False), Chain(lay, flat[:, split:], True)]
    for chain in joint:
        chain.send()
    small = jnp.concatenate([joint_bias.reshape(-1), expand_bias.reshape(-1)])
    n_small = small.shape[0]
    output = jnp.concatenate([output_weight.T, jnp.pad(small[None], ((0, 15), (0, cw - n_small)))])
    ((output,),) = gate(run, [output])
    output = Shards(lay, output)

    biases = output.bufs[0][:, dr].astype(F32)
    nb = joint_bias.size
    jb = biases[:, :nb].reshape(lay.ndp, nt, 2, hl, HEAD_DIM // lay.ndp)
    jb = jb.transpose(2, 1, 3, 0, 4).reshape(2, nt, 1, cw)
    bias_rows = jnp.concatenate([jb[0], jnp.zeros_like(jb[0]), jb[1]], axis=1).reshape(1, 3 * D)
    eb = biases[:, nb:n_small].reshape(lay.ndp, nt, FF // HEAD_DIM // nt, HEAD_DIM // lay.ndp)
    eb = eb.transpose(1, 2, 0, 3).reshape(nt, 2, half)
    expand_rows = [eb[:, g].reshape(1, nt * half) for g in range(2)]

    image_ids = tensor * own + jnp.arange(own, dtype=jnp.int32)
    image_live = image_ids < count
    inputs = pad_rows(tokens)
    live_rows = jnp.repeat(image_live, SEQ)[:, None]
    dresult = pad_rows(jnp.where(live_rows, cotangent, jnp.zeros_like(cotangent)))
    unit, _ = unit_of(inputs.astype(F32))
    normed = (unit * first_gain + first_shift).astype(BF)
    row = lambda v: v.reshape(1, D)

    def land(chains):
        for chain in chains:
            chain.land()
            chain.send_last() if len(chain.stages) == 1 else chain.send()

    ((joint[0].got, joint[1].got),) = gate(run, [chain.got for chain in joint])
    land(joint)
    shrink_t = (shrink_weight + run.token[0, 0].astype(BF)).T
    feeds = [Chain(lay, expand_weight[:, :half], False), Chain(lay, shrink_t[:, :half], True)]
    rest = jnp.concatenate([expand_weight[:, half:], shrink_t[:, half:]], axis=1)
    for chain in feeds:
        chain.send()
    while len(joint[0].stages) > 2:
        land(joint)
        if len(feeds[0].stages) > 3:
            land(feeds)
    (joint[0].got, joint[1].got), (feeds[0].got, feeds[1].got) = gate(
        run, [chain.got for chain in joint], [chain.got for chain in feeds]
    )
    land(joint)
    while len(feeds[0].stages) > 2:
        land(feeds)
    (joint[0].got, joint[1].got), (feeds[0].got, feeds[1].got), (inputs, dresult, normed), (rest,) = gate(
        run, [chain.got for chain in joint], [chain.got for chain in feeds], [inputs, dresult, normed], [rest]
    )
    for chain in joint:
        chain.share()
    rest = Shards(lay, rest)
    land(feeds)
    packed, mixed, lse, tops = attend_all(lay, run, joint, normed, bias_rows)
    (feeds[0].got, feeds[1].got), = gate(run, [chain.got for chain in feeds])
    for chain in feeds:
        chain.share()
    shrinks = [(feeds[1], 0), (rest, half)]
    middle, second = out_project(
        lay, run, output, mixed, inputs, row(output_bias), row(second_gain), row(second_shift)
    )

    active0, expand_sum0, dsecond, *pieces = feed(
        lay, run, (feeds[0], 0), shrinks[0], second, dresult, expand_rows[0]
    )
    grads = [Butterfly(lay, True, *pieces)]
    active1, expand_sum1, dsecond, *pieces = feed(
        lay, run, (rest, 0), shrinks[1], second, dresult, expand_rows[1], dsecond
    )
    grads.append(Butterfly(lay, False, *pieces))
    for sc in grads:
        sc.fold(run)
    dmiddle, dmixed, sums_two, *out_pieces = feed_back(
        lay, run, output, dsecond, middle, dresult, mixed, row(second_gain)
    )

    packed_sums, dnormed = [], []
    total = Direct(lay)

    def back(to, last=None, more=()):
        (part, out, *rest), more = attend_back(
            lay, run, to, joint, packed, mixed, dmixed, lse, normed, out_pieces, last, more
        )
        packed_sums.append(part)
        total.start(to, *rest[-2:])
        return out, rest[0], list(more)

    def spread(more=()):
        return list(total.spread(run, more))

    for n, to in enumerate(range(nt - 1, 0, -1)):
        if n == 0:
            out, _, more = back(to, None, [grads[0].got[0], grads[1].got[0]])
            grads[0].got[0], grads[1].got[0] = more
        else:
            out = back(to)[0]
        dnormed.append(out)
        if grads[0].bits:
            for sc in grads:
                sc.fold(run)
            if n:
                spread()
        elif not hasattr(grads[0], "ends"):
            for sc in grads:
                sc.along(run)
            spread()
        else:
            at = len(total.parts) - 1
            total.parts[at], *grads[0].ends[1:] = spread([total.parts[at], *grads[0].ends[1:]])
    token_rows, sums_one, _ = back(0, (dnormed, inputs, dmiddle, row(first_gain)))
    grads[1].ends[1:] = spread(grads[1].ends[1:])

    tops = jnp.max(tops, axis=-1).reshape(own, HEADS) / LOG2E
    peak = jnp.max(jnp.where(image_live[:, None], tops, NEG), axis=0)
    peak = jnp.broadcast_to(peak[:, None], (HEADS, 128))
    expand_sum = jnp.stack([expand_sum0.reshape(nt, half), expand_sum1.reshape(nt, half)], axis=1)
    heads = jnp.concatenate([jnp.sum(x, axis=0) for x in packed_sums[::-1]]).reshape(nt, 3, cw)
    heads = heads[jnp.arange(nt) ^ tensor]
    vectors = [sums_two, expand_sum, sums_one, heads[:, 0], heads[:, 2]]
    sums = jnp.concatenate([peak] + [v.reshape(-1, 128) for v in vectors])
    is_peak = lax.broadcasted_iota(jnp.int32, sums.shape, 0) < HEADS
    small = Sum(lay, sums, lambda a, b: jnp.where(is_peak, jnp.maximum(a, b), a + b))
    result, passed = feed_out(lay, run, shrinks[0], active0, middle, None, small.got)
    small.land(passed)
    total.along(run)
    result, passed = feed_out(lay, run, shrinks[1], active1, result, row(shrink_bias), small.got)
    small.land(passed)
    while small.got is not None:
        small.land()

    block_out = unpad_rows(result)
    tokens_grad = unpad_rows(token_rows)
    sums = small.x
    peak = sums[:HEADS, 0]
    at = [HEADS, HEADS + 4 * D // 128, HEADS + (4 * D + FF) // 128, HEADS + (6 * D + FF) // 128]
    sums_two = sums[at[0] : at[1]].reshape(4, D)
    expand_sum = sums[at[1] : at[2]].reshape(FF)
    sums_one = sums[at[2] : at[3]].reshape(2, D)
    bias_sum = sums[at[3] :].reshape(2, D)
    mine = lambda v: lax.dynamic_slice_in_dim(v, dp * dr, dr, v.ndim - 1)
    sums_one, sums_two = mine(sums_one), mine(sums_two)
    share = HEAD_DIM // lay.ndp
    units = FF // HEAD_DIM // nt
    expand_bias_grad = lax.dynamic_slice(
        expand_sum.reshape(FF // HEAD_DIM, HEAD_DIM), (tensor * units, dp * share), (units, share)
    )
    joint_bias_grad = lax.dynamic_slice(
        bias_sum.reshape(2, HEADS, HEAD_DIM), (0, tensor * hl, dp * share), (2, hl, share)
    )

    top = lax.dynamic_slice_in_dim(peak, tensor * hl, hl, 0)
    factors = jnp.sqrt(threshold / jnp.maximum(top, threshold))
    columns = jnp.repeat(factors, HEAD_DIM)
    clipped_joint = (joint_weight[:, 0:2, :].astype(F32) * columns).astype(BF)
    clipped_bias = (joint_bias[0].astype(F32) * factors[:, None]).astype(BF)

    feed_a, feed_b, total = [total_of(g.ends) for g in (*grads, total)]
    joint_grad = total[:, : 3 * cw].reshape(dr, 3, cw)
    output_grad = total[:, 3 * cw :].T
    expand_grad = jnp.concatenate([feed_a[:, :half], feed_b[:, :half]], axis=1)
    shrink_grad = jnp.concatenate([feed_a[:, half:], feed_b[:, half:]], axis=1).T
    return (
        block_out,
        tokens_grad,
        sums_one[0],
        sums_one[1],
        joint_grad,
        joint_bias_grad,
        output_grad,
        sums_two[2],
        sums_two[0],
        sums_two[1],
        expand_grad,
        expand_bias_grad,
        shrink_grad,
        sums_two[3],
        clipped_joint,
        clipped_bias,
        factors,
    )


def solution(mesh):
    placed = (
        P(("dp", "tensor"), None),
        P(),
        P(),
        P("dp", None, "tensor"),
        P(None, "tensor", "dp"),
        P("tensor", "dp"),
        P(),
        P(),
        P(),
        P("dp", "tensor"),
        P("tensor", "dp"),
        P("tensor", "dp"),
        P(),
        P(("dp", "tensor"), None),
        P("dp"),
        P("tensor"),
    )
    lay = Layout(mesh.shape["dp"], mesh.shape["tensor"])
    return jax.shard_map(
        partial(per_device, lay),
        mesh=mesh,
        in_specs=placed,
        out_specs=(
            P(("dp", "tensor"), None),
            P(("dp", "tensor"), None),
            P("dp"),
            P("dp"),
            P("dp", None, "tensor"),
            P(None, "tensor", "dp"),
            P("tensor", "dp"),
            P("dp"),
            P("dp"),
            P("dp"),
            P("dp", "tensor"),
            P("tensor", "dp"),
            P("tensor", "dp"),
            P("dp"),
            P("dp", None, "tensor"),
            P("tensor", "dp"),
            P("tensor"),
        ),
        check_vma=False,
    )
```

```python
from functools import partial

import jax
import jax.numpy as jnp
from jax import lax
from jax.experimental import pallas as pl
from jax.experimental.pallas import tpu as pltpu
from jax.sharding import PartitionSpec as P

D = 1024
FF = 4096
HEADS = 16
HEAD_DIM = 64
SEQ = 577
SP = 592
LP = 640
LOG2E = 1.4426950408889634
NEG = -1e30
BF = jnp.bfloat16
F32 = jnp.float32
AXES = ("dp", "tensor")
VMEM_LIMIT = 60 * 2**20


def dotf(a, b, ca, cb):
    return lax.dot_general(a, b, (((ca,), (cb,)), ((), ())), preferred_element_type=F32)


def whole(shape):
    zeros = (0,) * len(shape)
    return pl.BlockSpec(shape, lambda *_: zeros)


ANY = pl.BlockSpec(memory_space=pl.ANY)


class Runner:
    def __init__(self, me):
        self.me = me
        self.token = jnp.zeros((8, 128), F32)

    def __call__(self, name, us, kernel, grid, ins, outs, scratch=(), through=()):
        n_in, n_out = len(ins), len(outs)
        through = [self.token] + list(through)
        n = len(through)

        def body(me_ref, *refs):
            first = refs[:n_in]
            second = refs[n_in + n : n_in + n + n_out]
            kernel(me_ref, *first, *second, *refs[n_in + 2 * n + n_out :])

        got = pl.pallas_call(
            body,
            grid_spec=pltpu.PrefetchScalarGridSpec(
                num_scalar_prefetch=1,
                grid=grid,
                in_specs=[spec for _, spec in ins] + [ANY] * n,
                out_specs=[spec for _, spec in outs] + [ANY] * n,
                scratch_shapes=list(scratch),
            ),
            out_shape=[shape for shape, _ in outs] + [jax.ShapeDtypeStruct(a.shape, a.dtype) for a in through],
            input_output_aliases={1 + n_in + i: n_out + i for i in range(n)},
            compiler_params=pltpu.CompilerParams(vmem_limit_bytes=VMEM_LIMIT),
            cost_estimate=pl.CostEstimate(flops=int(us * 1.1e9), bytes_accessed=int(us * 1e6), transcendentals=0),
            name=name,
        )(self.me, *[a for a, _ in ins], *through)
        self.token = got[n_out]
        return got[:n_out], got[n_out + 1 :]


class Layout:
    def __init__(self, ndp, nt):
        self.ndp, self.nt, self.nz = ndp, nt, ndp // 2
        self.size = ndp * nt
        self.rows = D // ndp
        self.cols = FF // nt
        self.tbits = nt.bit_length() - 1
        self.zbits = self.nz.bit_length() - 1
        self.core = nt
        self.cw = D // nt


def stage_mask(lay, bit):
    kind, b = bit
    return (1 << b) if kind == "t" else (lay.nt * 2) << b


def swap(x, mask, size):
    return lax.ppermute(x, AXES, [(i, i ^ mask) for i in range(size)])


class Chain:
    def __init__(self, lay, piece, reverse):
        self.lay = lay
        z = [("z", b) for b in reversed(range(lay.zbits))]
        t = [("t", b) for b in range(lay.tbits)]
        t = t[::-1] if reverse else t
        self.stages = []
        while z or t:
            self.stages.append(z.pop(0) if z and len(z) >= len(t) else t.pop(0))
        self.held, self.offs = piece[None], [(0, 0)]

    def send(self):
        self.got = swap(self.held, stage_mask(self.lay, self.stages[0]), self.lay.size)

    def land(self):
        kind, b = self.stages.pop(0)
        dz, dt = ((1 << b), 0) if kind == "z" else (0, (1 << b))
        self.offs = self.offs + [(z ^ dz, t ^ dt) for z, t in self.offs]
        self.held = jnp.concatenate([self.held, self.got])

    def send_last(self):
        self.send()
        self.bufs = [self.held, None, swap(self.held, self.lay.core, self.lay.size), None]

    def share(self):
        (kind, b), lay = self.stages.pop(0), self.lay
        dz, dt = ((1 << b), 0) if kind == "z" else (0, (1 << b))
        self.bufs[1], self.bufs[3] = self.got, swap(self.got, lay.core, lay.size)
        more = [(z ^ dz, t ^ dt) for z, t in self.offs]
        self.pieces = [
            (2 * c + k, i, z, t, c)
            for c in range(2)
            for k, offs in enumerate((self.offs, more))
            for i, (z, t) in enumerate(offs)
        ]


class Shards:
    def __init__(self, lay, piece):
        self.bufs = [lax.all_gather(piece, AXES)]


def gate(run, *lists):
    flat = [x for some in lists for x in some]
    _, flat = run("gate", 0, lambda *refs: None, (1,), [], [], (), flat)
    flat = list(flat)
    return [[flat.pop(0) for _ in some] for some in lists]


def start_pieces(lay, group, bufs, me_ref, spans, sem, keep=None):
    me = (me_ref[0], me_ref[1], me_ref[2])
    if isinstance(group, Shards):
        pieces = []
        for to in range(lay.nt):
            t = to ^ me[2]
            if keep is None or keep(to):
                pieces += [(0, dp * lay.nt + t, dp * lay.rows, to, t) for dp in range(lay.ndp)]
    else:
        pieces = []
        for b, i, z, t, c in group.pieces:
            if keep is None or keep(t):
                row = pl.multiple_of(((z ^ me[0]) * 2 + (c ^ me[1])) * lay.rows, lay.rows)
                pieces.append((b, i, row, t, t ^ me[2]))
    for b, i, row, to, t in pieces:
        for first, width, place in spans:
            ref, at = place(to, t)
            if not isinstance(at, int):
                at = pl.multiple_of(at, 128)
            pltpu.make_async_copy(
                bufs[b].at[i, pl.ds(0, lay.rows), pl.ds(first, width)],
                ref.at[pl.ds(row, lay.rows), pl.ds(at, width)],
                sem(to),
            ).start()


def wait_all(ref, sem):
    pltpu.make_async_copy(ref, ref, sem).wait()


def flip(x):
    pad = jnp.zeros((LP - x.shape[0], x.shape[1]), x.dtype)
    return jnp.concatenate([x, pad], axis=0).T


def key_rows():
    row = lax.broadcasted_iota(jnp.int32, (16, LP), 0)
    lane = lax.broadcasted_iota(jnp.int32, (16, LP), 1)
    return jnp.where(row < 3, 1.0, jnp.where((row == 3) & (lane >= SEQ), NEG, 0.0)).astype(BF)


def split_rows(v):
    row = lax.broadcasted_iota(jnp.int32, (16, LP), 0)
    hi = v.astype(BF).astype(F32)
    mid = (v - hi).astype(BF).astype(F32)
    lo = v - hi - mid
    rest = jnp.where(row == 2, lo, jnp.where(row == 3, 1.0, 0.0))
    return jnp.where(row == 0, hi, jnp.where(row == 1, mid, rest)).astype(BF)


def split_query(q):
    v = q.astype(F32) * LOG2E
    hi = v.astype(BF)
    return hi, (v - hi.astype(F32)).astype(BF)


def attend_kernel(hl, p_ref, o_ref, lse_ref, top_ref):
    cw = hl * HEAD_DIM
    xt = flip(p_ref[...])
    aux = key_rows()
    none = split_rows(jnp.zeros((1, LP), F32))
    first = lax.broadcasted_iota(jnp.int32, (16, LP), 0) == 0
    ones = jnp.where(first, 1.0, 0.0).astype(BF)
    valid = lax.broadcasted_iota(jnp.int32, (1, LP), 1) < SEQ
    outs = []
    for h in range(hl):
        q = xt[h * HEAD_DIM : (h + 1) * HEAD_DIM]
        k = xt[cw + h * HEAD_DIM : cw + (h + 1) * HEAD_DIM]
        v = xt[2 * cw + h * HEAD_DIM : 2 * cw + (h + 1) * HEAD_DIM]
        hi, lo = split_query(q)
        s = dotf(jnp.concatenate([k, k, aux], 0), jnp.concatenate([hi, lo, none], 0), 0, 0)
        m = jnp.max(s, axis=0, keepdims=True)
        p = jnp.exp2(s - m).astype(BF)
        o = dotf(jnp.concatenate([v, ones], 0), p, 1, 0)
        total = o[HEAD_DIM : HEAD_DIM + 1]
        outs.append((o[:HEAD_DIM] / total).astype(BF))
        lse_ref[0, 0, h : h + 1, :] = m + jnp.log2(total)
        top_ref[0, 0, h : h + 1, :] = jnp.where(valid, m, NEG)
    o_ref[...] = jnp.concatenate(outs, 0).T[:SP]


def attend_back_kernel(hl, p_ref, o_ref, g_ref, lse_ref, d_ref, sum_ref):
    cw = hl * HEAD_DIM
    xt = flip(p_ref[...])
    ot = flip(o_ref[...])
    gt = flip(g_ref[...])
    aux = key_rows()
    ones = jnp.where(lax.broadcasted_iota(jnp.int32, (16, LP), 0) < 3, 1.0, 0.0).astype(BF)
    dq, dk, dv = [], [], []
    for h in range(hl):
        at = slice(h * HEAD_DIM, (h + 1) * HEAD_DIM)
        q = xt[at]
        k = xt[cw + h * HEAD_DIM : cw + (h + 1) * HEAD_DIM]
        v = xt[2 * cw + h * HEAD_DIM : 2 * cw + (h + 1) * HEAD_DIM]
        g = gt[at]
        hi, lo = split_query(q)
        delta = jnp.sum(ot[at].astype(F32) * g.astype(F32), axis=0, keepdims=True)
        minus = split_rows(-lse_ref[0, 0, h : h + 1, :])
        s = dotf(jnp.concatenate([k, k, aux], 0), jnp.concatenate([hi, lo, minus], 0), 0, 0)
        p = jnp.exp2(s)
        d = dotf(jnp.concatenate([v, ones], 0), jnp.concatenate([g, split_rows(-delta)], 0), 0, 0)
        ds = (p * d).astype(BF)
        dv.append(dotf(g, p.astype(BF), 1, 1).astype(BF))
        dq.append((HEAD_DIM**-0.5 * dotf(k, ds, 1, 0)).astype(BF))
        dk.append(dotf(q, ds, 1, 1).astype(BF))
    out = jnp.concatenate(dq + dk + dv, 0).T[:SP]
    d_ref[...] = out
    sum_ref[0, 0, :, :] = jnp.sum(out.astype(F32), axis=0, keepdims=True)


def unit_of(values):
    center = values - jnp.mean(values, axis=-1, keepdims=True)
    inverse = lax.rsqrt(jnp.mean(center * center, axis=-1, keepdims=True) + 1e-05)
    return center * inverse, inverse


def norm_back(grad, unit, inverse, gain):
    scaled = grad * gain
    inner = (
        scaled
        - jnp.mean(scaled, axis=-1, keepdims=True)
        - unit * jnp.mean(scaled * unit, axis=-1, keepdims=True)
    )
    return inner * inverse


def add_rows(ref, rows):
    step = pl.program_id(0)

    @pl.when(step == 0)
    def _():
        for r, row in enumerate(rows):
            ref[r : r + 1, :] = row

    @pl.when(step > 0)
    def _():
        for r, row in enumerate(rows):
            ref[r : r + 1, :] += row


def column_sum(x):
    return jnp.sum(x, axis=0, keepdims=True)


def row_block(width):
    return pl.BlockSpec((SP, width), lambda i, m: (i, 0))


def one_row(width):
    return pl.BlockSpec((1, width), lambda i, m: (0, 0))


def put_pieces(lay, me_ref, y, other, own, first=0):
    dr, width = lay.rows, y.shape[1]
    cs = pl.ds(first, width)
    y = y.astype(BF)
    for c in range(2):

        @pl.when(me_ref[1] == c)
        def _(c=c):
            for z in range(lay.nz):
                at = z ^ me_ref[0]
                a, b = (2 * z + c) * dr, (2 * z + 1 - c) * dr
                own[0, at, :, cs] = y[a : a + dr]
                other[0, at, :, cs] = y[b : b + dr]


def piece_out(lay, width):
    return (
        jax.ShapeDtypeStruct((lay.nt, lay.nz, lay.rows, width), BF),
        pl.BlockSpec((1, lay.nz, lay.rows, width), lambda o, *rest: (o, 0, 0, 0)),
    )


def start_joint(lay, joint, bufs, me_ref, place, sem, keep=None):
    for h, chain in enumerate(joint):
        width = chain.held.shape[-1]
        at = 0 if h == 0 else 3 * lay.cw - width
        spans = [(0, width, lambda to, t: (place(to), at))]
        start_pieces(lay, chain, bufs[4 * h : 4 * h + 4], me_ref, spans, sem, keep)


def prepare(run, tokens, cotangent, gain, shift):
    own = tokens.shape[0] // SEQ

    def kernel(me_ref, x_ref, c_ref, g_ref, s_ref, in_ref, n_ref, d_ref):
        none = jnp.zeros((SP - SEQ, D), F32)
        for i in range(own):
            rows, to = slice(i * SEQ, (i + 1) * SEQ), slice(i * SP, (i + 1) * SP)
            x = jnp.concatenate([x_ref[...].astype(F32)[rows], none])
            in_ref[to, :] = x.astype(BF)
            unit, _ = unit_of(x)
            n_ref[to, :] = (unit * g_ref[...] + s_ref[...]).astype(BF)
            c = jnp.concatenate([c_ref[...].astype(F32)[rows], none])
            live = me_ref[2] * own + i < me_ref[3]
            d_ref[to, :] = jnp.where(live, c, 0.0).astype(BF)

    shape = (jax.ShapeDtypeStruct((own * SP, D), BF), whole((own * SP, D)))
    out, _ = run(
        "prepare", 20, kernel, (1,),
        [(v, whole(v.shape)) for v in (tokens, cotangent, gain, shift)],
        [shape] * 3,
    )
    return out


def attend_all(lay, run, joint, normed, bias_rows):
    rows = normed.shape[0]
    own, cw = rows // SP, lay.cw
    hl = cw // HEAD_DIM
    wide = 3 * cw

    def kernel(me_ref, *refs):
        bufs = refs[:8]
        x_ref, b_ref, p_ref, o_ref, lse_ref, top_ref, w, sem = refs[8:]
        o, i = pl.program_id(0), pl.program_id(1)

        for k in range(1, lay.nt):

            @pl.when((o == k - 1) & (i == 0))
            def _(k=k):
                keep = lambda to: to == k or (k == 1 and to == 0)
                start_joint(lay, joint, bufs, me_ref, lambda to: w.at[to], lambda to: sem.at[to], keep)

        @pl.when(i == 0)
        def _():
            wait_all(w.at[o], sem.at[o])

        y = jnp.dot(x_ref[...], w[o], preferred_element_type=F32) + b_ref[...]
        p_ref[:, :cw] = (y[:, :cw] * HEAD_DIM**-0.5).astype(BF)
        p_ref[:, cw:] = y[:, cw:].astype(BF)
        attend_kernel(hl, p_ref, o_ref, lse_ref, top_ref)

    stat = pl.BlockSpec((1, 1, hl, LP), lambda o, i, m: (i, o ^ m[2], 0, 0))
    stat_shape = jax.ShapeDtypeStruct((own, lay.nt, hl, LP), F32)
    out, _ = run(
        "attend", 36, kernel, (lay.nt, own),
        [(b, ANY) for chain in joint for b in chain.bufs]
        + [
            (normed, pl.BlockSpec((SP, D), lambda o, i, m: (i, 0))),
            (bias_rows, pl.BlockSpec((1, wide), lambda o, i, m: (0, o ^ m[2]))),
        ],
        [
            (jax.ShapeDtypeStruct((rows, lay.nt * wide), BF), pl.BlockSpec((SP, wide), lambda o, i, m: (i, o ^ m[2]))),
            (jax.ShapeDtypeStruct((rows, D), BF), pl.BlockSpec((SP, cw), lambda o, i, m: (i, o ^ m[2]))),
            (stat_shape, stat),
            (stat_shape, stat),
        ],
        [pltpu.VMEM((lay.nt, D, wide), BF), pltpu.SemaphoreType.DMA((lay.nt,))],
    )
    return out


def out_project(lay, run, group, mixed, inputs, bias, gain, shift):
    rows = inputs.shape[0]
    cw = lay.cw
    nb = len(group.bufs)

    def kernel(me_ref, *refs):
        bufs = refs[:nb]
        m_ref, x_ref, b_ref, g_ref, s_ref, mid_ref, sec_ref, w, sem = refs[nb:]

        @pl.when(pl.program_id(0) == 0)
        def _():
            spans = [(0, cw, lambda to, t: (w, t * cw))]
            start_pieces(lay, group, bufs, me_ref, spans, lambda to: sem)
            wait_all(w, sem)

        middle = x_ref[...].astype(F32) + dotf(m_ref[...], w[...], 1, 1) + b_ref[...]
        mid_ref[...] = middle.astype(BF)
        unit, _ = unit_of(middle)
        sec_ref[...] = (unit * g_ref[...] + s_ref[...]).astype(BF)

    out, _ = run(
        "out_project", 9, kernel, (rows // SP,),
        [(b, ANY) for b in group.bufs]
        + [(mixed, row_block(D)), (inputs, row_block(D))]
        + [(v, one_row(D)) for v in (bias, gain, shift)],
        [
            (jax.ShapeDtypeStruct((rows, D), BF), row_block(D)),
            (jax.ShapeDtypeStruct((rows, D), BF), row_block(D)),
        ],
        [pltpu.VMEM((D, D), BF), pltpu.SemaphoreType.DMA],
    )
    return out


def feed(lay, run, expand, shrink, second, dresult, bias, dsecond=None):
    rows = second.shape[0]
    half = lay.cols // 2
    more = dsecond is not None
    (group_e, first_e), (group_s, first_s) = expand, shrink
    ne, ns = len(group_e.bufs), len(group_s.bufs)

    def kernel(me_ref, *refs):
        bufs_e, bufs_s = refs[:ne], refs[ne : ne + ns]
        x_ref, g_ref, b_ref, *refs = refs[ne + ns :]
        if more:
            before, *refs = refs
        a_ref, s_ref, sec_ref, other, mine, we, ws, d_s, acc, sem_e, sem_s, sem = refs
        o = pl.program_id(0)

        def fetch(k):
            keep = lambda to: to == k
            spans = [(first_e, half, lambda to, t: (we.at[to], 0))]
            start_pieces(lay, group_e, bufs_e, me_ref, spans, lambda to: sem_e.at[to], keep)
            spans = [(first_s, half, lambda to, t: (ws.at[to], 0))]
            start_pieces(lay, group_s, bufs_s, me_ref, spans, lambda to: sem_s.at[to], keep)

        for k in range(1, lay.nt):

            @pl.when(o == k - 1)
            def _(k=k):
                if k == 1:
                    fetch(0)
                fetch(k)

        @pl.when(o == 0)
        def _():
            if more:
                pltpu.make_async_copy(before, acc, sem).start()
                pltpu.make_async_copy(before, acc, sem).wait()
            else:
                acc[...] = jnp.zeros_like(acc)

        wait_all(we.at[o], sem_e.at[o])
        wait_all(ws.at[o], sem_s.at[o])
        total = None
        for r in range(rows // SP):
            rs = slice(r * SP, (r + 1) * SP)
            hidden = jnp.dot(x_ref[rs, :], we[o], preferred_element_type=F32) + b_ref[...]
            dact = jnp.dot(g_ref[rs, :], ws[o], preferred_element_type=F32)
            hidden = hidden.astype(BF)
            sigma = 0.5 + 0.5 * jnp.tanh(0.851 * hidden)
            active = hidden * sigma
            a_ref[rs, :] = active
            dh = dact.astype(BF) * (sigma + 1.702 * active * (1.0 - sigma))
            d_s[rs, :] = dh
            part = column_sum(dh.astype(F32))
            total = part if total is None else total + part
            acc[rs, :] += dotf(dh, we[o], 1, 1)
        s_ref[...] = total
        put_pieces(lay, me_ref, dotf(x_ref[...], d_s[...], 0, 0), other, mine)
        put_pieces(lay, me_ref, dotf(g_ref[...], a_ref[...], 0, 0), other, mine, half)

        @pl.when(o == lay.nt - 1)
        def _():
            sec_ref[...] = acc[...].astype(sec_ref.dtype)

    line = pl.BlockSpec((1, half), lambda o, m: (0, o ^ m[2]))
    full = pl.BlockSpec((rows, D), lambda o, m: (0, 0))
    weights = pltpu.VMEM((lay.nt, D, half), BF)
    sems = pltpu.SemaphoreType.DMA((lay.nt,))
    out, _ = run(
        "feed", 40, kernel, (lay.nt,),
        [(b, ANY) for b in (*group_e.bufs, *group_s.bufs)]
        + [(second, full), (dresult, full), (bias, line)] + ([(dsecond, ANY)] if more else []),
        [
            (jax.ShapeDtypeStruct((rows, lay.nt * half), BF), pl.BlockSpec((rows, half), lambda o, m: (0, o ^ m[2]))),
            (jax.ShapeDtypeStruct((1, lay.nt * half), F32), line),
            (jax.ShapeDtypeStruct((rows, D), BF if more else F32), full),
        ]
        + [piece_out(lay, 2 * half)] * 2,
        [
            weights,
            weights,
            pltpu.VMEM((rows, half), BF),
            pltpu.VMEM((rows, D), F32),
            sems,
            sems,
            pltpu.SemaphoreType.DMA,
        ],
    )
    return out


def feed_out(lay, run, shrink, active, base, bias=None, more=()):
    rows = base.shape[0]
    own = rows // SP
    half = lay.cols // 2
    wide = lay.nt * half
    group, first = shrink
    nb = len(group.bufs)

    def kernel(me_ref, *refs):
        bufs = refs[:nb]
        a_ref, base_ref, *refs = refs[nb:]
        o_ref, w, sem = refs[-3:]

        @pl.when(pl.program_id(0) == 0)
        def _():
            spans = [(first, half, lambda to, t: (w, t * half))]
            start_pieces(lay, group, bufs, me_ref, spans, lambda to: sem)
            wait_all(w, sem)

        out = base_ref[...].astype(F32) + dotf(a_ref[...], w[...], 1, 1)
        if bias is None:
            o_ref[...] = out
        else:
            live = me_ref[2] * own + pl.program_id(0) < me_ref[3]
            o_ref[...] = jnp.where(live, out + refs[0][...], 0.0).astype(BF)

    (result,), more = run(
        "feed_out", 12, kernel, (own,),
        [(b, ANY) for b in group.bufs]
        + [(active, row_block(wide)), (base, row_block(D))]
        + ([] if bias is None else [(bias, one_row(D))]),
        [(jax.ShapeDtypeStruct((rows, D), F32 if bias is None else BF), row_block(D))],
        [pltpu.VMEM((D, wide), BF), pltpu.SemaphoreType.DMA],
        more,
    )
    return result, more


def feed_back(lay, run, group, dsecond, middle, dresult, mixed, gain):
    rows = middle.shape[0]
    cw, nt = lay.cw, lay.nt
    steps = rows // SP

    nb = len(group.bufs)

    def kernel(me_ref, *refs):
        bufs = refs[:nb]
        d_ref, mid_ref, g_ref, m_ref, n_ref, dm_ref, dx_ref, v_ref, other, own, w, acc, sem = refs[nb:]
        i = pl.program_id(0)

        @pl.when(i == 0)
        def _():
            spans = [(0, cw, lambda to, t: (w, t * cw))]
            start_pieces(lay, group, bufs, me_ref, spans, lambda to: sem)
            wait_all(w, sem)

        dsecond = d_ref[...].astype(F32)
        unit, inverse = unit_of(mid_ref[...].astype(F32))
        dout = g_ref[...].astype(F32)
        dmiddle = dout + norm_back(dsecond, unit, inverse, n_ref[...])
        dbranch = dmiddle.astype(BF)
        dm_ref[...] = dbranch
        dx_ref[...] = jnp.dot(dbranch, w[...], preferred_element_type=F32).astype(BF)
        sums = [dsecond * unit, dsecond, dbranch.astype(F32), dout]
        add_rows(v_ref, [column_sum(v) for v in sums])
        y = dotf(dbranch, m_ref[...], 0, 0)

        @pl.when(i == 0)
        def _():
            acc[...] = y

        @pl.when(i > 0)
        def _():
            acc[...] += y

        @pl.when(i == steps - 1)
        def _():
            for t in range(nt):
                to = t ^ me_ref[2]
                put_pieces(
                    lay, me_ref, acc[:, t * cw : (t + 1) * cw], other.at[pl.ds(to, 1)], own.at[pl.ds(to, 1)]
                )

    piece = jax.ShapeDtypeStruct((nt, lay.nz, lay.rows, cw), BF)
    out, _ = run(
        "feed_back", 19, kernel, (steps,),
        [(b, ANY) for b in group.bufs]
        + [(v, row_block(D)) for v in (dsecond, middle, dresult, mixed)]
        + [(gain, one_row(D))],
        [
            (jax.ShapeDtypeStruct((rows, D), BF), row_block(D)),
            (jax.ShapeDtypeStruct((rows, D), BF), row_block(D)),
            (jax.ShapeDtypeStruct((4, D), F32), whole((4, D))),
            (piece, whole(piece.shape)),
            (piece, whole(piece.shape)),
        ],
        [pltpu.VMEM((D, D), BF), pltpu.VMEM((D, D), F32), pltpu.SemaphoreType.DMA],
    )
    return out


def attend_back(lay, run, to, joint, packed, mixed, dmixed, lse, normed, output, last=None, more=()):
    rows = packed.shape[0]
    own, cw = rows // SP, lay.cw
    hl = cw // HEAD_DIM
    w3 = 3 * cw
    np = 0 if last is None else len(last[0])

    def kernel(me_ref, *refs):
        bufs = refs[:8]
        p_ref, m_ref, g_ref, lse_ref, x_ref, go_other, go_own, *refs = refs[8:]
        if last is not None:
            parts = refs[:np]
            in_ref, dm_ref, gain_ref, *refs = refs[np:]
            sum_ref, out_ref, v_ref, other, mine, w, dp, total, sem = refs
        else:
            sum_ref, out_ref, other, mine, w, dp, total, sem = refs
        i = pl.program_id(0)

        @pl.when(i == 0)
        def _():
            start_joint(lay, joint, bufs, me_ref, lambda _: w, lambda _: sem, lambda t: t == to)

        attend_back_kernel(hl, p_ref, m_ref, g_ref, lse_ref, dp, sum_ref)

        @pl.when(i == 0)
        def _():
            wait_all(w, sem)

        dnormed = dotf(dp[...], w[...], 1, 1)
        y = dotf(x_ref[...], dp[...], 0, 0)
        if last is None:
            out_ref[...] = dnormed.astype(BF)
        else:
            for part in parts:
                dnormed += part[...].astype(F32)
            unit, inverse = unit_of(in_ref[...].astype(F32))
            dinput = norm_back(dnormed, unit, inverse, gain_ref[...])
            out_ref[...] = (dm_ref[...].astype(F32) + dinput).astype(BF)
            add_rows(v_ref, [column_sum(dnormed * unit), column_sum(dnormed)])

        @pl.when(i == 0)
        def _():
            total[...] = y

        @pl.when(i > 0)
        def _():
            total[...] += y

        @pl.when(i == own - 1)
        def _():
            put_pieces(lay, me_ref, total[...], other, mine)
            other[:, :, :, w3:] = go_other[...]
            mine[:, :, :, w3:] = go_own[...]

    spec = lambda width: pl.BlockSpec((SP, width), lambda i, m: (i, to ^ m[2]))
    part = pl.BlockSpec((1, lay.nz, lay.rows, cw), lambda i, m: (to, 0, 0, 0))
    piece = jax.ShapeDtypeStruct((1, lay.nz, lay.rows, w3 + cw), BF)
    return run(
        "attend_back", 20, kernel, (own,),
        [(b, ANY) for chain in joint for b in chain.bufs]
        + [
            (packed, spec(w3)),
            (mixed, spec(cw)),
            (dmixed, spec(cw)),
            (lse, pl.BlockSpec((1, 1, hl, LP), lambda i, m: (i, to ^ m[2], 0, 0))),
            (normed, row_block(D)),
            (output[0], part),
            (output[1], part),
        ]
        + ([(x, row_block(D)) for x in (*last[0], last[1], last[2])] + [(last[3], one_row(D))] if last else []),
        [
            (jax.ShapeDtypeStruct((own, 1, 1, w3), F32), pl.BlockSpec((1, 1, 1, w3), lambda i, m: (i, 0, 0, 0))),
            (jax.ShapeDtypeStruct((rows, D), BF), row_block(D)),
        ]
        + ([(jax.ShapeDtypeStruct((2, D), F32), whole((2, D)))] if last else [])
        + [(piece, whole(piece.shape))] * 2,
        [pltpu.VMEM((D, w3), BF), pltpu.VMEM((SP, w3), BF), pltpu.VMEM((D, w3), F32), pltpu.SemaphoreType.DMA],
        more,
    )


def insert_bit(s, b, value):
    return ((s >> b) << (b + 1)) | (value << b) | (s & ((1 << b) - 1))


def along(lay, run, arrays, more=()):
    z, dr, width = arrays[0].shape
    n = len(arrays)
    w = width // 2

    def kernel(me_ref, *refs):
        for k in range(z):
            total = refs[0][k].astype(F32)
            for ref in refs[1:n]:
                total += ref[k].astype(F32)
            refs[n + k][...] = total.astype(BF)

    block = pl.BlockSpec((z, dr, w), lambda s, m: (0, 0, s))
    out = (jax.ShapeDtypeStruct((dr, width), BF), pl.BlockSpec((dr, w), lambda s, m: (0, s)))
    sums, more = run("add_plane", 0, kernel, (width // w,), [(x, block) for x in arrays], [out] * z, (), more)
    return [swap(x, k * 2 * lay.nt, lay.size) if k else x for k, x in enumerate(sums)], more


def total_of(ends):
    total = ends[0].astype(F32)
    for x in ends[1:]:
        total = total + x.astype(F32)
    return total


class Butterfly:
    def __init__(self, lay, reverse, other, own):
        self.lay = lay
        bits = list(range(lay.tbits))
        self.bits = bits[::-1] if reverse else bits
        self.keep, self.got = [own], [swap(other, lay.core, lay.size)]
        self.left = list(range(lay.nt))

    def fold(self, run, more=()):
        bit = self.bits.pop(0)
        n = len(self.left)
        z, dr, width = self.keep[0].shape[-3:]
        one = len(self.keep) == 1
        block = pl.BlockSpec((n, 1, dr, width), lambda s, m: (0, s, 0, 0)) if one else None
        deep = 1 if one else z // 2
        piece = pl.BlockSpec((deep, dr, width), lambda s, m: (s, 0, 0))
        k = len(self.keep)

        def kernel(me_ref, *refs):
            for i in range(n):
                a, b = (refs[0][i], refs[1][i]) if one else (refs[i][...], refs[k + i][...])
                refs[2 * k + i][...] = a + b

        shape = jax.ShapeDtypeStruct((z, dr, width), BF)
        sums, more = run(
            "add", 0, kernel, (z // deep,), [(x, block or piece) for x in (*self.keep, *self.got)], [(shape, piece)] * n, (), more
        )
        self.keep = [x for t, x in zip(self.left, sums) if not t >> bit & 1]
        self.got = [swap(x, 1 << bit, self.lay.size) for t, x in zip(self.left, sums) if t >> bit & 1]
        self.left = [t for t in self.left if not t >> bit & 1]
        return more

    def along(self, run, more=()):
        self.ends, more = along(self.lay, run, self.keep + self.got, more)
        return more


class Direct:
    def __init__(self, lay):
        self.lay = lay
        self.parts, self.waiting = [], []

    def start(self, to, other, own):
        self.waiting.append((to, own[0], swap(other[0], self.lay.core, self.lay.size)))

    def spread(self, run, more=()):
        to, own, got = self.waiting.pop(0)
        z, dr, width = own.shape

        def kernel(me_ref, a_ref, b_ref, o_ref):
            o_ref[...] = a_ref[...] + b_ref[...]

        block = pl.BlockSpec((z, dr, width), lambda s, m: (0, 0, 0))
        shape = jax.ShapeDtypeStruct(own.shape, BF)
        (x,), more = run("add_core", 0, kernel, (1,), [(own, block), (got, block)], [(shape, block)], (), more)
        self.parts.append(swap(x, to, self.lay.size))
        return more

    def along(self, run, more=()):
        self.ends, more = along(self.lay, run, [*self.waiting[0][1:], *self.parts], more)
        return more


def unpad_rows(x):
    own = x.shape[0] // SP
    return x.reshape(own, SP, D)[:, :SEQ].reshape(own * SEQ, D)


def per_device(
    lay,
    tokens,
    first_gain,
    first_shift,
    joint_weight,
    joint_bias,
    output_weight,
    output_bias,
    second_gain,
    second_shift,
    expand_weight,
    expand_bias,
    shrink_weight,
    shrink_bias,
    cotangent,
    image_count,
    threshold,
):
    own = tokens.shape[0] // SEQ
    nt, cw, dr = lay.nt, lay.cw, lay.rows
    half = lay.cols // 2
    hl = cw // HEAD_DIM
    tensor = lax.axis_index("tensor").astype(jnp.int32)
    dp = lax.axis_index("dp").astype(jnp.int32)
    count = image_count[0]
    run = Runner(jnp.stack([dp // 2, dp % 2, tensor, count]))

    split = 3 * cw // 2 if cw % 256 == 0 else 2 * cw
    flat = joint_weight.reshape(dr, 3 * cw)
    joint = [Chain(lay, flat[:, :split], False), Chain(lay, flat[:, split:], True)]
    for chain in joint:
        chain.send()
    small = jnp.concatenate([joint_bias.reshape(-1), expand_bias.reshape(-1)])
    n_small = small.shape[0]
    output = jnp.concatenate([output_weight.T, jnp.pad(small[None], ((0, 15), (0, cw - n_small)))])
    (joint[0].got, joint[1].got), (output,) = gate(run, [chain.got for chain in joint], [output])
    output = Shards(lay, output)

    biases = output.bufs[0][:, dr].astype(F32)
    nb = joint_bias.size
    jb = biases[:, :nb].reshape(lay.ndp, nt, 2, hl, HEAD_DIM // lay.ndp)
    jb = jb.transpose(2, 1, 3, 0, 4).reshape(2, nt, 1, cw)
    bias_rows = jnp.concatenate([jb[0], jnp.zeros_like(jb[0]), jb[1]], axis=1).reshape(1, 3 * D)
    eb = biases[:, nb:n_small].reshape(lay.ndp, nt, FF // HEAD_DIM // nt, HEAD_DIM // lay.ndp)
    eb = eb.transpose(1, 2, 0, 3).reshape(nt, 2, half)
    expand_rows = [eb[:, g].reshape(1, nt * half) for g in range(2)]

    image_ids = tensor * own + jnp.arange(own, dtype=jnp.int32)
    image_live = image_ids < count
    row = lambda v: v.reshape(1, D)

    def land(chains):
        for chain in chains:
            chain.land()
            chain.send_last() if len(chain.stages) == 1 else chain.send()

    land(joint)
    shrink_t = (shrink_weight + run.token[0, 0].astype(BF)).T
    feeds = [Chain(lay, expand_weight[:, :half], False), Chain(lay, shrink_t[:, :half], True)]
    rest = jnp.concatenate([expand_weight[:, half:], shrink_t[:, half:]], axis=1)
    for chain in feeds:
        chain.send()
    while len(joint[0].stages) > 2:
        land(joint)
        if len(feeds[0].stages) > 3:
            land(feeds)
    (joint[0].got, joint[1].got), (feeds[0].got, feeds[1].got) = gate(
        run, [chain.got for chain in joint], [chain.got for chain in feeds]
    )
    land(joint)
    while len(feeds[0].stages) > 2:
        land(feeds)
    inputs, normed, dresult = prepare(run, tokens, cotangent, row(first_gain), row(first_shift))
    (joint[0].got, joint[1].got), (feeds[0].got, feeds[1].got), (rest,) = gate(
        run, [chain.got for chain in joint], [chain.got for chain in feeds], [rest]
    )
    for chain in joint:
        chain.share()
    rest = Shards(lay, rest)
    land(feeds)
    packed, mixed, lse, tops = attend_all(lay, run, joint, normed, bias_rows)
    (feeds[0].got, feeds[1].got), = gate(run, [chain.got for chain in feeds])
    for chain in feeds:
        chain.share()
    shrinks = [(feeds[1], 0), (rest, half)]
    middle, second = out_project(
        lay, run, output, mixed, inputs, row(output_bias), row(second_gain), row(second_shift)
    )

    active0, expand_sum0, dsecond, *pieces = feed(
        lay, run, (feeds[0], 0), shrinks[0], second, dresult, expand_rows[0]
    )
    grads = [Butterfly(lay, True, *pieces)]
    active1, expand_sum1, dsecond, *pieces = feed(
        lay, run, (rest, 0), shrinks[1], second, dresult, expand_rows[1], dsecond
    )
    grads.append(Butterfly(lay, False, *pieces))
    for sc in grads:
        sc.fold(run)
    dmiddle, dmixed, sums_two, *out_pieces = feed_back(
        lay, run, output, dsecond, middle, dresult, mixed, row(second_gain)
    )

    packed_sums, dnormed = [], []
    total = Direct(lay)

    def back(to, last=None, more=()):
        (part, out, *rest), more = attend_back(
            lay, run, to, joint, packed, mixed, dmixed, lse, normed, out_pieces, last, more
        )
        packed_sums.append(part)
        total.start(to, *rest[-2:])
        return out, rest[0], list(more)

    def spread(more=()):
        return list(total.spread(run, more))

    for n, to in enumerate(range(nt - 1, 0, -1)):
        if n == 0:
            out, _, more = back(to, None, [grads[0].got[0], grads[1].got[0]])
            grads[0].got[0], grads[1].got[0] = more
        else:
            out = back(to)[0]
        dnormed.append(out)
        if grads[0].bits:
            for sc in grads:
                sc.fold(run)
            if n:
                spread()
        elif not hasattr(grads[0], "ends"):
            for sc in grads:
                sc.along(run)
            spread()
        else:
            at = len(total.parts) - 1
            total.parts[at], *grads[0].ends[1:] = spread([total.parts[at], *grads[0].ends[1:]])
    token_rows, sums_one, _ = back(0, (dnormed, inputs, dmiddle, row(first_gain)))
    grads[1].ends[1:] = spread(grads[1].ends[1:])

    tops = jnp.max(tops, axis=-1).reshape(own, HEADS) / LOG2E
    peak = jnp.max(jnp.where(image_live[:, None], tops, NEG), axis=0)
    peak = jnp.broadcast_to(peak[:, None], (HEADS, 128))
    expand_sum = jnp.stack([expand_sum0.reshape(nt, half), expand_sum1.reshape(nt, half)], axis=1)
    heads = jnp.concatenate([jnp.sum(x, axis=0) for x in packed_sums[::-1]]).reshape(nt, 3, cw)
    heads = heads[jnp.arange(nt) ^ tensor]
    vectors = [sums_two, expand_sum, sums_one, heads[:, 0], heads[:, 2]]
    sums = jnp.concatenate([peak] + [v.reshape(-1, 128) for v in vectors])
    sums = lax.all_gather(sums, AXES)
    result, _ = feed_out(lay, run, shrinks[0], active0, middle)
    total.along(run)
    result, _ = feed_out(lay, run, shrinks[1], active1, result, row(shrink_bias))

    block_out = unpad_rows(result)
    tokens_grad = unpad_rows(token_rows)
    peak = jnp.max(sums[:, :HEADS, 0], axis=0)
    sums = jnp.sum(sums, axis=0)
    at = [HEADS, HEADS + 4 * D // 128, HEADS + (4 * D + FF) // 128, HEADS + (6 * D + FF) // 128]
    sums_two = sums[at[0] : at[1]].reshape(4, D)
    expand_sum = sums[at[1] : at[2]].reshape(FF)
    sums_one = sums[at[2] : at[3]].reshape(2, D)
    bias_sum = sums[at[3] :].reshape(2, D)
    mine = lambda v: lax.dynamic_slice_in_dim(v, dp * dr, dr, v.ndim - 1)
    sums_one, sums_two = mine(sums_one), mine(sums_two)
    share = HEAD_DIM // lay.ndp
    units = FF // HEAD_DIM // nt
    expand_bias_grad = lax.dynamic_slice(
        expand_sum.reshape(FF // HEAD_DIM, HEAD_DIM), (tensor * units, dp * share), (units, share)
    )
    joint_bias_grad = lax.dynamic_slice(
        bias_sum.reshape(2, HEADS, HEAD_DIM), (0, tensor * hl, dp * share), (2, hl, share)
    )

    top = lax.dynamic_slice_in_dim(peak, tensor * hl, hl, 0)
    factors = jnp.sqrt(threshold / jnp.maximum(top, threshold))
    columns = jnp.repeat(factors, HEAD_DIM)
    clipped_joint = (joint_weight[:, 0:2, :].astype(F32) * columns).astype(BF)
    clipped_bias = (joint_bias[0].astype(F32) * factors[:, None]).astype(BF)

    feed_a, feed_b, total = [total_of(g.ends) for g in (*grads, total)]
    joint_grad = total[:, : 3 * cw].reshape(dr, 3, cw)
    output_grad = total[:, 3 * cw :].T
    expand_grad = jnp.concatenate([feed_a[:, :half], feed_b[:, :half]], axis=1)
    shrink_grad = jnp.concatenate([feed_a[:, half:], feed_b[:, half:]], axis=1).T
    return (
        block_out,
        tokens_grad,
        sums_one[0],
        sums_one[1],
        joint_grad,
        joint_bias_grad,
        output_grad,
        sums_two[2],
        sums_two[0],
        sums_two[1],
        expand_grad,
        expand_bias_grad,
        shrink_grad,
        sums_two[3],
        clipped_joint,
        clipped_bias,
        factors,
    )


def solution(mesh):
    placed = (
        P(("dp", "tensor"), None),
        P(),
        P(),
        P("dp", None, "tensor"),
        P(None, "tensor", "dp"),
        P("tensor", "dp"),
        P(),
        P(),
        P(),
        P("dp", "tensor"),
        P("tensor", "dp"),
        P("tensor", "dp"),
        P(),
        P(("dp", "tensor"), None),
        P("dp"),
        P("tensor"),
    )
    lay = Layout(mesh.shape["dp"], mesh.shape["tensor"])
    return jax.shard_map(
        partial(per_device, lay),
        mesh=mesh,
        in_specs=placed,
        out_specs=(
            P(("dp", "tensor"), None),
            P(("dp", "tensor"), None),
            P("dp"),
            P("dp"),
            P("dp", None, "tensor"),
            P(None, "tensor", "dp"),
            P("tensor", "dp"),
            P("dp"),
            P("dp"),
            P("dp"),
            P("dp", "tensor"),
            P("tensor", "dp"),
            P("tensor", "dp"),
            P("dp"),
            P("dp", None, "tensor"),
            P("tensor", "dp"),
            P("tensor"),
        ),
        check_vma=False,
    )
```

```python
from functools import partial

import jax
import jax.numpy as jnp
from jax import lax
from jax.experimental import pallas as pl
from jax.experimental.pallas import tpu as pltpu
from jax.sharding import PartitionSpec as P

D = 1024
FF = 4096
HEADS = 16
HEAD_DIM = 64
SEQ = 577
SP = 592
LP = 640
LOG2E = 1.4426950408889634
NEG = -1e30
BF = jnp.bfloat16
F32 = jnp.float32
AXES = ("dp", "tensor")
VMEM_LIMIT = 64 * 2**20 - 2**18


def dotf(a, b, ca, cb):
    return lax.dot_general(a, b, (((ca,), (cb,)), ((), ())), preferred_element_type=F32)


def whole(shape):
    zeros = (0,) * len(shape)
    return pl.BlockSpec(shape, lambda *_: zeros)


ANY = pl.BlockSpec(memory_space=pl.ANY)


class Runner:
    def __init__(self, me):
        self.me = me
        self.token = jnp.zeros((8, 128), F32)

    def __call__(self, name, us, kernel, grid, ins, outs, scratch=(), through=()):
        n_in, n_out = len(ins), len(outs)
        through = [self.token] + list(through)
        n = len(through)

        def body(me_ref, *refs):
            first = refs[:n_in]
            second = refs[n_in + n : n_in + n + n_out]
            kernel(me_ref, *first, *second, *refs[n_in + 2 * n + n_out :])

        got = pl.pallas_call(
            body,
            grid_spec=pltpu.PrefetchScalarGridSpec(
                num_scalar_prefetch=1,
                grid=grid,
                in_specs=[spec for _, spec in ins] + [ANY] * n,
                out_specs=[spec for _, spec in outs] + [ANY] * n,
                scratch_shapes=list(scratch),
            ),
            out_shape=[shape for shape, _ in outs] + [jax.ShapeDtypeStruct(a.shape, a.dtype) for a in through],
            input_output_aliases={1 + n_in + i: n_out + i for i in range(n)},
            compiler_params=pltpu.CompilerParams(vmem_limit_bytes=VMEM_LIMIT),
            cost_estimate=pl.CostEstimate(flops=int(us * 1.1e9), bytes_accessed=int(us * 1e6), transcendentals=0),
            name=name,
        )(self.me, *[a for a, _ in ins], *through)
        self.token = got[n_out]
        return got[:n_out], got[n_out + 1 :]


class Layout:
    def __init__(self, ndp, nt):
        self.ndp, self.nt, self.nz = ndp, nt, ndp // 2
        self.size = ndp * nt
        self.rows = D // ndp
        self.cols = FF // nt
        self.tbits = nt.bit_length() - 1
        self.zbits = self.nz.bit_length() - 1
        self.core = nt
        self.cw = D // nt


def stage_mask(lay, bit):
    kind, b = bit
    return (1 << b) if kind == "t" else (lay.nt * 2) << b


def swap(x, mask, size):
    return lax.ppermute(x, AXES, [(i, i ^ mask) for i in range(size)])


class Chain:
    def __init__(self, lay, piece, reverse):
        self.lay = lay
        z = [("z", b) for b in reversed(range(lay.zbits))]
        t = [("t", b) for b in range(lay.tbits)]
        t = t[::-1] if reverse else t
        self.stages = []
        while z or t:
            self.stages.append(z.pop(0) if z and len(z) >= len(t) else t.pop(0))
        self.held, self.offs = piece[None], [(0, 0)]

    def send(self):
        self.got = swap(self.held, stage_mask(self.lay, self.stages[0]), self.lay.size)

    def land(self):
        kind, b = self.stages.pop(0)
        dz, dt = ((1 << b), 0) if kind == "z" else (0, (1 << b))
        self.offs = self.offs + [(z ^ dz, t ^ dt) for z, t in self.offs]
        self.held = jnp.concatenate([self.held, self.got])

    def send_last(self):
        self.send()
        self.bufs = [self.held, None, swap(self.held, self.lay.core, self.lay.size), None]

    def share(self):
        (kind, b), lay = self.stages.pop(0), self.lay
        dz, dt = ((1 << b), 0) if kind == "z" else (0, (1 << b))
        self.bufs[1], self.bufs[3] = self.got, swap(self.got, lay.core, lay.size)
        more = [(z ^ dz, t ^ dt) for z, t in self.offs]
        self.pieces = [
            (2 * c + k, i, z, t, c)
            for c in range(2)
            for k, offs in enumerate((self.offs, more))
            for i, (z, t) in enumerate(offs)
        ]


class Shards:
    def __init__(self, lay, piece):
        self.bufs = [lax.all_gather(piece, AXES)]


def gate(run, *lists):
    flat = [x for some in lists for x in some]
    _, flat = run("gate", 0, lambda *refs: None, (1,), [], [], (), flat)
    flat = list(flat)
    return [[flat.pop(0) for _ in some] for some in lists]


def start_pieces(lay, group, bufs, me_ref, spans, sem, keep=None):
    me = (me_ref[0], me_ref[1], me_ref[2])
    if isinstance(group, Shards):
        pieces = []
        for to in range(lay.nt):
            t = to ^ me[2]
            if keep is None or keep(to):
                pieces += [(0, dp * lay.nt + t, dp * lay.rows, to, t) for dp in range(lay.ndp)]
    else:
        pieces = []
        for b, i, z, t, c in group.pieces:
            if keep is None or keep(t):
                row = pl.multiple_of(((z ^ me[0]) * 2 + (c ^ me[1])) * lay.rows, lay.rows)
                pieces.append((b, i, row, t, t ^ me[2]))
    for b, i, row, to, t in pieces:
        for first, width, place in spans:
            ref, at = place(to, t)
            if not isinstance(at, int):
                at = pl.multiple_of(at, 128)
            pltpu.make_async_copy(
                bufs[b].at[i, pl.ds(0, lay.rows), pl.ds(first, width)],
                ref.at[pl.ds(row, lay.rows), pl.ds(at, width)],
                sem(to),
            ).start()


def wait_all(ref, sem):
    pltpu.make_async_copy(ref, ref, sem).wait()


def flip(x):
    pad = jnp.zeros((LP - x.shape[0], x.shape[1]), x.dtype)
    return jnp.concatenate([x, pad], axis=0).T


def key_rows():
    row = lax.broadcasted_iota(jnp.int32, (16, LP), 0)
    lane = lax.broadcasted_iota(jnp.int32, (16, LP), 1)
    return jnp.where(row < 3, 1.0, jnp.where((row == 3) & (lane >= SEQ), NEG, 0.0)).astype(BF)


def split_rows(v):
    row = lax.broadcasted_iota(jnp.int32, (16, LP), 0)
    hi = v.astype(BF).astype(F32)
    mid = (v - hi).astype(BF).astype(F32)
    lo = v - hi - mid
    rest = jnp.where(row == 2, lo, jnp.where(row == 3, 1.0, 0.0))
    return jnp.where(row == 0, hi, jnp.where(row == 1, mid, rest)).astype(BF)


def split_query(q):
    v = q.astype(F32) * LOG2E
    hi = v.astype(BF)
    return hi, (v - hi.astype(F32)).astype(BF)


def attend_kernel(hl, p_ref, o_ref, lse_ref, top_ref):
    cw = hl * HEAD_DIM
    xt = flip(p_ref[...])
    aux = key_rows()
    none = split_rows(jnp.zeros((1, LP), F32))
    first = lax.broadcasted_iota(jnp.int32, (16, LP), 0) == 0
    ones = jnp.where(first, 1.0, 0.0).astype(BF)
    valid = lax.broadcasted_iota(jnp.int32, (1, LP), 1) < SEQ
    outs = []
    for h in range(hl):
        q = xt[h * HEAD_DIM : (h + 1) * HEAD_DIM]
        k = xt[cw + h * HEAD_DIM : cw + (h + 1) * HEAD_DIM]
        v = xt[2 * cw + h * HEAD_DIM : 2 * cw + (h + 1) * HEAD_DIM]
        hi, lo = split_query(q)
        s = dotf(jnp.concatenate([k, k, aux], 0), jnp.concatenate([hi, lo, none], 0), 0, 0)
        m = jnp.max(s, axis=0, keepdims=True)
        p = jnp.exp2(s - m).astype(BF)
        o = dotf(jnp.concatenate([v, ones], 0), p, 1, 0)
        total = o[HEAD_DIM : HEAD_DIM + 1]
        outs.append((o[:HEAD_DIM] / total).astype(BF))
        lse_ref[0, 0, h : h + 1, :] = m + jnp.log2(total)
        top_ref[0, 0, h : h + 1, :] = jnp.where(valid, m, NEG)
    o_ref[...] = jnp.concatenate(outs, 0).T[:SP]


def attend_back_kernel(hl, p_ref, o_ref, g_ref, lse_ref, d_ref, sum_ref):
    cw = hl * HEAD_DIM
    xt = flip(p_ref[...])
    ot = flip(o_ref[...])
    gt = flip(g_ref[...])
    aux = key_rows()
    ones = jnp.where(lax.broadcasted_iota(jnp.int32, (16, LP), 0) < 3, 1.0, 0.0).astype(BF)
    dq, dk, dv = [], [], []
    for h in range(hl):
        at = slice(h * HEAD_DIM, (h + 1) * HEAD_DIM)
        q = xt[at]
        k = xt[cw + h * HEAD_DIM : cw + (h + 1) * HEAD_DIM]
        v = xt[2 * cw + h * HEAD_DIM : 2 * cw + (h + 1) * HEAD_DIM]
        g = gt[at]
        hi, lo = split_query(q)
        delta = jnp.sum(ot[at].astype(F32) * g.astype(F32), axis=0, keepdims=True)
        minus = split_rows(-lse_ref[0, 0, h : h + 1, :])
        s = dotf(jnp.concatenate([k, k, aux], 0), jnp.concatenate([hi, lo, minus], 0), 0, 0)
        p = jnp.exp2(s)
        d = dotf(jnp.concatenate([v, ones], 0), jnp.concatenate([g, split_rows(-delta)], 0), 0, 0)
        ds = (p * d).astype(BF)
        dv.append(dotf(g, p.astype(BF), 1, 1).astype(BF))
        dq.append((HEAD_DIM**-0.5 * dotf(k, ds, 1, 0)).astype(BF))
        dk.append(dotf(q, ds, 1, 1).astype(BF))
    out = jnp.concatenate(dq + dk + dv, 0).T[:SP]
    d_ref[...] = out
    sum_ref[0, 0, :, :] = jnp.sum(out.astype(F32), axis=0, keepdims=True)


def unit_of(values):
    center = values - jnp.mean(values, axis=-1, keepdims=True)
    inverse = lax.rsqrt(jnp.mean(center * center, axis=-1, keepdims=True) + 1e-05)
    return center * inverse, inverse


def norm_back(grad, unit, inverse, gain):
    scaled = grad * gain
    inner = (
        scaled
        - jnp.mean(scaled, axis=-1, keepdims=True)
        - unit * jnp.mean(scaled * unit, axis=-1, keepdims=True)
    )
    return inner * inverse


def add_rows(ref, rows):
    step = pl.program_id(0)

    @pl.when(step == 0)
    def _():
        for r, row in enumerate(rows):
            ref[r : r + 1, :] = row

    @pl.when(step > 0)
    def _():
        for r, row in enumerate(rows):
            ref[r : r + 1, :] += row


def column_sum(x):
    return jnp.sum(x, axis=0, keepdims=True)


def row_block(width):
    return pl.BlockSpec((SP, width), lambda i, m: (i, 0))


def one_row(width):
    return pl.BlockSpec((1, width), lambda i, m: (0, 0))


def put_pieces(lay, me_ref, y, other, own, first=0):
    dr, width = lay.rows, y.shape[1]
    cs = pl.ds(first, width)
    y = y.astype(BF)
    for c in range(2):

        @pl.when(me_ref[1] == c)
        def _(c=c):
            for z in range(lay.nz):
                at = z ^ me_ref[0]
                a, b = (2 * z + c) * dr, (2 * z + 1 - c) * dr
                own[0, at, :, cs] = y[a : a + dr]
                other[0, at, :, cs] = y[b : b + dr]


def piece_out(lay, width):
    return (
        jax.ShapeDtypeStruct((lay.nt, lay.nz, lay.rows, width), BF),
        pl.BlockSpec((1, lay.nz, lay.rows, width), lambda o, *rest: (o, 0, 0, 0)),
    )


def start_joint(lay, joint, bufs, me_ref, place, sem, keep=None):
    for h, chain in enumerate(joint):
        width = chain.held.shape[-1]
        at = 0 if h == 0 else 3 * lay.cw - width
        spans = [(0, width, lambda to, t: (place(to), at))]
        start_pieces(lay, chain, bufs[4 * h : 4 * h + 4], me_ref, spans, sem, keep)


def prepare(run, tokens, cotangent, gain, shift):
    own = tokens.shape[0] // SEQ

    def kernel(me_ref, x_ref, c_ref, g_ref, s_ref, in_ref, n_ref, d_ref):
        none = jnp.zeros((SP - SEQ, D), F32)
        for i in range(own):
            rows, to = slice(i * SEQ, (i + 1) * SEQ), slice(i * SP, (i + 1) * SP)
            x = jnp.concatenate([x_ref[...].astype(F32)[rows], none])
            in_ref[to, :] = x.astype(BF)
            unit, _ = unit_of(x)
            n_ref[to, :] = (unit * g_ref[...] + s_ref[...]).astype(BF)
            c = jnp.concatenate([c_ref[...].astype(F32)[rows], none])
            live = me_ref[2] * own + i < me_ref[3]
            d_ref[to, :] = jnp.where(live, c, 0.0).astype(BF)

    shape = (jax.ShapeDtypeStruct((own * SP, D), BF), whole((own * SP, D)))
    out, _ = run(
        "prepare", 20, kernel, (1,),
        [(v, whole(v.shape)) for v in (tokens, cotangent, gain, shift)],
        [shape] * 3,
    )
    return out


def attend_all(lay, run, joint, normed, bias_rows):
    rows = normed.shape[0]
    own, cw = rows // SP, lay.cw
    hl = cw // HEAD_DIM
    wide = 3 * cw

    def kernel(me_ref, *refs):
        bufs = refs[:8]
        x_ref, b_ref, p_ref, o_ref, lse_ref, top_ref, w, sem = refs[8:]
        o, i = pl.program_id(0), pl.program_id(1)

        for k in range(1, lay.nt):

            @pl.when((o == k - 1) & (i == 0))
            def _(k=k):
                keep = lambda to: to == k or (k == 1 and to == 0)
                start_joint(lay, joint, bufs, me_ref, lambda to: w.at[to], lambda to: sem.at[to], keep)

        @pl.when(i == 0)
        def _():
            wait_all(w.at[o], sem.at[o])

        y = jnp.dot(x_ref[...], w[o], preferred_element_type=F32) + b_ref[...]
        p_ref[:, :cw] = (y[:, :cw] * HEAD_DIM**-0.5).astype(BF)
        p_ref[:, cw:] = y[:, cw:].astype(BF)
        attend_kernel(hl, p_ref, o_ref, lse_ref, top_ref)

    stat = pl.BlockSpec((1, 1, hl, LP), lambda o, i, m: (i, o ^ m[2], 0, 0))
    stat_shape = jax.ShapeDtypeStruct((own, lay.nt, hl, LP), F32)
    out, _ = run(
        "attend", 36, kernel, (lay.nt, own),
        [(b, ANY) for chain in joint for b in chain.bufs]
        + [
            (normed, pl.BlockSpec((SP, D), lambda o, i, m: (i, 0))),
            (bias_rows, pl.BlockSpec((1, wide), lambda o, i, m: (0, o ^ m[2]))),
        ],
        [
            (jax.ShapeDtypeStruct((rows, lay.nt * wide), BF), pl.BlockSpec((SP, wide), lambda o, i, m: (i, o ^ m[2]))),
            (jax.ShapeDtypeStruct((rows, D), BF), pl.BlockSpec((SP, cw), lambda o, i, m: (i, o ^ m[2]))),
            (stat_shape, stat),
            (stat_shape, stat),
        ],
        [pltpu.VMEM((lay.nt, D, wide), BF), pltpu.SemaphoreType.DMA((lay.nt,))],
    )
    return out


def out_project(lay, run, group, mixed, inputs, bias, gain, shift):
    rows = inputs.shape[0]
    cw = lay.cw
    nb = len(group.bufs)

    def kernel(me_ref, *refs):
        bufs = refs[:nb]
        m_ref, x_ref, b_ref, g_ref, s_ref, mid_ref, sec_ref, w, sem = refs[nb:]

        @pl.when(pl.program_id(0) == 0)
        def _():
            spans = [(0, cw, lambda to, t: (w, t * cw))]
            start_pieces(lay, group, bufs, me_ref, spans, lambda to: sem)
            wait_all(w, sem)

        middle = x_ref[...].astype(F32) + dotf(m_ref[...], w[...], 1, 1) + b_ref[...]
        mid_ref[...] = middle.astype(BF)
        unit, _ = unit_of(middle)
        sec_ref[...] = (unit * g_ref[...] + s_ref[...]).astype(BF)

    out, _ = run(
        "out_project", 9, kernel, (rows // SP,),
        [(b, ANY) for b in group.bufs]
        + [(mixed, row_block(D)), (inputs, row_block(D))]
        + [(v, one_row(D)) for v in (bias, gain, shift)],
        [
            (jax.ShapeDtypeStruct((rows, D), BF), row_block(D)),
            (jax.ShapeDtypeStruct((rows, D), BF), row_block(D)),
        ],
        [pltpu.VMEM((D, D), BF), pltpu.SemaphoreType.DMA],
    )
    return out


def feed(lay, run, expand, shrink, second, dresult, bias, dsecond=None):
    rows = second.shape[0]
    half = lay.cols // 2
    more = dsecond is not None
    (group_e, first_e), (group_s, first_s) = expand, shrink
    ne, ns = len(group_e.bufs), len(group_s.bufs)

    def kernel(me_ref, *refs):
        bufs_e, bufs_s = refs[:ne], refs[ne : ne + ns]
        x_ref, g_ref, b_ref, *refs = refs[ne + ns :]
        if more:
            before, *refs = refs
        a_ref, s_ref, sec_ref, other, mine, we, ws, d_s, acc, sem_e, sem_s, sem = refs
        o = pl.program_id(0)

        def fetch(k):
            keep = lambda to: to == k
            spans = [(first_e, half, lambda to, t: (we.at[to], 0))]
            start_pieces(lay, group_e, bufs_e, me_ref, spans, lambda to: sem_e.at[to], keep)
            spans = [(first_s, half, lambda to, t: (ws.at[to], 0))]
            start_pieces(lay, group_s, bufs_s, me_ref, spans, lambda to: sem_s.at[to], keep)

        for k in range(1, lay.nt):

            @pl.when(o == k - 1)
            def _(k=k):
                if k == 1:
                    fetch(0)
                fetch(k)

        @pl.when(o == 0)
        def _():
            if more:
                pltpu.make_async_copy(before, acc, sem).start()
                pltpu.make_async_copy(before, acc, sem).wait()
            else:
                acc[...] = jnp.zeros_like(acc)

        wait_all(we.at[o], sem_e.at[o])
        wait_all(ws.at[o], sem_s.at[o])
        total = None
        for r in range(rows // SP):
            rs = slice(r * SP, (r + 1) * SP)
            hidden = jnp.dot(x_ref[rs, :], we[o], preferred_element_type=F32) + b_ref[...]
            dact = jnp.dot(g_ref[rs, :], ws[o], preferred_element_type=F32)
            hidden = hidden.astype(BF)
            sigma = 0.5 + 0.5 * jnp.tanh(0.851 * hidden)
            active = hidden * sigma
            a_ref[rs, :] = active
            dh = dact.astype(BF) * (sigma + 1.702 * active * (1.0 - sigma))
            d_s[rs, :] = dh
            part = column_sum(dh.astype(F32))
            total = part if total is None else total + part
            acc[rs, :] += dotf(dh, we[o], 1, 1)
        s_ref[...] = total
        put_pieces(lay, me_ref, dotf(x_ref[...], d_s[...], 0, 0), other, mine)
        put_pieces(lay, me_ref, dotf(g_ref[...], a_ref[...], 0, 0), other, mine, half)

        @pl.when(o == lay.nt - 1)
        def _():
            sec_ref[...] = acc[...].astype(sec_ref.dtype)

    line = pl.BlockSpec((1, half), lambda o, m: (0, o ^ m[2]))
    full = pl.BlockSpec((rows, D), lambda o, m: (0, 0))
    weights = pltpu.VMEM((lay.nt, D, half), BF)
    sems = pltpu.SemaphoreType.DMA((lay.nt,))
    out, _ = run(
        "feed", 40, kernel, (lay.nt,),
        [(b, ANY) for b in (*group_e.bufs, *group_s.bufs)]
        + [(second, full), (dresult, full), (bias, line)] + ([(dsecond, ANY)] if more else []),
        [
            (jax.ShapeDtypeStruct((rows, lay.nt * half), BF), pl.BlockSpec((rows, half), lambda o, m: (0, o ^ m[2]))),
            (jax.ShapeDtypeStruct((1, lay.nt * half), F32), line),
            (jax.ShapeDtypeStruct((rows, D), BF if more else F32), full),
        ]
        + [piece_out(lay, 2 * half)] * 2,
        [
            weights,
            weights,
            pltpu.VMEM((rows, half), BF),
            pltpu.VMEM((rows, D), F32),
            sems,
            sems,
            pltpu.SemaphoreType.DMA,
        ],
    )
    return out


def feed_out(lay, run, shrink, active, base, bias=None, more=()):
    rows = base.shape[0]
    own = rows // SP
    half = lay.cols // 2
    wide = lay.nt * half
    group, first = shrink
    nb = len(group.bufs)

    def kernel(me_ref, *refs):
        bufs = refs[:nb]
        a_ref, base_ref, *refs = refs[nb:]
        o_ref, w, sem = refs[-3:]

        @pl.when(pl.program_id(0) == 0)
        def _():
            spans = [(first, half, lambda to, t: (w, t * half))]
            start_pieces(lay, group, bufs, me_ref, spans, lambda to: sem)
            wait_all(w, sem)

        out = base_ref[...].astype(F32) + dotf(a_ref[...], w[...], 1, 1)
        if bias is None:
            o_ref[...] = out
        else:
            live = me_ref[2] * own + pl.program_id(0) < me_ref[3]
            o_ref[...] = jnp.where(live, out + refs[0][...], 0.0).astype(BF)

    (result,), more = run(
        "feed_out", 12, kernel, (own,),
        [(b, ANY) for b in group.bufs]
        + [(active, row_block(wide)), (base, row_block(D))]
        + ([] if bias is None else [(bias, one_row(D))]),
        [(jax.ShapeDtypeStruct((rows, D), F32 if bias is None else BF), row_block(D))],
        [pltpu.VMEM((D, wide), BF), pltpu.SemaphoreType.DMA],
        more,
    )
    return result, more


def feed_back(lay, run, group, dsecond, middle, dresult, mixed, gain):
    rows = middle.shape[0]
    cw, nt = lay.cw, lay.nt
    steps = rows // SP

    nb = len(group.bufs)

    def kernel(me_ref, *refs):
        bufs = refs[:nb]
        d_ref, mid_ref, g_ref, m_ref, n_ref, dm_ref, dx_ref, v_ref, other, own, w, acc, sem = refs[nb:]
        i = pl.program_id(0)

        @pl.when(i == 0)
        def _():
            spans = [(0, cw, lambda to, t: (w, t * cw))]
            start_pieces(lay, group, bufs, me_ref, spans, lambda to: sem)
            wait_all(w, sem)

        dsecond = d_ref[...].astype(F32)
        unit, inverse = unit_of(mid_ref[...].astype(F32))
        dout = g_ref[...].astype(F32)
        dmiddle = dout + norm_back(dsecond, unit, inverse, n_ref[...])
        dbranch = dmiddle.astype(BF)
        dm_ref[...] = dbranch
        dx_ref[...] = jnp.dot(dbranch, w[...], preferred_element_type=F32).astype(BF)
        sums = [dsecond * unit, dsecond, dbranch.astype(F32), dout]
        add_rows(v_ref, [column_sum(v) for v in sums])
        y = dotf(dbranch, m_ref[...], 0, 0)

        @pl.when(i == 0)
        def _():
            acc[...] = y

        @pl.when(i > 0)
        def _():
            acc[...] += y

        @pl.when(i == steps - 1)
        def _():
            for t in range(nt):
                to = t ^ me_ref[2]
                put_pieces(
                    lay, me_ref, acc[:, t * cw : (t + 1) * cw], other.at[pl.ds(to, 1)], own.at[pl.ds(to, 1)]
                )

    piece = jax.ShapeDtypeStruct((nt, lay.nz, lay.rows, cw), BF)
    out, _ = run(
        "feed_back", 19, kernel, (steps,),
        [(b, ANY) for b in group.bufs]
        + [(v, row_block(D)) for v in (dsecond, middle, dresult, mixed)]
        + [(gain, one_row(D))],
        [
            (jax.ShapeDtypeStruct((rows, D), BF), row_block(D)),
            (jax.ShapeDtypeStruct((rows, D), BF), row_block(D)),
            (jax.ShapeDtypeStruct((4, D), F32), whole((4, D))),
            (piece, whole(piece.shape)),
            (piece, whole(piece.shape)),
        ],
        [pltpu.VMEM((D, D), BF), pltpu.VMEM((D, D), F32), pltpu.SemaphoreType.DMA],
    )
    return out


def attend_back(lay, run, to, joint, packed, mixed, dmixed, lse, normed, output, last=None, more=()):
    rows = packed.shape[0]
    own, cw = rows // SP, lay.cw
    hl = cw // HEAD_DIM
    w3 = 3 * cw
    np = 0 if last is None else len(last[0])

    def kernel(me_ref, *refs):
        bufs = refs[:8]
        p_ref, m_ref, g_ref, lse_ref, x_ref, go_other, go_own, *refs = refs[8:]
        if last is not None:
            parts = refs[:np]
            in_ref, dm_ref, gain_ref, *refs = refs[np:]
            sum_ref, out_ref, v_ref, other, mine, w, dp, total, sem = refs
        else:
            sum_ref, out_ref, other, mine, w, dp, total, sem = refs
        i = pl.program_id(0)

        @pl.when(i == 0)
        def _():
            start_joint(lay, joint, bufs, me_ref, lambda _: w, lambda _: sem, lambda t: t == to)

        attend_back_kernel(hl, p_ref, m_ref, g_ref, lse_ref, dp, sum_ref)

        @pl.when(i == 0)
        def _():
            wait_all(w, sem)

        dnormed = dotf(dp[...], w[...], 1, 1)
        y = dotf(x_ref[...], dp[...], 0, 0)
        if last is None:
            out_ref[...] = dnormed.astype(BF)
        else:
            for part in parts:
                dnormed += part[...].astype(F32)
            unit, inverse = unit_of(in_ref[...].astype(F32))
            dinput = norm_back(dnormed, unit, inverse, gain_ref[...])
            out_ref[...] = (dm_ref[...].astype(F32) + dinput).astype(BF)
            add_rows(v_ref, [column_sum(dnormed * unit), column_sum(dnormed)])

        @pl.when(i == 0)
        def _():
            total[...] = y

        @pl.when(i > 0)
        def _():
            total[...] += y

        @pl.when(i == own - 1)
        def _():
            put_pieces(lay, me_ref, total[...], other, mine)
            other[:, :, :, w3:] = go_other[...]
            mine[:, :, :, w3:] = go_own[...]

    spec = lambda width: pl.BlockSpec((SP, width), lambda i, m: (i, to ^ m[2]))
    part = pl.BlockSpec((1, lay.nz, lay.rows, cw), lambda i, m: (to, 0, 0, 0))
    piece = jax.ShapeDtypeStruct((1, lay.nz, lay.rows, w3 + cw), BF)
    return run(
        "attend_back", 20, kernel, (own,),
        [(b, ANY) for chain in joint for b in chain.bufs]
        + [
            (packed, spec(w3)),
            (mixed, spec(cw)),
            (dmixed, spec(cw)),
            (lse, pl.BlockSpec((1, 1, hl, LP), lambda i, m: (i, to ^ m[2], 0, 0))),
            (normed, row_block(D)),
            (output[0], part),
            (output[1], part),
        ]
        + ([(x, row_block(D)) for x in (*last[0], last[1], last[2])] + [(last[3], one_row(D))] if last else []),
        [
            (jax.ShapeDtypeStruct((own, 1, 1, w3), F32), pl.BlockSpec((1, 1, 1, w3), lambda i, m: (i, 0, 0, 0))),
            (jax.ShapeDtypeStruct((rows, D), BF), row_block(D)),
        ]
        + ([(jax.ShapeDtypeStruct((2, D), F32), whole((2, D)))] if last else [])
        + [(piece, whole(piece.shape))] * 2,
        [pltpu.VMEM((D, w3), BF), pltpu.VMEM((SP, w3), BF), pltpu.VMEM((D, w3), F32), pltpu.SemaphoreType.DMA],
        more,
    )


def insert_bit(s, b, value):
    return ((s >> b) << (b + 1)) | (value << b) | (s & ((1 << b) - 1))


def along(lay, run, arrays, more=()):
    z, dr, width = arrays[0].shape
    n = len(arrays)
    w = width // 2

    def kernel(me_ref, *refs):
        for k in range(z):
            total = refs[0][k].astype(F32)
            for ref in refs[1:n]:
                total += ref[k].astype(F32)
            refs[n + k][...] = total.astype(BF)

    block = pl.BlockSpec((z, dr, w), lambda s, m: (0, 0, s))
    out = (jax.ShapeDtypeStruct((dr, width), BF), pl.BlockSpec((dr, w), lambda s, m: (0, s)))
    sums, more = run("add_plane", 0, kernel, (width // w,), [(x, block) for x in arrays], [out] * z, (), more)
    return [swap(x, k * 2 * lay.nt, lay.size) if k else x for k, x in enumerate(sums)], more


def total_of(ends):
    total = ends[0].astype(F32)
    for x in ends[1:]:
        total = total + x.astype(F32)
    return total


class Butterfly:
    def __init__(self, lay, reverse, other, own):
        self.lay = lay
        bits = list(range(lay.tbits))
        self.bits = bits[::-1] if reverse else bits
        self.keep, self.got = [own], [swap(other, lay.core, lay.size)]
        self.left = list(range(lay.nt))

    def fold(self, run, more=()):
        bit = self.bits.pop(0)
        n = len(self.left)
        z, dr, width = self.keep[0].shape[-3:]
        one = len(self.keep) == 1
        block = pl.BlockSpec((n, 1, dr, width), lambda s, m: (0, s, 0, 0)) if one else None
        deep = 1 if one else z // 2
        piece = pl.BlockSpec((deep, dr, width), lambda s, m: (s, 0, 0))
        k = len(self.keep)

        def kernel(me_ref, *refs):
            for i in range(n):
                a, b = (refs[0][i], refs[1][i]) if one else (refs[i][...], refs[k + i][...])
                refs[2 * k + i][...] = a + b

        shape = jax.ShapeDtypeStruct((z, dr, width), BF)
        sums, more = run(
            "add", 0, kernel, (z // deep,), [(x, block or piece) for x in (*self.keep, *self.got)], [(shape, piece)] * n, (), more
        )
        self.keep = [x for t, x in zip(self.left, sums) if not t >> bit & 1]
        self.got = [swap(x, 1 << bit, self.lay.size) for t, x in zip(self.left, sums) if t >> bit & 1]
        self.left = [t for t in self.left if not t >> bit & 1]
        return more

    def along(self, run, more=()):
        self.ends, more = along(self.lay, run, self.keep + self.got, more)
        return more


class Direct:
    def __init__(self, lay):
        self.lay = lay
        self.parts, self.waiting = [], []

    def start(self, to, other, own):
        self.waiting.append((to, own[0], swap(other[0], self.lay.core, self.lay.size)))

    def spread(self, run, more=()):
        to, own, got = self.waiting.pop(0)
        z, dr, width = own.shape

        def kernel(me_ref, a_ref, b_ref, o_ref):
            o_ref[...] = a_ref[...] + b_ref[...]

        block = pl.BlockSpec((z, dr, width), lambda s, m: (0, 0, 0))
        shape = jax.ShapeDtypeStruct(own.shape, BF)
        (x,), more = run("add_core", 0, kernel, (1,), [(own, block), (got, block)], [(shape, block)], (), more)
        self.parts.append(swap(x, to, self.lay.size))
        return more

    def along(self, run, more=()):
        self.ends, more = along(self.lay, run, [*self.waiting[0][1:], *self.parts], more)
        return more


def unpad_rows(x):
    own = x.shape[0] // SP
    return x.reshape(own, SP, D)[:, :SEQ].reshape(own * SEQ, D)


def per_device(
    lay,
    tokens,
    first_gain,
    first_shift,
    joint_weight,
    joint_bias,
    output_weight,
    output_bias,
    second_gain,
    second_shift,
    expand_weight,
    expand_bias,
    shrink_weight,
    shrink_bias,
    cotangent,
    image_count,
    threshold,
):
    own = tokens.shape[0] // SEQ
    nt, cw, dr = lay.nt, lay.cw, lay.rows
    half = lay.cols // 2
    hl = cw // HEAD_DIM
    tensor = lax.axis_index("tensor").astype(jnp.int32)
    dp = lax.axis_index("dp").astype(jnp.int32)
    count = image_count[0]
    run = Runner(jnp.stack([dp // 2, dp % 2, tensor, count]))

    split = 3 * cw // 2 if cw % 256 == 0 else 2 * cw
    flat = joint_weight.reshape(dr, 3 * cw)
    joint = [Chain(lay, flat[:, :split], False), Chain(lay, flat[:, split:], True)]
    for chain in joint:
        chain.send()
    small = jnp.concatenate([joint_bias.reshape(-1), expand_bias.reshape(-1)])
    n_small = small.shape[0]
    output = jnp.concatenate([output_weight.T, jnp.pad(small[None], ((0, 15), (0, cw - n_small)))])
    (joint[0].got, joint[1].got), (output,) = gate(run, [chain.got for chain in joint], [output])
    output = Shards(lay, output)

    biases = output.bufs[0][:, dr].astype(F32)
    nb = joint_bias.size
    jb = biases[:, :nb].reshape(lay.ndp, nt, 2, hl, HEAD_DIM // lay.ndp)
    jb = jb.transpose(2, 1, 3, 0, 4).reshape(2, nt, 1, cw)
    bias_rows = jnp.concatenate([jb[0], jnp.zeros_like(jb[0]), jb[1]], axis=1).reshape(1, 3 * D)
    eb = biases[:, nb:n_small].reshape(lay.ndp, nt, FF // HEAD_DIM // nt, HEAD_DIM // lay.ndp)
    eb = eb.transpose(1, 2, 0, 3).reshape(nt, 2, half)
    expand_rows = [eb[:, g].reshape(1, nt * half) for g in range(2)]

    image_ids = tensor * own + jnp.arange(own, dtype=jnp.int32)
    image_live = image_ids < count
    row = lambda v: v.reshape(1, D)

    def land(chains):
        for chain in chains:
            chain.land()
            chain.send_last() if len(chain.stages) == 1 else chain.send()

    land(joint)
    shrink_t = (shrink_weight + run.token[0, 0].astype(BF)).T
    feeds = [Chain(lay, expand_weight[:, :half], False), Chain(lay, shrink_t[:, :half], True)]
    rest = jnp.concatenate([expand_weight[:, half:], shrink_t[:, half:]], axis=1)
    for chain in feeds:
        chain.send()
    while len(joint[0].stages) > 2:
        land(joint)
        if len(feeds[0].stages) > 3:
            land(feeds)
    (joint[0].got, joint[1].got), (feeds[0].got, feeds[1].got) = gate(
        run, [chain.got for chain in joint], [chain.got for chain in feeds]
    )
    land(joint)
    while len(feeds[0].stages) > 2:
        land(feeds)
    inputs, normed, dresult = prepare(run, tokens, cotangent, row(first_gain), row(first_shift))
    (joint[0].got, joint[1].got), (feeds[0].got, feeds[1].got), (rest,) = gate(
        run, [chain.got for chain in joint], [chain.got for chain in feeds], [rest]
    )
    for chain in joint:
        chain.share()
    rest = Shards(lay, rest)
    land(feeds)
    packed, mixed, lse, tops = attend_all(lay, run, joint, normed, bias_rows)
    (feeds[0].got, feeds[1].got), = gate(run, [chain.got for chain in feeds])
    for chain in feeds:
        chain.share()
    shrinks = [(feeds[1], 0), (rest, half)]
    middle, second = out_project(
        lay, run, output, mixed, inputs, row(output_bias), row(second_gain), row(second_shift)
    )

    active0, expand_sum0, dsecond, *pieces = feed(
        lay, run, (feeds[0], 0), shrinks[0], second, dresult, expand_rows[0]
    )
    grads = [Butterfly(lay, True, *pieces)]
    active1, expand_sum1, dsecond, *pieces = feed(
        lay, run, (rest, 0), shrinks[1], second, dresult, expand_rows[1], dsecond
    )
    grads.append(Butterfly(lay, False, *pieces))
    for sc in grads:
        sc.fold(run)
    dmiddle, dmixed, sums_two, *out_pieces = feed_back(
        lay, run, output, dsecond, middle, dresult, mixed, row(second_gain)
    )

    packed_sums, dnormed = [], []
    total = Direct(lay)

    def back(to, last=None, more=()):
        (part, out, *rest), more = attend_back(
            lay, run, to, joint, packed, mixed, dmixed, lse, normed, out_pieces, last, more
        )
        packed_sums.append(part)
        total.start(to, *rest[-2:])
        return out, rest[0], list(more)

    def spread(more=()):
        return list(total.spread(run, more))

    for n, to in enumerate(range(nt - 1, 0, -1)):
        if n == 0:
            out, _, more = back(to, None, [grads[0].got[0], grads[1].got[0]])
            grads[0].got[0], grads[1].got[0] = more
        else:
            out = back(to)[0]
        dnormed.append(out)
        if grads[0].bits:
            for sc in grads:
                sc.fold(run)
            if n:
                spread()
        elif not hasattr(grads[0], "ends"):
            for sc in grads:
                sc.along(run)
            spread()
        else:
            at = len(total.parts) - 1
            total.parts[at], *grads[0].ends[1:] = spread([total.parts[at], *grads[0].ends[1:]])
    token_rows, sums_one, _ = back(0, (dnormed, inputs, dmiddle, row(first_gain)))

    tops = jnp.max(tops, axis=-1).reshape(own, HEADS) / LOG2E
    peak = jnp.max(jnp.where(image_live[:, None], tops, NEG), axis=0)
    peak = jnp.broadcast_to(peak[:, None], (HEADS, 128))
    expand_sum = jnp.stack([expand_sum0.reshape(nt, half), expand_sum1.reshape(nt, half)], axis=1)
    heads = jnp.concatenate([jnp.sum(x, axis=0) for x in packed_sums[::-1]]).reshape(nt, 3, cw)
    heads = heads[jnp.arange(nt) ^ tensor]
    vectors = [sums_two, expand_sum, sums_one, heads[:, 0], heads[:, 2]]
    sums = jnp.concatenate([peak] + [v.reshape(-1, 128) for v in vectors])
    ((sums,),) = gate(run, [sums])
    sums = lax.all_gather(sums, AXES)
    grads[1].ends[1:] = spread(grads[1].ends[1:])
    result, _ = feed_out(lay, run, shrinks[0], active0, middle)
    total.along(run)
    ends = [x for sc in grads for x in sc.ends]
    result, (token_rows, *ends) = feed_out(
        lay, run, shrinks[1], active1, result, row(shrink_bias), [token_rows, *ends]
    )
    for n, sc in enumerate(grads):
        sc.ends = ends[n * lay.nz : (n + 1) * lay.nz]

    block_out = unpad_rows(result)
    tokens_grad = unpad_rows(token_rows)
    peak = jnp.max(sums[:, :HEADS, 0], axis=0)
    sums = jnp.sum(sums, axis=0)
    at = [HEADS, HEADS + 4 * D // 128, HEADS + (4 * D + FF) // 128, HEADS + (6 * D + FF) // 128]
    sums_two = sums[at[0] : at[1]].reshape(4, D)
    expand_sum = sums[at[1] : at[2]].reshape(FF)
    sums_one = sums[at[2] : at[3]].reshape(2, D)
    bias_sum = sums[at[3] :].reshape(2, D)
    mine = lambda v: lax.dynamic_slice_in_dim(v, dp * dr, dr, v.ndim - 1)
    sums_one, sums_two = mine(sums_one), mine(sums_two)
    share = HEAD_DIM // lay.ndp
    units = FF // HEAD_DIM // nt
    expand_bias_grad = lax.dynamic_slice(
        expand_sum.reshape(FF // HEAD_DIM, HEAD_DIM), (tensor * units, dp * share), (units, share)
    )
    joint_bias_grad = lax.dynamic_slice(
        bias_sum.reshape(2, HEADS, HEAD_DIM), (0, tensor * hl, dp * share), (2, hl, share)
    )

    top = lax.dynamic_slice_in_dim(peak, tensor * hl, hl, 0)
    factors = jnp.sqrt(threshold / jnp.maximum(top, threshold))
    columns = jnp.repeat(factors, HEAD_DIM)
    clipped_joint = (joint_weight[:, 0:2, :].astype(F32) * columns).astype(BF)
    clipped_bias = (joint_bias[0].astype(F32) * factors[:, None]).astype(BF)

    feed_a, feed_b, total = [total_of(g.ends) for g in (*grads, total)]
    joint_grad = total[:, : 3 * cw].reshape(dr, 3, cw)
    output_grad = total[:, 3 * cw :].T
    expand_grad = jnp.concatenate([feed_a[:, :half], feed_b[:, :half]], axis=1)
    shrink_grad = jnp.concatenate([feed_a[:, half:], feed_b[:, half:]], axis=1).T
    return (
        block_out,
        tokens_grad,
        sums_one[0],
        sums_one[1],
        joint_grad,
        joint_bias_grad,
        output_grad,
        sums_two[2],
        sums_two[0],
        sums_two[1],
        expand_grad,
        expand_bias_grad,
        shrink_grad,
        sums_two[3],
        clipped_joint,
        clipped_bias,
        factors,
    )


def solution(mesh):
    placed = (
        P(("dp", "tensor"), None),
        P(),
        P(),
        P("dp", None, "tensor"),
        P(None, "tensor", "dp"),
        P("tensor", "dp"),
        P(),
        P(),
        P(),
        P("dp", "tensor"),
        P("tensor", "dp"),
        P("tensor", "dp"),
        P(),
        P(("dp", "tensor"), None),
        P("dp"),
        P("tensor"),
    )
    lay = Layout(mesh.shape["dp"], mesh.shape["tensor"])
    return jax.shard_map(
        partial(per_device, lay),
        mesh=mesh,
        in_specs=placed,
        out_specs=(
            P(("dp", "tensor"), None),
            P(("dp", "tensor"), None),
            P("dp"),
            P("dp"),
            P("dp", None, "tensor"),
            P(None, "tensor", "dp"),
            P("tensor", "dp"),
            P("dp"),
            P("dp"),
            P("dp"),
            P("dp", "tensor"),
            P("tensor", "dp"),
            P("tensor", "dp"),
            P("dp"),
            P("dp", None, "tensor"),
            P("tensor", "dp"),
            P("tensor"),
        ),
        check_vma=False,
    )
```

```python
from functools import partial

import jax
import jax.numpy as jnp
from jax import lax
from jax.experimental import pallas as pl
from jax.experimental.pallas import tpu as pltpu
from jax.sharding import PartitionSpec as P

D = 1024
FF = 4096
HEADS = 16
HEAD_DIM = 64
SEQ = 577
SP = 592
LP = 640
LOG2E = 1.4426950408889634
NEG = -1e30
BF = jnp.bfloat16
F32 = jnp.float32
AXES = ("dp", "tensor")
VMEM_LIMIT = 64 * 2**20 - 2**18


def dotf(a, b, ca, cb):
    return lax.dot_general(a, b, (((ca,), (cb,)), ((), ())), preferred_element_type=F32)


def whole(shape):
    zeros = (0,) * len(shape)
    return pl.BlockSpec(shape, lambda *_: zeros)


ANY = pl.BlockSpec(memory_space=pl.ANY)


class Runner:
    def __init__(self, me):
        self.me = me
        self.token = jnp.zeros((8, 128), F32)

    def __call__(self, name, us, kernel, grid, ins, outs, scratch=(), through=()):
        n_in, n_out = len(ins), len(outs)
        through = [self.token] + list(through)
        n = len(through)

        def body(me_ref, *refs):
            first = refs[:n_in]
            second = refs[n_in + n : n_in + n + n_out]
            kernel(me_ref, *first, *second, *refs[n_in + 2 * n + n_out :])

        got = pl.pallas_call(
            body,
            grid_spec=pltpu.PrefetchScalarGridSpec(
                num_scalar_prefetch=1,
                grid=grid,
                in_specs=[spec for _, spec in ins] + [ANY] * n,
                out_specs=[spec for _, spec in outs] + [ANY] * n,
                scratch_shapes=list(scratch),
            ),
            out_shape=[shape for shape, _ in outs] + [jax.ShapeDtypeStruct(a.shape, a.dtype) for a in through],
            input_output_aliases={1 + n_in + i: n_out + i for i in range(n)},
            compiler_params=pltpu.CompilerParams(vmem_limit_bytes=VMEM_LIMIT),
            cost_estimate=pl.CostEstimate(flops=int(us * 1.1e9), bytes_accessed=int(us * 1e6), transcendentals=0),
            name=name,
        )(self.me, *[a for a, _ in ins], *through)
        self.token = got[n_out]
        return got[:n_out], got[n_out + 1 :]


class Layout:
    def __init__(self, ndp, nt):
        self.ndp, self.nt, self.nz = ndp, nt, ndp // 2
        self.size = ndp * nt
        self.rows = D // ndp
        self.cols = FF // nt
        self.tbits = nt.bit_length() - 1
        self.zbits = self.nz.bit_length() - 1
        self.core = nt
        self.cw = D // nt


def stage_mask(lay, bit):
    kind, b = bit
    return (1 << b) if kind == "t" else (lay.nt * 2) << b


def swap(x, mask, size):
    return lax.ppermute(x, AXES, [(i, i ^ mask) for i in range(size)])


class Chain:
    def __init__(self, lay, piece, reverse):
        self.lay = lay
        z = [("z", b) for b in reversed(range(lay.zbits))]
        t = [("t", b) for b in range(lay.tbits)]
        t = t[::-1] if reverse else t
        self.stages = []
        while z or t:
            self.stages.append(z.pop(0) if z and len(z) >= len(t) else t.pop(0))
        self.held, self.offs = piece[None], [(0, 0)]

    def send(self):
        self.got = swap(self.held, stage_mask(self.lay, self.stages[0]), self.lay.size)

    def land(self):
        kind, b = self.stages.pop(0)
        dz, dt = ((1 << b), 0) if kind == "z" else (0, (1 << b))
        self.offs = self.offs + [(z ^ dz, t ^ dt) for z, t in self.offs]
        self.held = jnp.concatenate([self.held, self.got])

    def send_last(self):
        self.send()
        self.bufs = [self.held, None, swap(self.held, self.lay.core, self.lay.size), None]

    def share(self):
        (kind, b), lay = self.stages.pop(0), self.lay
        dz, dt = ((1 << b), 0) if kind == "z" else (0, (1 << b))
        self.bufs[1], self.bufs[3] = self.got, swap(self.got, lay.core, lay.size)
        more = [(z ^ dz, t ^ dt) for z, t in self.offs]
        self.pieces = [
            (2 * c + k, i, z, t, c)
            for c in range(2)
            for k, offs in enumerate((self.offs, more))
            for i, (z, t) in enumerate(offs)
        ]


class Shards:
    def __init__(self, lay, piece):
        self.bufs = [lax.all_gather(piece, AXES)]


def gate(run, *lists):
    flat = [x for some in lists for x in some]
    _, flat = run("gate", 0, lambda *refs: None, (1,), [], [], (), flat)
    flat = list(flat)
    return [[flat.pop(0) for _ in some] for some in lists]


def start_pieces(lay, group, bufs, me_ref, spans, sem, keep=None):
    me = (me_ref[0], me_ref[1], me_ref[2])
    if isinstance(group, Shards):
        pieces = []
        for to in range(lay.nt):
            t = to ^ me[2]
            if keep is None or keep(to):
                pieces += [(0, dp * lay.nt + t, dp * lay.rows, to, t) for dp in range(lay.ndp)]
    else:
        pieces = []
        for b, i, z, t, c in group.pieces:
            if keep is None or keep(t):
                row = pl.multiple_of(((z ^ me[0]) * 2 + (c ^ me[1])) * lay.rows, lay.rows)
                pieces.append((b, i, row, t, t ^ me[2]))
    for b, i, row, to, t in pieces:
        for first, width, place in spans:
            ref, at = place(to, t)
            if not isinstance(at, int):
                at = pl.multiple_of(at, 128)
            pltpu.make_async_copy(
                bufs[b].at[i, pl.ds(0, lay.rows), pl.ds(first, width)],
                ref.at[pl.ds(row, lay.rows), pl.ds(at, width)],
                sem(to),
            ).start()


def wait_all(ref, sem):
    pltpu.make_async_copy(ref, ref, sem).wait()


def flip(x):
    pad = jnp.zeros((LP - x.shape[0], x.shape[1]), x.dtype)
    return jnp.concatenate([x, pad], axis=0).T


def key_rows():
    row = lax.broadcasted_iota(jnp.int32, (16, LP), 0)
    lane = lax.broadcasted_iota(jnp.int32, (16, LP), 1)
    return jnp.where(row < 3, 1.0, jnp.where((row == 3) & (lane >= SEQ), NEG, 0.0)).astype(BF)


def split_rows(v):
    row = lax.broadcasted_iota(jnp.int32, (16, LP), 0)
    hi = v.astype(BF).astype(F32)
    mid = (v - hi).astype(BF).astype(F32)
    lo = v - hi - mid
    rest = jnp.where(row == 2, lo, jnp.where(row == 3, 1.0, 0.0))
    return jnp.where(row == 0, hi, jnp.where(row == 1, mid, rest)).astype(BF)


def split_query(q):
    v = q.astype(F32) * LOG2E
    hi = v.astype(BF)
    return hi, (v - hi.astype(F32)).astype(BF)


def attend_kernel(hl, p_ref, o_ref, lse_ref, top_ref):
    cw = hl * HEAD_DIM
    xt = flip(p_ref[...])
    aux = key_rows()
    none = split_rows(jnp.zeros((1, LP), F32))
    first = lax.broadcasted_iota(jnp.int32, (16, LP), 0) == 0
    ones = jnp.where(first, 1.0, 0.0).astype(BF)
    valid = lax.broadcasted_iota(jnp.int32, (1, LP), 1) < SEQ
    outs = []
    for h in range(hl):
        q = xt[h * HEAD_DIM : (h + 1) * HEAD_DIM]
        k = xt[cw + h * HEAD_DIM : cw + (h + 1) * HEAD_DIM]
        v = xt[2 * cw + h * HEAD_DIM : 2 * cw + (h + 1) * HEAD_DIM]
        hi, lo = split_query(q)
        s = dotf(jnp.concatenate([k, k, aux], 0)[:, :SP], jnp.concatenate([hi, lo, none], 0), 0, 0)
        m = jnp.max(s, axis=0, keepdims=True)
        p = jnp.exp2(s - m).astype(BF)
        o = dotf(jnp.concatenate([v, ones], 0)[:, :SP], p, 1, 0)
        total = o[HEAD_DIM : HEAD_DIM + 1]
        outs.append((o[:HEAD_DIM] / total).astype(BF))
        lse_ref[0, 0, h : h + 1, :] = m + jnp.log2(total)
        top_ref[0, 0, h : h + 1, :] = jnp.where(valid, m, NEG)
    o_ref[...] = jnp.concatenate(outs, 0).T[:SP]


def attend_back_kernel(hl, p_ref, o_ref, g_ref, lse_ref, d_ref, sum_ref):
    cw = hl * HEAD_DIM
    xt = flip(p_ref[...])
    ot = flip(o_ref[...])
    gt = flip(g_ref[...])
    aux = key_rows()
    ones = jnp.where(lax.broadcasted_iota(jnp.int32, (16, LP), 0) < 3, 1.0, 0.0).astype(BF)
    dq, dk, dv = [], [], []
    for h in range(hl):
        at = slice(h * HEAD_DIM, (h + 1) * HEAD_DIM)
        q = xt[at]
        k = xt[cw + h * HEAD_DIM : cw + (h + 1) * HEAD_DIM]
        v = xt[2 * cw + h * HEAD_DIM : 2 * cw + (h + 1) * HEAD_DIM]
        g = gt[at]
        hi, lo = split_query(q)
        delta = jnp.sum(ot[at].astype(F32) * g.astype(F32), axis=0, keepdims=True)
        minus = split_rows(-lse_ref[0, 0, h : h + 1, :])
        s = dotf(jnp.concatenate([k, k, aux], 0)[:, :SP], jnp.concatenate([hi, lo, minus], 0), 0, 0)
        p = jnp.exp2(s)
        d = dotf(jnp.concatenate([v, ones], 0)[:, :SP], jnp.concatenate([g, split_rows(-delta)], 0), 0, 0)
        ds = (p * d).astype(BF)
        dv.append(dotf(g, p.astype(BF), 1, 1).astype(BF))
        dq.append((HEAD_DIM**-0.5 * dotf(k[:, :SP], ds, 1, 0)).astype(BF))
        dk.append(dotf(q, ds, 1, 1).astype(BF))
    out = jnp.concatenate([jnp.concatenate(dq, 0).T[:SP], jnp.concatenate(dk + dv, 0).T], 1)
    d_ref[...] = out
    sum_ref[0, 0, :, :] = jnp.sum(out.astype(F32), axis=0, keepdims=True)


def unit_of(values):
    center = values - jnp.mean(values, axis=-1, keepdims=True)
    inverse = lax.rsqrt(jnp.mean(center * center, axis=-1, keepdims=True) + 1e-05)
    return center * inverse, inverse


def norm_back(grad, unit, inverse, gain):
    scaled = grad * gain
    inner = (
        scaled
        - jnp.mean(scaled, axis=-1, keepdims=True)
        - unit * jnp.mean(scaled * unit, axis=-1, keepdims=True)
    )
    return inner * inverse


def add_rows(ref, rows):
    step = pl.program_id(0)

    @pl.when(step == 0)
    def _():
        for r, row in enumerate(rows):
            ref[r : r + 1, :] = row

    @pl.when(step > 0)
    def _():
        for r, row in enumerate(rows):
            ref[r : r + 1, :] += row


def column_sum(x):
    return jnp.sum(x, axis=0, keepdims=True)


def row_block(width):
    return pl.BlockSpec((SP, width), lambda i, m: (i, 0))


def one_row(width):
    return pl.BlockSpec((1, width), lambda i, m: (0, 0))


def put_pieces(lay, me_ref, y, other, own, first=0):
    dr, width = lay.rows, y.shape[1]
    cs = pl.ds(first, width)
    y = y.astype(BF)
    for c in range(2):

        @pl.when(me_ref[1] == c)
        def _(c=c):
            for z in range(lay.nz):
                at = z ^ me_ref[0]
                a, b = (2 * z + c) * dr, (2 * z + 1 - c) * dr
                own[0, at, :, cs] = y[a : a + dr]
                other[0, at, :, cs] = y[b : b + dr]


def piece_out(lay, width):
    return (
        jax.ShapeDtypeStruct((lay.nt, lay.nz, lay.rows, width), BF),
        pl.BlockSpec((1, lay.nz, lay.rows, width), lambda o, *rest: (o, 0, 0, 0)),
    )


def start_joint(lay, joint, bufs, me_ref, place, sem, keep=None):
    for h, chain in enumerate(joint):
        width = chain.held.shape[-1]
        at = 0 if h == 0 else 3 * lay.cw - width
        spans = [(0, width, lambda to, t: (place(to), at))]
        start_pieces(lay, chain, bufs[4 * h : 4 * h + 4], me_ref, spans, sem, keep)


def prepare(run, tokens, cotangent, gain, shift):
    own = tokens.shape[0] // SEQ

    def kernel(me_ref, x_ref, c_ref, g_ref, s_ref, in_ref, n_ref, d_ref):
        none = jnp.zeros((SP - SEQ, D), F32)
        for i in range(own):
            rows, to = slice(i * SEQ, (i + 1) * SEQ), slice(i * SP, (i + 1) * SP)
            x = jnp.concatenate([x_ref[...].astype(F32)[rows], none])
            in_ref[to, :] = x.astype(BF)
            unit, _ = unit_of(x)
            n_ref[to, :] = (unit * g_ref[...] + s_ref[...]).astype(BF)
            c = jnp.concatenate([c_ref[...].astype(F32)[rows], none])
            live = me_ref[2] * own + i < me_ref[3]
            d_ref[to, :] = jnp.where(live, c, 0.0).astype(BF)

    shape = (jax.ShapeDtypeStruct((own * SP, D), BF), whole((own * SP, D)))
    out, _ = run(
        "prepare", 20, kernel, (1,),
        [(v, whole(v.shape)) for v in (tokens, cotangent, gain, shift)],
        [shape] * 3,
    )
    return out


def attend_all(lay, run, joint, normed, bias_rows):
    rows = normed.shape[0]
    own, cw = rows // SP, lay.cw
    hl = cw // HEAD_DIM
    wide = 3 * cw

    def kernel(me_ref, *refs):
        bufs = refs[:8]
        x_ref, b_ref, p_ref, o_ref, lse_ref, top_ref, w, sem = refs[8:]
        o, i = pl.program_id(0), pl.program_id(1)

        for k in range(1, lay.nt):

            @pl.when((o == k - 1) & (i == 0))
            def _(k=k):
                keep = lambda to: to == k or (k == 1 and to == 0)
                start_joint(lay, joint, bufs, me_ref, lambda to: w.at[to], lambda to: sem.at[to], keep)

        @pl.when(i == 0)
        def _():
            wait_all(w.at[o], sem.at[o])

        y = jnp.dot(x_ref[...], w[o], preferred_element_type=F32) + b_ref[...]
        p_ref[:, :cw] = (y[:, :cw] * HEAD_DIM**-0.5).astype(BF)
        p_ref[:, cw:] = y[:, cw:].astype(BF)
        attend_kernel(hl, p_ref, o_ref, lse_ref, top_ref)

    stat = pl.BlockSpec((1, 1, hl, LP), lambda o, i, m: (i, o ^ m[2], 0, 0))
    stat_shape = jax.ShapeDtypeStruct((own, lay.nt, hl, LP), F32)
    out, _ = run(
        "attend", 36, kernel, (lay.nt, own),
        [(b, ANY) for chain in joint for b in chain.bufs]
        + [
            (normed, pl.BlockSpec((SP, D), lambda o, i, m: (i, 0))),
            (bias_rows, pl.BlockSpec((1, wide), lambda o, i, m: (0, o ^ m[2]))),
        ],
        [
            (jax.ShapeDtypeStruct((rows, lay.nt * wide), BF), pl.BlockSpec((SP, wide), lambda o, i, m: (i, o ^ m[2]))),
            (jax.ShapeDtypeStruct((rows, D), BF), pl.BlockSpec((SP, cw), lambda o, i, m: (i, o ^ m[2]))),
            (stat_shape, stat),
            (stat_shape, stat),
        ],
        [pltpu.VMEM((lay.nt, D, wide), BF), pltpu.SemaphoreType.DMA((lay.nt,))],
    )
    return out


def out_project(lay, run, group, mixed, inputs, bias, gain, shift):
    rows = inputs.shape[0]
    cw = lay.cw
    nb = len(group.bufs)

    def kernel(me_ref, *refs):
        bufs = refs[:nb]
        m_ref, x_ref, b_ref, g_ref, s_ref, mid_ref, sec_ref, w, sem = refs[nb:]

        @pl.when(pl.program_id(0) == 0)
        def _():
            spans = [(0, cw, lambda to, t: (w, t * cw))]
            start_pieces(lay, group, bufs, me_ref, spans, lambda to: sem)
            wait_all(w, sem)

        middle = x_ref[...].astype(F32) + dotf(m_ref[...], w[...], 1, 1) + b_ref[...]
        mid_ref[...] = middle.astype(BF)
        unit, _ = unit_of(middle)
        sec_ref[...] = (unit * g_ref[...] + s_ref[...]).astype(BF)

    out, _ = run(
        "out_project", 9, kernel, (rows // SP,),
        [(b, ANY) for b in group.bufs]
        + [(mixed, row_block(D)), (inputs, row_block(D))]
        + [(v, one_row(D)) for v in (bias, gain, shift)],
        [
            (jax.ShapeDtypeStruct((rows, D), BF), row_block(D)),
            (jax.ShapeDtypeStruct((rows, D), BF), row_block(D)),
        ],
        [pltpu.VMEM((D, D), BF), pltpu.SemaphoreType.DMA],
    )
    return out


def feed(lay, run, expand, shrink, second, dresult, bias, dsecond=None):
    rows = second.shape[0]
    half = lay.cols // 2
    more = dsecond is not None
    (group_e, first_e), (group_s, first_s) = expand, shrink
    ne, ns = len(group_e.bufs), len(group_s.bufs)

    def kernel(me_ref, *refs):
        bufs_e, bufs_s = refs[:ne], refs[ne : ne + ns]
        x_ref, g_ref, b_ref, *refs = refs[ne + ns :]
        if more:
            before, *refs = refs
        a_ref, s_ref, sec_ref, other, mine, we, ws, d_s, acc, sem_e, sem_s, sem = refs
        o = pl.program_id(0)

        def fetch(k):
            keep = lambda to: to == k
            spans = [(first_e, half, lambda to, t: (we.at[to], 0))]
            start_pieces(lay, group_e, bufs_e, me_ref, spans, lambda to: sem_e.at[to], keep)
            spans = [(first_s, half, lambda to, t: (ws.at[to], 0))]
            start_pieces(lay, group_s, bufs_s, me_ref, spans, lambda to: sem_s.at[to], keep)

        for k in range(1, lay.nt):

            @pl.when(o == k - 1)
            def _(k=k):
                if k == 1:
                    fetch(0)
                fetch(k)

        @pl.when(o == 0)
        def _():
            if more:
                pltpu.make_async_copy(before, acc, sem).start()
                pltpu.make_async_copy(before, acc, sem).wait()
            else:
                acc[...] = jnp.zeros_like(acc)

        wait_all(we.at[o], sem_e.at[o])
        wait_all(ws.at[o], sem_s.at[o])
        total = None
        for r in range(rows // SP):
            rs = slice(r * SP, (r + 1) * SP)
            hidden = jnp.dot(x_ref[rs, :], we[o], preferred_element_type=F32) + b_ref[...]
            dact = jnp.dot(g_ref[rs, :], ws[o], preferred_element_type=F32)
            hidden = hidden.astype(BF)
            sigma = 0.5 + 0.5 * jnp.tanh(0.851 * hidden)
            active = hidden * sigma
            a_ref[rs, :] = active
            dh = dact.astype(BF) * (sigma + 1.702 * active * (1.0 - sigma))
            d_s[rs, :] = dh
            part = column_sum(dh.astype(F32))
            total = part if total is None else total + part
            acc[rs, :] += dotf(dh, we[o], 1, 1)
        s_ref[...] = total
        put_pieces(lay, me_ref, dotf(x_ref[...], d_s[...], 0, 0), other, mine)
        put_pieces(lay, me_ref, dotf(g_ref[...], a_ref[...], 0, 0), other, mine, half)

        @pl.when(o == lay.nt - 1)
        def _():
            sec_ref[...] = acc[...].astype(sec_ref.dtype)

    line = pl.BlockSpec((1, half), lambda o, m: (0, o ^ m[2]))
    full = pl.BlockSpec((rows, D), lambda o, m: (0, 0))
    weights = pltpu.VMEM((lay.nt, D, half), BF)
    sems = pltpu.SemaphoreType.DMA((lay.nt,))
    out, _ = run(
        "feed", 40, kernel, (lay.nt,),
        [(b, ANY) for b in (*group_e.bufs, *group_s.bufs)]
        + [(second, full), (dresult, full), (bias, line)] + ([(dsecond, ANY)] if more else []),
        [
            (jax.ShapeDtypeStruct((rows, lay.nt * half), BF), pl.BlockSpec((rows, half), lambda o, m: (0, o ^ m[2]))),
            (jax.ShapeDtypeStruct((1, lay.nt * half), F32), line),
            (jax.ShapeDtypeStruct((rows, D), BF if more else F32), full),
        ]
        + [piece_out(lay, 2 * half)] * 2,
        [
            weights,
            weights,
            pltpu.VMEM((rows, half), BF),
            pltpu.VMEM((rows, D), F32),
            sems,
            sems,
            pltpu.SemaphoreType.DMA,
        ],
    )
    return out


def feed_out(lay, run, shrink, active, base, bias=None, more=()):
    rows = base.shape[0]
    own = rows // SP
    half = lay.cols // 2
    wide = lay.nt * half
    group, first = shrink
    nb = len(group.bufs)

    def kernel(me_ref, *refs):
        bufs = refs[:nb]
        a_ref, base_ref, *refs = refs[nb:]
        o_ref, w, sem = refs[-3:]

        @pl.when(pl.program_id(0) == 0)
        def _():
            spans = [(first, half, lambda to, t: (w, t * half))]
            start_pieces(lay, group, bufs, me_ref, spans, lambda to: sem)
            wait_all(w, sem)

        out = base_ref[...].astype(F32) + dotf(a_ref[...], w[...], 1, 1)
        if bias is None:
            o_ref[...] = out
        else:
            live = me_ref[2] * own + pl.program_id(0) < me_ref[3]
            o_ref[...] = jnp.where(live, out + refs[0][...], 0.0).astype(BF)

    (result,), more = run(
        "feed_out", 12, kernel, (own,),
        [(b, ANY) for b in group.bufs]
        + [(active, row_block(wide)), (base, row_block(D))]
        + ([] if bias is None else [(bias, one_row(D))]),
        [(jax.ShapeDtypeStruct((rows, D), F32 if bias is None else BF), row_block(D))],
        [pltpu.VMEM((D, wide), BF), pltpu.SemaphoreType.DMA],
        more,
    )
    return result, more


def feed_back(lay, run, group, dsecond, middle, dresult, mixed, gain):
    rows = middle.shape[0]
    cw, nt = lay.cw, lay.nt
    steps = rows // SP

    nb = len(group.bufs)

    def kernel(me_ref, *refs):
        bufs = refs[:nb]
        d_ref, mid_ref, g_ref, m_ref, n_ref, dm_ref, dx_ref, v_ref, other, own, w, acc, sem = refs[nb:]
        i = pl.program_id(0)

        @pl.when(i == 0)
        def _():
            spans = [(0, cw, lambda to, t: (w, t * cw))]
            start_pieces(lay, group, bufs, me_ref, spans, lambda to: sem)
            wait_all(w, sem)

        dsecond = d_ref[...].astype(F32)
        unit, inverse = unit_of(mid_ref[...].astype(F32))
        dout = g_ref[...].astype(F32)
        dmiddle = dout + norm_back(dsecond, unit, inverse, n_ref[...])
        dbranch = dmiddle.astype(BF)
        dm_ref[...] = dbranch
        dx_ref[...] = jnp.dot(dbranch, w[...], preferred_element_type=F32).astype(BF)
        sums = [dsecond * unit, dsecond, dbranch.astype(F32), dout]
        add_rows(v_ref, [column_sum(v) for v in sums])
        y = dotf(dbranch, m_ref[...], 0, 0)

        @pl.when(i == 0)
        def _():
            acc[...] = y

        @pl.when(i > 0)
        def _():
            acc[...] += y

        @pl.when(i == steps - 1)
        def _():
            for t in range(nt):
                to = t ^ me_ref[2]
                put_pieces(
                    lay, me_ref, acc[:, t * cw : (t + 1) * cw], other.at[pl.ds(to, 1)], own.at[pl.ds(to, 1)]
                )

    piece = jax.ShapeDtypeStruct((nt, lay.nz, lay.rows, cw), BF)
    out, _ = run(
        "feed_back", 19, kernel, (steps,),
        [(b, ANY) for b in group.bufs]
        + [(v, row_block(D)) for v in (dsecond, middle, dresult, mixed)]
        + [(gain, one_row(D))],
        [
            (jax.ShapeDtypeStruct((rows, D), BF), row_block(D)),
            (jax.ShapeDtypeStruct((rows, D), BF), row_block(D)),
            (jax.ShapeDtypeStruct((4, D), F32), whole((4, D))),
            (piece, whole(piece.shape)),
            (piece, whole(piece.shape)),
        ],
        [pltpu.VMEM((D, D), BF), pltpu.VMEM((D, D), F32), pltpu.SemaphoreType.DMA],
    )
    return out


def attend_back(lay, run, to, joint, packed, mixed, dmixed, lse, normed, output, last=None, more=()):
    rows = packed.shape[0]
    own, cw = rows // SP, lay.cw
    hl = cw // HEAD_DIM
    w3 = 3 * cw
    np = 0 if last is None else len(last[0])

    def kernel(me_ref, *refs):
        bufs = refs[:8]
        p_ref, m_ref, g_ref, lse_ref, x_ref, go_other, go_own, *refs = refs[8:]
        if last is not None:
            parts = refs[:np]
            in_ref, dm_ref, gain_ref, *refs = refs[np:]
            sum_ref, out_ref, v_ref, other, mine, w, dp, total, sem = refs
        else:
            sum_ref, out_ref, other, mine, w, dp, total, sem = refs
        i = pl.program_id(0)

        @pl.when(i == 0)
        def _():
            start_joint(lay, joint, bufs, me_ref, lambda _: w, lambda _: sem, lambda t: t == to)

        attend_back_kernel(hl, p_ref, m_ref, g_ref, lse_ref, dp, sum_ref)

        @pl.when(i == 0)
        def _():
            wait_all(w, sem)

        dnormed = dotf(dp[...], w[...], 1, 1)
        y = dotf(x_ref[...], dp[...], 0, 0)
        if last is None:
            out_ref[...] = dnormed.astype(BF)
        else:
            for part in parts:
                dnormed += part[...].astype(F32)
            unit, inverse = unit_of(in_ref[...].astype(F32))
            dinput = norm_back(dnormed, unit, inverse, gain_ref[...])
            out_ref[...] = (dm_ref[...].astype(F32) + dinput).astype(BF)
            add_rows(v_ref, [column_sum(dnormed * unit), column_sum(dnormed)])

        @pl.when(i == 0)
        def _():
            total[...] = y

        @pl.when(i > 0)
        def _():
            total[...] += y

        @pl.when(i == own - 1)
        def _():
            put_pieces(lay, me_ref, total[...], other, mine)
            other[:, :, :, w3:] = go_other[...]
            mine[:, :, :, w3:] = go_own[...]

    spec = lambda width: pl.BlockSpec((SP, width), lambda i, m: (i, to ^ m[2]))
    part = pl.BlockSpec((1, lay.nz, lay.rows, cw), lambda i, m: (to, 0, 0, 0))
    piece = jax.ShapeDtypeStruct((1, lay.nz, lay.rows, w3 + cw), BF)
    return run(
        "attend_back", 20, kernel, (own,),
        [(b, ANY) for chain in joint for b in chain.bufs]
        + [
            (packed, spec(w3)),
            (mixed, spec(cw)),
            (dmixed, spec(cw)),
            (lse, pl.BlockSpec((1, 1, hl, LP), lambda i, m: (i, to ^ m[2], 0, 0))),
            (normed, row_block(D)),
            (output[0], part),
            (output[1], part),
        ]
        + ([(x, row_block(D)) for x in (*last[0], last[1], last[2])] + [(last[3], one_row(D))] if last else []),
        [
            (jax.ShapeDtypeStruct((own, 1, 1, w3), F32), pl.BlockSpec((1, 1, 1, w3), lambda i, m: (i, 0, 0, 0))),
            (jax.ShapeDtypeStruct((rows, D), BF), row_block(D)),
        ]
        + ([(jax.ShapeDtypeStruct((2, D), F32), whole((2, D)))] if last else [])
        + [(piece, whole(piece.shape))] * 2,
        [pltpu.VMEM((D, w3), BF), pltpu.VMEM((SP, w3), BF), pltpu.VMEM((D, w3), F32), pltpu.SemaphoreType.DMA],
        more,
    )


def insert_bit(s, b, value):
    return ((s >> b) << (b + 1)) | (value << b) | (s & ((1 << b) - 1))


def along(lay, run, arrays, more=()):
    z, dr, width = arrays[0].shape
    n = len(arrays)
    w = width // 2

    def kernel(me_ref, *refs):
        for k in range(z):
            total = refs[0][k].astype(F32)
            for ref in refs[1:n]:
                total += ref[k].astype(F32)
            refs[n + k][...] = total.astype(BF)

    block = pl.BlockSpec((z, dr, w), lambda s, m: (0, 0, s))
    out = (jax.ShapeDtypeStruct((dr, width), BF), pl.BlockSpec((dr, w), lambda s, m: (0, s)))
    sums, more = run("add_plane", 0, kernel, (width // w,), [(x, block) for x in arrays], [out] * z, (), more)
    return [swap(x, k * 2 * lay.nt, lay.size) if k else x for k, x in enumerate(sums)], more


def total_of(ends):
    total = ends[0].astype(F32)
    for x in ends[1:]:
        total = total + x.astype(F32)
    return total


class Butterfly:
    def __init__(self, lay, reverse, other, own):
        self.lay = lay
        bits = list(range(lay.tbits))
        self.bits = bits[::-1] if reverse else bits
        self.keep, self.got = [own], [swap(other, lay.core, lay.size)]
        self.left = list(range(lay.nt))

    def fold(self, run, more=()):
        bit = self.bits.pop(0)
        n = len(self.left)
        z, dr, width = self.keep[0].shape[-3:]
        one = len(self.keep) == 1
        block = pl.BlockSpec((n, 1, dr, width), lambda s, m: (0, s, 0, 0)) if one else None
        deep = 1 if one else z // 2
        piece = pl.BlockSpec((deep, dr, width), lambda s, m: (s, 0, 0))
        k = len(self.keep)

        def kernel(me_ref, *refs):
            for i in range(n):
                a, b = (refs[0][i], refs[1][i]) if one else (refs[i][...], refs[k + i][...])
                refs[2 * k + i][...] = a + b

        shape = jax.ShapeDtypeStruct((z, dr, width), BF)
        sums, more = run(
            "add", 0, kernel, (z // deep,), [(x, block or piece) for x in (*self.keep, *self.got)], [(shape, piece)] * n, (), more
        )
        self.keep = [x for t, x in zip(self.left, sums) if not t >> bit & 1]
        self.got = [swap(x, 1 << bit, self.lay.size) for t, x in zip(self.left, sums) if t >> bit & 1]
        self.left = [t for t in self.left if not t >> bit & 1]
        return more

    def along(self, run, more=()):
        self.ends, more = along(self.lay, run, self.keep + self.got, more)
        return more


class Direct:
    def __init__(self, lay):
        self.lay = lay
        self.parts, self.waiting = [], []

    def start(self, to, other, own):
        self.waiting.append((to, own[0], swap(other[0], self.lay.core, self.lay.size)))

    def spread(self, run, more=()):
        to, own, got = self.waiting.pop(0)
        z, dr, width = own.shape

        def kernel(me_ref, a_ref, b_ref, o_ref):
            o_ref[...] = a_ref[...] + b_ref[...]

        block = pl.BlockSpec((z, dr, width), lambda s, m: (0, 0, 0))
        shape = jax.ShapeDtypeStruct(own.shape, BF)
        (x,), more = run("add_core", 0, kernel, (1,), [(own, block), (got, block)], [(shape, block)], (), more)
        self.parts.append(swap(x, to, self.lay.size))
        return more

    def along(self, run, more=()):
        self.ends, more = along(self.lay, run, [*self.waiting[0][1:], *self.parts], more)
        return more


def unpad_rows(x):
    own = x.shape[0] // SP
    return x.reshape(own, SP, D)[:, :SEQ].reshape(own * SEQ, D)


def per_device(
    lay,
    tokens,
    first_gain,
    first_shift,
    joint_weight,
    joint_bias,
    output_weight,
    output_bias,
    second_gain,
    second_shift,
    expand_weight,
    expand_bias,
    shrink_weight,
    shrink_bias,
    cotangent,
    image_count,
    threshold,
):
    own = tokens.shape[0] // SEQ
    nt, cw, dr = lay.nt, lay.cw, lay.rows
    half = lay.cols // 2
    hl = cw // HEAD_DIM
    tensor = lax.axis_index("tensor").astype(jnp.int32)
    dp = lax.axis_index("dp").astype(jnp.int32)
    count = image_count[0]
    run = Runner(jnp.stack([dp // 2, dp % 2, tensor, count]))

    split = 3 * cw // 2 if cw % 256 == 0 else 2 * cw
    flat = joint_weight.reshape(dr, 3 * cw)
    joint = [Chain(lay, flat[:, :split], False), Chain(lay, flat[:, split:], True)]
    for chain in joint:
        chain.send()
    small = jnp.concatenate([joint_bias.reshape(-1), expand_bias.reshape(-1)])
    n_small = small.shape[0]
    output = jnp.concatenate([output_weight.T, jnp.pad(small[None], ((0, 15), (0, cw - n_small)))])
    (joint[0].got, joint[1].got), (output,) = gate(run, [chain.got for chain in joint], [output])
    output = Shards(lay, output)

    biases = output.bufs[0][:, dr].astype(F32)
    nb = joint_bias.size
    jb = biases[:, :nb].reshape(lay.ndp, nt, 2, hl, HEAD_DIM // lay.ndp)
    jb = jb.transpose(2, 1, 3, 0, 4).reshape(2, nt, 1, cw)
    bias_rows = jnp.concatenate([jb[0], jnp.zeros_like(jb[0]), jb[1]], axis=1).reshape(1, 3 * D)
    eb = biases[:, nb:n_small].reshape(lay.ndp, nt, FF // HEAD_DIM // nt, HEAD_DIM // lay.ndp)
    eb = eb.transpose(1, 2, 0, 3).reshape(nt, 2, half)
    expand_rows = [eb[:, g].reshape(1, nt * half) for g in range(2)]

    image_ids = tensor * own + jnp.arange(own, dtype=jnp.int32)
    image_live = image_ids < count
    row = lambda v: v.reshape(1, D)

    def land(chains):
        for chain in chains:
            chain.land()
            chain.send_last() if len(chain.stages) == 1 else chain.send()

    land(joint)
    shrink_t = (shrink_weight + run.token[0, 0].astype(BF)).T
    feeds = [Chain(lay, expand_weight[:, :half], False), Chain(lay, shrink_t[:, :half], True)]
    rest = jnp.concatenate([expand_weight[:, half:], shrink_t[:, half:]], axis=1)
    for chain in feeds:
        chain.send()
    while len(joint[0].stages) > 2:
        land(joint)
        if len(feeds[0].stages) > 3:
            land(feeds)
    (joint[0].got, joint[1].got), (feeds[0].got, feeds[1].got) = gate(
        run, [chain.got for chain in joint], [chain.got for chain in feeds]
    )
    land(joint)
    while len(feeds[0].stages) > 2:
        land(feeds)
    inputs, normed, dresult = prepare(run, tokens, cotangent, row(first_gain), row(first_shift))
    (joint[0].got, joint[1].got), (feeds[0].got, feeds[1].got), (rest,) = gate(
        run, [chain.got for chain in joint], [chain.got for chain in feeds], [rest]
    )
    for chain in joint:
        chain.share()
    rest = Shards(lay, rest)
    land(feeds)
    packed, mixed, lse, tops = attend_all(lay, run, joint, normed, bias_rows)
    (feeds[0].got, feeds[1].got), = gate(run, [chain.got for chain in feeds])
    for chain in feeds:
        chain.share()
    shrinks = [(feeds[1], 0), (rest, half)]
    middle, second = out_project(
        lay, run, output, mixed, inputs, row(output_bias), row(second_gain), row(second_shift)
    )

    active0, expand_sum0, dsecond, *pieces = feed(
        lay, run, (feeds[0], 0), shrinks[0], second, dresult, expand_rows[0]
    )
    grads = [Butterfly(lay, True, *pieces)]
    active1, expand_sum1, dsecond, *pieces = feed(
        lay, run, (rest, 0), shrinks[1], second, dresult, expand_rows[1], dsecond
    )
    grads.append(Butterfly(lay, False, *pieces))
    for sc in grads:
        sc.fold(run)
    dmiddle, dmixed, sums_two, *out_pieces = feed_back(
        lay, run, output, dsecond, middle, dresult, mixed, row(second_gain)
    )

    packed_sums, dnormed = [], []
    total = Direct(lay)

    def back(to, last=None, more=()):
        (part, out, *rest), more = attend_back(
            lay, run, to, joint, packed, mixed, dmixed, lse, normed, out_pieces, last, more
        )
        packed_sums.append(part)
        total.start(to, *rest[-2:])
        return out, rest[0], list(more)

    def spread(more=()):
        return list(total.spread(run, more))

    for n, to in enumerate(range(nt - 1, 0, -1)):
        if n == 0:
            out, _, more = back(to, None, [grads[0].got[0], grads[1].got[0]])
            grads[0].got[0], grads[1].got[0] = more
        else:
            out = back(to)[0]
        dnormed.append(out)
        if grads[0].bits:
            for sc in grads:
                sc.fold(run)
            if n:
                spread()
        elif not hasattr(grads[0], "ends"):
            for sc in grads:
                sc.along(run)
            spread()
        else:
            at = len(total.parts) - 1
            total.parts[at], *grads[0].ends[1:] = spread([total.parts[at], *grads[0].ends[1:]])
    token_rows, sums_one, _ = back(0, (dnormed, inputs, dmiddle, row(first_gain)))

    tops = jnp.max(tops, axis=-1).reshape(own, HEADS) / LOG2E
    peak = jnp.max(jnp.where(image_live[:, None], tops, NEG), axis=0)
    peak = jnp.broadcast_to(peak[:, None], (HEADS, 128))
    expand_sum = jnp.stack([expand_sum0.reshape(nt, half), expand_sum1.reshape(nt, half)], axis=1)
    heads = jnp.concatenate([jnp.sum(x, axis=0) for x in packed_sums[::-1]]).reshape(nt, 3, cw)
    heads = heads[jnp.arange(nt) ^ tensor]
    vectors = [sums_two, expand_sum, sums_one, heads[:, 0], heads[:, 2]]
    sums = jnp.concatenate([peak] + [v.reshape(-1, 128) for v in vectors])
    ((sums,),) = gate(run, [sums])
    sums = lax.all_gather(sums, AXES)
    grads[1].ends[1:] = spread(grads[1].ends[1:])
    result, _ = feed_out(lay, run, shrinks[0], active0, middle)
    total.along(run)
    ends = [x for sc in grads for x in sc.ends]
    result, (token_rows, *ends) = feed_out(
        lay, run, shrinks[1], active1, result, row(shrink_bias), [token_rows, *ends]
    )
    for n, sc in enumerate(grads):
        sc.ends = ends[n * lay.nz : (n + 1) * lay.nz]

    block_out = unpad_rows(result)
    tokens_grad = unpad_rows(token_rows)
    peak = jnp.max(sums[:, :HEADS, 0], axis=0)
    sums = jnp.sum(sums, axis=0)
    at = [HEADS, HEADS + 4 * D // 128, HEADS + (4 * D + FF) // 128, HEADS + (6 * D + FF) // 128]
    sums_two = sums[at[0] : at[1]].reshape(4, D)
    expand_sum = sums[at[1] : at[2]].reshape(FF)
    sums_one = sums[at[2] : at[3]].reshape(2, D)
    bias_sum = sums[at[3] :].reshape(2, D)
    mine = lambda v: lax.dynamic_slice_in_dim(v, dp * dr, dr, v.ndim - 1)
    sums_one, sums_two = mine(sums_one), mine(sums_two)
    share = HEAD_DIM // lay.ndp
    units = FF // HEAD_DIM // nt
    expand_bias_grad = lax.dynamic_slice(
        expand_sum.reshape(FF // HEAD_DIM, HEAD_DIM), (tensor * units, dp * share), (units, share)
    )
    joint_bias_grad = lax.dynamic_slice(
        bias_sum.reshape(2, HEADS, HEAD_DIM), (0, tensor * hl, dp * share), (2, hl, share)
    )

    top = lax.dynamic_slice_in_dim(peak, tensor * hl, hl, 0)
    factors = jnp.sqrt(threshold / jnp.maximum(top, threshold))
    columns = jnp.repeat(factors, HEAD_DIM)
    clipped_joint = (joint_weight[:, 0:2, :].astype(F32) * columns).astype(BF)
    clipped_bias = (joint_bias[0].astype(F32) * factors[:, None]).astype(BF)

    feed_a, feed_b, total = [total_of(g.ends) for g in (*grads, total)]
    joint_grad = total[:, : 3 * cw].reshape(dr, 3, cw)
    output_grad = total[:, 3 * cw :].T
    expand_grad = jnp.concatenate([feed_a[:, :half], feed_b[:, :half]], axis=1)
    shrink_grad = jnp.concatenate([feed_a[:, half:], feed_b[:, half:]], axis=1).T
    return (
        block_out,
        tokens_grad,
        sums_one[0],
        sums_one[1],
        joint_grad,
        joint_bias_grad,
        output_grad,
        sums_two[2],
        sums_two[0],
        sums_two[1],
        expand_grad,
        expand_bias_grad,
        shrink_grad,
        sums_two[3],
        clipped_joint,
        clipped_bias,
        factors,
    )


def solution(mesh):
    placed = (
        P(("dp", "tensor"), None),
        P(),
        P(),
        P("dp", None, "tensor"),
        P(None, "tensor", "dp"),
        P("tensor", "dp"),
        P(),
        P(),
        P(),
        P("dp", "tensor"),
        P("tensor", "dp"),
        P("tensor", "dp"),
        P(),
        P(("dp", "tensor"), None),
        P("dp"),
        P("tensor"),
    )
    lay = Layout(mesh.shape["dp"], mesh.shape["tensor"])
    return jax.shard_map(
        partial(per_device, lay),
        mesh=mesh,
        in_specs=placed,
        out_specs=(
            P(("dp", "tensor"), None),
            P(("dp", "tensor"), None),
            P("dp"),
            P("dp"),
            P("dp", None, "tensor"),
            P(None, "tensor", "dp"),
            P("tensor", "dp"),
            P("dp"),
            P("dp"),
            P("dp"),
            P("dp", "tensor"),
            P("tensor", "dp"),
            P("tensor", "dp"),
            P("dp"),
            P("dp", None, "tensor"),
            P("tensor", "dp"),
            P("tensor"),
        ),
        check_vma=False,
    )
```
